32 devices in a mesh: section: 2 (over core), seq: 4 (over z), wshard: 4 (over y, x).
Axes of the slice: x: 2, y: 2, z: 4, core: 2. Of those that a mesh axis runs over, the one named last changes fastest.
Arguments:
- layer_input: bfloat16 [2, 8192, 1024], P(None, ('wshard', 'seq')), may hold values from -6 to 6
- out_grad: bfloat16 [2, 8192, 1024], P(None, ('wshard', 'seq')), may hold values from -6 to 6
- doc_index: int32 [2, 8192], P(None, ('wshard', 'seq')), may hold values from 0 to 7, as said below
- doc_adapter: int32 [2, 4, 16], P(None, 'wshard'), may hold values from 0 to 7
- in_weight: bfloat16 [2, 1024, 4384], P('section', 'wshard'), may hold values from -0.1875 to 0.1875
- out_weight: bfloat16 [2, 2048, 1024], P('section', 'wshard'), may hold values from -0.125 to 0.125
- norm_gain: float32 [2, 1024], P('section'), may hold values from 0.5 to 1.5
- conv_weight: float32 [2, 4, 2304], P('section'), may hold values from -3 to 3
- conv_bias: float32 [2, 2304], P('section'), may hold values from -1.5 to 1.5
- dt_bias: float32 [2, 32], P('section'), may hold values from -11 to -3
- a_log: float32 [2, 32], P('section'), may hold values from 0 to 2.77
- skip_gain: float32 [2, 32], P('section'), may hold values from 0.5 to 1.5
- gate_gain: float32 [2, 2048], P('section'), may hold values from 0.5 to 1.5
- in_down: bfloat16 [2, 1024, 128], P('section'), may hold values from -0.1875 to 0.1875
- in_up: bfloat16 [2, 128, 4384], P('section'), may hold values from -0.75 to 0.75
- out_down: bfloat16 [2, 2048, 128], P('section'), may hold values from -0.125 to 0.125
- out_up: bfloat16 [2, 128, 1024], P('section'), may hold values from -0.75 to 0.75
Outputs:
- section_out: bfloat16 [2, 2, 8192, 1024], P('section', None, ('wshard', 'seq'))
- input_grad: bfloat16 [2, 2, 8192, 1024], P('section', None, ('wshard', 'seq'))
- in_down_grad: float32 [2, 1024, 128], P('section')
- in_up_grad: float32 [2, 128, 4384], P('section')
- out_down_grad: float32 [2, 2048, 128], P('section')
- out_up_grad: float32 [2, 128, 1024], P('section')
The draws below stay inside these ranges and needn't reach their ends.
Inputs may be any that keep to these rules, and one draw needn't show every extreme that they name: `doc_index`: within each aligned block of 2048 tokens the numbers start at 0, never fall, and rise by one exactly once inside each eighth of the block after the first, so that each block holds 8 documents.
All inputs are finite; a program needn't handle non-finite values.
Results may differ from the reference program's by a relative error of at most 0.018.
Values may be sent and summed in bfloat16 or wider, within the bound.
No kernel may reach another device: no remote copies, remote signals or barrier semaphores. Data moves between devices by JAX's collectives and lax.ppermute only.
A program may use at most 256 MiB of HBM per device.

```python
import jax
import jax.numpy as jnp
from jax import lax

D = 1024
INNER = 2048
HEADS = 32
HEAD = 64
STATE = 128
CONV_K = 4
SPAN = 256
ADAPT = 8
RANK = 16
DOCS = 16
MB = 2
PROJ = 4384
XBC = 2304
GROUP = 2048
GROUPS = 4
TOKS = 8192


def draw_doc_index(key, part):
    key = jax.random.fold_in(key, 11)
    block_count = MB * GROUPS
    eighth = GROUP // 8
    places = jnp.arange(GROUP)
    offsets = jax.random.randint(key, (block_count, 7), 0, eighth)
    opening = (jnp.arange(1, 8)[None, :] * eighth + offsets).astype(jnp.int32)
    starts = jnp.any(places[None, :, None] == opening[:, None, :], axis=2)
    numbers = jnp.cumsum(starts.astype(jnp.int32), axis=1)
    return numbers.reshape(MB, TOKS).astype(jnp.int32)


def with_ends(values, own_key, smallest, largest):
    longest = values.shape.index(max(values.shape))
    spots = []
    for shift in (0, 1):
        where = [jax.random.randint(jax.random.fold_in(own_key, axis), (), 0, length) for axis, length in enumerate(values.shape)]
        where[longest] = (where[longest] + shift) % values.shape[longest]
        spots.append(tuple(where))
    return values.at[spots[0]].set(smallest).at[spots[1]].set(largest)


def shard_levels(key, dims, cuts, least, largest):
    loudness, own = 1.0, jax.random.fold_in(key, 6)
    for axis_at, blocks in cuts:
        draws = jnp.exp(jax.random.uniform(jax.random.fold_in(own, axis_at), (blocks,), jnp.float32, least / len(cuts), largest / len(cuts)))
        loudness = loudness * jnp.repeat(draws, dims[axis_at] // blocks).reshape([-1 if axis == axis_at else 1 for axis in range(len(dims))])
    return loudness


def gaussian(own_key, shape, deviation, limit, split=(), held_as=jnp.bfloat16):
    entries = deviation * jax.random.normal(own_key, shape, jnp.float32)
    if split:
        entries = entries * shard_levels(own_key, shape, split, -0.22, 0.18)
    return jnp.clip(entries, -limit, limit).astype(held_as)


def setup_inputs(seed: int = 0) -> dict:
    streams_of = jax.random.split(jax.random.key(seed), 18)
    layer_input = gaussian(streams_of[0], (MB, TOKS, D), 1.0, 6.0, ((1, 16),))
    out_grad = gaussian(streams_of[1], (MB, TOKS, D), 1.0, 6.0, ((1, 16),))
    doc_index = draw_doc_index(jax.random.fold_in(streams_of[17], 71), 0)
    doc_adapter = with_ends(jax.random.randint(streams_of[3], (MB, GROUPS, DOCS), 0, ADAPT), jax.random.fold_in(streams_of[3], 1), 0, ADAPT - 1).astype(jnp.int32)
    in_weight = gaussian(streams_of[4], (2, D, PROJ), D ** -0.5, 0.1875, ((0, 2), (1, 4)))
    out_weight = gaussian(streams_of[5], (2, INNER, D), INNER ** -0.5, 0.125, ((0, 2), (1, 4)))
    norm_gain = jnp.clip(1.0 + 0.1 * jax.random.normal(streams_of[6], (2, D), jnp.float32), 0.5, 1.5)
    conv_weight = gaussian(streams_of[7], (2, CONV_K, XBC), CONV_K ** -0.5, 3.0, ((0, 2),), jnp.float32)
    conv_bias = gaussian(streams_of[8], (2, XBC), 0.3, 1.5, ((0, 2),), jnp.float32)
    dt_bias = jnp.clip(-11.0 + 8.0 * jax.random.uniform(streams_of[9], (2, HEADS), jnp.float32) ** shard_levels(streams_of[9], (2, HEADS), ((0, 2),), -0.2, 0.2), -11.0, -3.0)
    a_log = jnp.clip(2.77 * jax.random.uniform(streams_of[10], (2, HEADS), jnp.float32) ** shard_levels(streams_of[10], (2, HEADS), ((0, 2),), -0.2, 0.2), 0.0, 2.77)
    skip_gain = jnp.clip(0.5 + 1.0 * jax.random.uniform(streams_of[11], (2, HEADS), jnp.float32) ** shard_levels(streams_of[11], (2, HEADS), ((0, 2),), -0.2, 0.2), 0.5, 1.5)
    gate_gain = jnp.clip(1.0 + 0.1 * jax.random.normal(streams_of[12], (2, INNER), jnp.float32), 0.5, 1.5)
    in_down = gaussian(streams_of[13], (2, D, ADAPT * RANK), D ** -0.5, 0.1875, ((0, 2),))
    in_up = gaussian(streams_of[14], (2, ADAPT * RANK, PROJ), (4 * RANK) ** -0.5, 0.75, ((0, 2),))
    out_down = gaussian(streams_of[15], (2, INNER, ADAPT * RANK), INNER ** -0.5, 0.125, ((0, 2),))
    out_up = gaussian(streams_of[16], (2, ADAPT * RANK, D), (4 * RANK) ** -0.5, 0.75, ((0, 2),))
    return dict(layer_input=layer_input, out_grad=out_grad, doc_index=doc_index, doc_adapter=doc_adapter, in_weight=in_weight, out_weight=out_weight, norm_gain=norm_gain, conv_weight=conv_weight, conv_bias=conv_bias, dt_bias=dt_bias, a_log=a_log, skip_gain=skip_gain, gate_gain=gate_gain, in_down=in_down, in_up=in_up, out_down=out_down, out_up=out_up)


EPSILON = 1e-05
PRECISE = lax.Precision.HIGHEST

@jax.custom_vjp
def low(v):
    return lax.optimization_barrier(v.astype(jnp.bfloat16)).astype(jnp.float32)

@jax.custom_vjp
def low_back(v):
    return v

def low_keep(v):
    return (low(v), None)

def low_pass(kept, grad):
    return (grad,)

def back_keep(v):
    return (v, None)

def back_low(kept, grad):
    return (low(grad),)
low.defvjp(low_keep, low_pass)
low_back.defvjp(back_keep, back_low)

def matmul(left, right):
    return jnp.dot(left, right, precision=PRECISE, preferred_element_type=jnp.float32)

def rms_scale(values, gain_row):
    return values * lax.rsqrt(lax.optimization_barrier(jnp.mean(values * values, axis=-1, keepdims=True)) + EPSILON) * gain_row

def gated_norm(mixed, gate_in, gain_row):
    return rms_scale(mixed * jax.nn.silu(gate_in), gain_row)

def conv_mix(extended, extended_ids, doc_ids, weight, conv_offset):
    length = doc_ids.shape[0]
    tap_count = weight.shape[0]
    total = jnp.zeros((length, weight.shape[1]), jnp.float32) + conv_offset[None, :]
    for tap_index in range(tap_count):
        same_doc = (extended_ids[tap_index:tap_index + length] == doc_ids)[:, None]
        total = total + jnp.where(same_doc, extended[tap_index:tap_index + length], 0.0) * weight[tap_index][None, :]
    return jax.nn.silu(total)

def conv_part(mixed_in, rim_rows, rim_ids, doc_ids, step_raw, weight, conv_offset, step_bias):
    extended = jnp.concatenate([rim_rows, mixed_in], axis=0)
    extended_ids = jnp.concatenate([rim_ids, doc_ids], axis=0)
    return (conv_mix(extended, extended_ids, doc_ids, weight, conv_offset), jax.nn.softplus(step_raw + step_bias[None, :]))

def ssd_scan(values, step_rows, decay_rate, in_state, out_state, doc_ids, skip_rows):
    length, head_count, head_size = values.shape
    state_size = in_state.shape[1]
    blocks = length // SPAN
    log_decay = jnp.cumsum((-(step_rows * decay_rate[None, :])).reshape(blocks, SPAN, head_count), axis=1)
    lower_mask = jnp.arange(SPAN)[:, None] >= jnp.arange(SPAN)[None, :]

    def one_block(carried, pieces):
        state_now, last_doc = carried
        block_values, block_steps, block_decay, block_in, block_out, block_docs = pieces
        same_doc = ((block_docs[:, None] == block_docs[None, :]) & lower_mask)[:, :, None]
        spread = block_decay[:, None, :] - block_decay[None, :, :]
        kernel = jnp.where(same_doc, jnp.exp(jnp.where(same_doc, spread, 0.0)), 0.0)
        scores = jnp.dot(block_out, block_in.T, precision=PRECISE, preferred_element_type=jnp.float32)
        driven = block_steps[:, :, None] * block_values
        inside = jnp.einsum('tsh,shp->thp', scores[:, :, None] * kernel, driven, precision=PRECISE)
        carry_on = jnp.exp(block_decay) * (block_docs == last_doc).astype(jnp.float32)[:, None]
        before = jnp.einsum('tn,hpn->thp', block_out, state_now, precision=PRECISE) * carry_on[:, :, None]
        tail_weight = jnp.exp(block_decay[-1][None, :] - block_decay) * (block_docs == block_docs[-1]).astype(jnp.float32)[:, None]
        keep_state = jnp.exp(block_decay[-1]) * (last_doc == block_docs[-1]).astype(jnp.float32)
        state_next = jnp.einsum('sh,shp,sn->hpn', tail_weight, driven, block_in, precision=PRECISE) + state_now * keep_state[:, None, None]
        output = inside + before + skip_rows[None, :, None] * block_values
        return ((state_next, block_docs[-1]), output)
    pieces = (values.reshape(blocks, SPAN, head_count, head_size), step_rows.reshape(blocks, SPAN, head_count), log_decay, in_state.reshape(blocks, SPAN, state_size), out_state.reshape(blocks, SPAN, state_size), doc_ids.reshape(blocks, SPAN))
    initial = (jnp.zeros((head_count, head_size, state_size), jnp.float32), jnp.array(-1, jnp.int32))
    unused, outputs = lax.scan(jax.checkpoint(one_block), initial, pieces)
    return outputs.reshape(length, head_count, head_size)

def layer(inputs, doc_ids, lane_mask, frozen, adapters):
    in_full, out_full, norm_row, conv_w, conv_offset, step_bias, decay_rate, skip_row, gate_row = frozen
    down_in, up_in, down_out, up_out = adapters
    length = inputs.shape[0]
    normed = low(rms_scale(inputs, norm_row))
    narrow = low_back(low(matmul(normed, down_in) * lane_mask))
    projected = low_back(low(matmul(normed, in_full) + matmul(narrow, up_in)))
    gate_in = projected[:, :INNER]
    mixed_in = projected[:, INNER:INNER + XBC]
    step_raw = projected[:, INNER + XBC:]
    rim_rows = jnp.zeros((CONV_K - 1, XBC), jnp.float32)
    rim_ids = jnp.full((CONV_K - 1,), -1, jnp.int32)
    activated, step_size = conv_part(mixed_in, rim_rows, rim_ids, doc_ids, step_raw, conv_w, conv_offset, step_bias)
    activated = low(activated)
    values_in = low_back(activated[:, :INNER])
    step_size = low_back(low(step_size))
    scanned = ssd_scan(values_in.reshape(length, HEADS, HEAD), step_size, decay_rate, activated[:, INNER:INNER + STATE], activated[:, INNER + STATE:], doc_ids, skip_row)
    scanned = low_back(low(scanned.reshape(length, INNER)))
    normed_out = low(gated_norm(scanned, gate_in, gate_row))
    narrow_out = low_back(low(matmul(normed_out, down_out) * lane_mask))
    branch = low_back(matmul(normed_out, out_full) + matmul(narrow_out, up_out))
    return inputs + branch

def reference(layer_input, out_grad, doc_index, doc_adapter, in_weight, out_weight, norm_gain, conv_weight, conv_bias, dt_bias, a_log, skip_gain, gate_gain, in_down, in_up, out_down, out_up):
    as_float = lambda array: array.astype(jnp.float32)
    frozen = [(as_float(in_weight[level]), as_float(out_weight[level]), norm_gain[level], conv_weight[level], conv_bias[level], dt_bias[level], jnp.exp(a_log[level]), skip_gain[level], gate_gain[level]) for level in range(2)]
    adapters = tuple(((as_float(in_down[level]), as_float(in_up[level]), as_float(out_down[level]), as_float(out_up[level])) for level in range(2)))
    block_count = MB * GROUPS
    inputs_all = layer_input.reshape(block_count, GROUP, D)
    grads_all = out_grad.reshape(block_count, GROUP, D)
    docs_all = doc_index.reshape(block_count, GROUP)
    tables_all = doc_adapter.reshape(block_count, DOCS)
    lane_ids = jnp.arange(ADAPT * RANK) // RANK

    def one_group(totals, pieces):
        block_input, block_grad, block_docs, block_table = pieces
        adapter = jnp.take(block_table, block_docs)
        lane_mask = (adapter[:, None] == lane_ids[None, :]).astype(jnp.float32)

        def two_layers(first_in, probe, first_adapters, second_adapters):
            middle = low_back(low(layer(first_in, block_docs, lane_mask, frozen[0], first_adapters))) + probe
            return (middle, layer(middle, block_docs, lane_mask, frozen[1], second_adapters))
        probe = jnp.zeros((GROUP, D), jnp.float32)
        (middle, final), back_fn = jax.vjp(two_layers, as_float(block_input), probe, adapters[0], adapters[1])
        grad_input, grad_probe, grad_first, grad_second = back_fn((jnp.zeros_like(middle), as_float(block_grad)))
        totals = jax.tree.map(jnp.add, totals, (grad_first, grad_second))
        return (totals, (middle.astype(jnp.bfloat16), final.astype(jnp.bfloat16), grad_input.astype(jnp.bfloat16), grad_probe.astype(jnp.bfloat16)))
    start_totals = jax.tree.map(jnp.zeros_like, adapters)
    totals, (middles, finals, grad_inputs, grad_probes) = lax.scan(one_group, start_totals, (inputs_all, grads_all, docs_all, tables_all))
    section_out = jnp.stack([middles.reshape(MB, TOKS, D), finals.reshape(MB, TOKS, D)])
    input_grad = jnp.stack([grad_inputs.reshape(MB, TOKS, D), grad_probes.reshape(MB, TOKS, D)])
    grads = [jnp.stack([totals[0][index], totals[1][index]]) for index in range(4)]
    return (section_out, input_grad, grads[0], grads[1], grads[2], grads[3])
```

```python
import functools

import jax
import jax.numpy as jnp
from jax import lax
from jax.experimental import pallas as pl
from jax.experimental.pallas import tpu as pltpu
from jax.sharding import PartitionSpec as P

SPAN = 256
RANK = 16
LANES = 128
DOCS_PER_BLOCK = 8
EPSILON = 1e-05
EXACT = lax.Precision.HIGHEST
BF16 = jnp.bfloat16
F32 = jnp.float32
PARAMS = pltpu.CompilerParams(vmem_limit_bytes=56 * 1024 * 1024)


def from_behind(value, axis, steps):
    count = lax.axis_size(axis)
    initial, last = (max(0, -steps), min(count, count - steps))
    return lax.ppermute(value, axis, [(source, source + steps) for source in range(initial, last)])


def dot(left, right):
    return jnp.dot(left, right, preferred_element_type=F32)


def dot_last(left, right):
    return lax.dot_general(left, right, (((1,), (1,)), ((), ())), preferred_element_type=F32)


def dot_first(left, right):
    return lax.dot_general(left, right, (((0,), (0,)), ((), ())), preferred_element_type=F32)


def rms_rate(values):
    return lax.rsqrt(jnp.mean(values * values, axis=-1, keepdims=True) + EPSILON)


def sigmoid(v):
    return 1.0 / (1.0 + jnp.exp(-v))


def lower_ones(shape):
    rows = lax.broadcasted_iota(jnp.int32, shape, 0)
    columns = lax.broadcasted_iota(jnp.int32, shape, 1)
    return rows <= columns


def conv_rows(rows, rim, weight, offset, valid):
    length = rows.shape[0]
    extended = jnp.concatenate([rim, rows], axis=0)
    taps = weight.shape[0]
    total = offset + weight[taps - 1 : taps] * rows
    for back in range(1, taps):
        shifted = extended[8 - back : 8 - back + length]
        total = total + jnp.where(valid >= back, shifted, 0.0) * weight[taps - 1 - back : taps - back]
    gate = sigmoid(total)
    active = total * gate
    return active, gate + active * (1.0 - gate)


def conv_kernel(
    spans, head, heads, state,
    mixed_ref, mixed_bc_ref, rim_ref, rim_bc_ref, weight_ref, weight_bc_ref, offset_ref, offset_bc_ref,
    valid_ref, raw_ref, bias_ref, rate_ref, token_ref,
    values_ref, slope_ref, bc_ref, slope_bc_ref, state_ref, step_ref, decay_ref, sig_ref, tail_ref,
):
    group = pl.program_id(0)
    valid = valid_ref[:, :1]
    heads_here = mixed_ref.shape[1] // head

    @pl.when(group == 0)
    def _():
        active, slope = conv_rows(
            mixed_bc_ref[...].astype(F32), rim_bc_ref[...].astype(F32), weight_bc_ref[...], offset_bc_ref[...], valid
        )
        bc_ref[...] = active.astype(BF16)
        slope_bc_ref[...] = slope.astype(BF16)
        raw = (raw_ref[...].astype(F32) + bias_ref[...]).T[:heads]
        step = (jnp.maximum(raw, 0.0) + jnp.log1p(jnp.exp(-jnp.abs(raw)))).astype(BF16).astype(F32)
        step_ref[...] = step
        sig_ref[...] = sigmoid(raw)
        drop = -(step * rate_ref[:, :1])
        ones = lower_ones((SPAN, SPAN)).astype(F32)
        for span in range(spans):
            here = slice(span * SPAN, (span + 1) * SPAN)
            decay = jnp.dot(drop[:, here], ones, precision=EXACT, preferred_element_type=F32)
            decay_ref[:, here] = decay
            tail = jnp.exp(decay[:, SPAN - 1 :] - decay) * token_ref[span][1:2]
            tail_ref[:, here] = tail * step[:, here]

    active, slope = conv_rows(
        mixed_ref[...].astype(F32), rim_ref[...].astype(F32), weight_ref[...], offset_ref[...], valid
    )
    slope_ref[...] = slope.astype(BF16)
    turned = active.T
    low = turned.astype(BF16)
    values_ref[...] = low
    low = low.astype(F32)
    first = pl.multiple_of(group * heads_here, heads_here)
    tail_rows = tail_ref[pl.ds(first, heads_here), :]
    for span in range(spans):
        here = slice(span * SPAN, (span + 1) * SPAN)
        driven = jnp.concatenate(
            [
                (low[place * head : (place + 1) * head, here] * tail_rows[place : place + 1, here]).astype(BF16)
                for place in range(heads_here)
            ],
            axis=0,
        )
        state_ref[span] = dot(driven, bc_ref[here, :state]).astype(BF16)


def scan_kernel(
    head, state,
    values_ref, bc_ref, step_ref, decay_ref, token_ref, doc_column_ref, doc_row_ref, state_ref, skip_ref, gate_ref,
    gain_ref, *rest,
):
    mixed_ref, normed_ref, score_ref, scanned_ref = rest[-4:]
    group, groups = pl.program_id(0), pl.num_programs(0)
    width = values_ref.shape[0]
    heads_here = width // head

    @pl.when(group == 0)
    def _():
        score = dot_last(bc_ref[:, :state], bc_ref[:, state:])
        same = (doc_column_ref[:, :1] == doc_row_ref[:1]) & lower_ones((SPAN, SPAN))
        score_ref[...] = jnp.where(same, score, 0.0)

    decay, step = decay_ref[...], step_ref[...]
    carry = jnp.exp(decay) * token_ref[0][:1]
    columns = jnp.concatenate([decay] * (LANES // heads_here), axis=0).T
    out_map = bc_ref[:, state:]
    parts = []
    for place in range(heads_here):
        rows = slice(place * head, (place + 1) * head)
        one = slice(place, place + 1)
        kernel = (jnp.exp(jnp.minimum(decay[one] - columns[:, one], 0.0)) * score_ref[...]).astype(BF16)
        values = values_ref[rows].astype(F32)
        driven = (values * step[one]).astype(BF16)
        before = dot_last(state_ref[rows], out_map) * carry[one]
        parts.append(dot(driven, kernel) + before + skip_ref[one, :1] * values)
    turned = jnp.concatenate(parts, axis=0).T
    scanned_ref[:, pl.ds(pl.multiple_of(group * width, width), width)] = turned.astype(BF16)

    @pl.when(group == groups - 1)
    def _():
        def rows_at(index, _):
            rows = pl.ds(pl.multiple_of(index * 16, 16), 16)
            mixed = scanned_ref[rows, :]
            mixed_ref[rows, :] = mixed
            gate = gate_ref[rows, :].astype(F32)
            gated = mixed.astype(F32) * (gate * sigmoid(gate))
            normed_ref[rows, :] = (gated * rms_rate(gated) * gain_ref[...]).astype(BF16)
            return 0

        lax.fori_loop(0, SPAN // 16, rows_at, 0)


def out_back_kernel(
    head, heads, state,
    up_ref, lane_ref, up_out_ref, down_out_ref, first_ref, second_ref, third_ref, near_ref, far_ref, where_ref,
    mixed_ref, gate_ref, gain_ref, decay_ref, token_ref, bc_ref,
    project_ref, turned_ref, state_ref, narrow_ref, grad_ref, grad_mixed_ref,
):
    width = mixed_ref.shape[1]
    up = up_ref[...]
    narrow = (dot_last(up, up_out_ref[...]) * lane_ref[...]).astype(BF16)
    narrow_ref[...] = narrow
    left = jnp.concatenate([up, narrow], axis=1)
    for offset, part in out_places(where_ref, (first_ref, second_ref, third_ref), near_ref, far_ref):
        here = pl.ds(offset, part.shape[0])
        grad_ref[:, here] = dot_last(left, jnp.concatenate([part[...], down_out_ref[here, :]], axis=1))

    def rows_at(index, _):
        rows = pl.ds(pl.multiple_of(index * 16, 16), 16)
        mixed = mixed_ref[rows, :].astype(F32)
        gate = gate_ref[rows, :].astype(F32)
        share = sigmoid(gate)
        silu = gate * share
        gated = mixed * silu
        grad = grad_ref[rows, :] * gain_ref[...]
        rate = rms_rate(gated)
        pull = jnp.mean(gated * grad, axis=-1, keepdims=True) * rate * rate * rate
        grad_gated = rate * grad - gated * pull
        project_ref[rows, :] = (grad_gated * mixed * (share + silu * (1.0 - share))).astype(BF16)
        grad_mixed_ref[rows, :] = (grad_gated * silu).astype(BF16)
        return 0

    lax.fori_loop(0, SPAN // 16, rows_at, 0)
    carry = jnp.exp(decay_ref[...]) * token_ref[0][:1]
    out_map = bc_ref[:, state:]
    wide = 512
    for first in range(0, width, wide):
        low = grad_mixed_ref[:, first : first + wide].astype(F32).T
        turned_ref[first : first + wide, :] = low.astype(BF16)
        scaled = [
            (low[place * head : (place + 1) * head] * carry[first // head + place : first // head + place + 1]).astype(BF16)
            for place in range(wide // head)
        ]
        state_ref[0, first : first + wide, :] = dot(jnp.concatenate(scaled, axis=0), out_map).astype(BF16)


def aligned(value, unit):
    return pl.multiple_of(value * unit, unit)


def out_places(where_ref, parts, near, far):
    rows, half = parts[0].shape[0], near.shape[0]
    places = [(aligned(where_ref[place], rows), part) for place, part in enumerate(parts)]
    apart = where_ref[3] * 2
    places.append((aligned(apart + where_ref[4], half), near))
    places.append((aligned(apart + 1 - where_ref[4], half), far))
    return places


def in_columns(ref, where_ref, parts):
    columns = ref.shape[1] // parts
    return [ref[:, pl.ds(aligned(where_ref[place], columns), columns)] for place in range(parts)]


def mixed_kernel(
    main, lanes,
    input_ref, gain_ref, down_ref, lane_ref, up_ref, first_ref, second_ref, third_ref, near_ref, far_ref, where_ref,
    normed_ref, narrow_ref, mixed_ref, raw_ref,
):
    rows = input_ref.shape[0]
    inputs = input_ref[...].astype(F32)
    normed = (inputs * rms_rate(inputs) * gain_ref[...]).astype(BF16)
    normed_ref[...] = normed
    narrow = (dot(normed, down_ref[...]) * lane_ref[...]).astype(BF16)
    narrow_ref[...] = narrow
    left = jnp.concatenate(in_columns(normed_ref, where_ref, 4) + [narrow], axis=1)
    first = where_ref[4] == 0
    half, whole_rows = near_ref.shape[0], first_ref.shape[0]
    step = main // 6

    def product(start, size):
        here = slice(start, start + size)
        if start < main // 2:
            there = slice(start, start + size)
            apart = jnp.where(first, near_ref[there], far_ref[there])
        else:
            there = slice(start - whole_rows + half, start - whole_rows + half + size)
            apart = jnp.where(first, far_ref[there], near_ref[there])
        parts = [first_ref[here], second_ref[here], third_ref[here], apart, up_ref[here]]
        return dot_last(left, jnp.concatenate(parts, axis=1))

    for start in range(0, main, step):
        mixed_ref[:, start : start + step] = product(start, step).astype(BF16)
    extra = whole_rows - main
    raw_ref[...] = jnp.concatenate([product(main, extra), jnp.zeros((rows, lanes - extra), F32)], axis=1).astype(BF16)


def gate_kernel(normed_ref, narrow_ref, up_ref, first_ref, second_ref, third_ref, near_ref, far_ref, where_ref, gate_ref):
    tile, tiles = pl.program_id(0), pl.num_programs(0)
    near = (where_ref[4] == 0) == (tile < tiles // 2)
    left = jnp.concatenate(in_columns(normed_ref, where_ref, 4) + [narrow_ref[...]], axis=1)
    apart = jnp.where(near, near_ref[...], far_ref[...])
    right = jnp.concatenate([first_ref[...], second_ref[...], third_ref[...], apart, up_ref[...]], axis=1)
    gate_ref[...] = dot_last(left, right).astype(BF16)


def out_kernel(
    normed_ref, input_ref, down_ref, lane_ref, up_ref, first_ref, second_ref, third_ref, near_ref, far_ref, where_ref,
    narrow_ref, out_ref,
):
    narrow = (dot(normed_ref[...], down_ref[...]) * lane_ref[...]).astype(BF16)
    narrow_ref[...] = narrow
    places = out_places(where_ref, (first_ref, second_ref, third_ref), near_ref, far_ref)
    left = [normed_ref[:, pl.ds(offset, part.shape[0])] for offset, part in places]
    left = jnp.concatenate(left + [narrow], axis=1)
    wide = 256
    for start in range(0, out_ref.shape[1], wide):
        here = slice(start, start + wide)
        right = jnp.concatenate([part[:, here] for _, part in places] + [up_ref[:, here]], axis=0)
        out_ref[:, here] = (input_ref[:, here].astype(F32) + dot(left, right)).astype(BF16)


def gate_in_back_kernel(
    grad_ref, up_ref, first_ref, second_ref, third_ref, near_ref, far_ref, where_ref, out_ref
):
    tile, tiles = pl.program_id(0), pl.num_programs(0)
    near = (where_ref[4] == 0) == (tile < tiles // 2)
    apart = jnp.where(near, near_ref[...], far_ref[...])
    right = jnp.concatenate([first_ref[...], second_ref[...], third_ref[...], apart, up_ref[...]], axis=1)
    product = dot(grad_ref[...], right)

    @pl.when(tile == 0)
    def _():
        out_ref[...] = product

    @pl.when(tile > 0)
    def _():
        out_ref[...] += product


def mixed_in_back_kernel(
    main,
    grad_ref, raw_ref, part_ref, input_ref, up_stream_ref, gain_ref, lane_ref, down_ref, up_ref,
    first_ref, second_ref, third_ref, near_ref, far_ref, where_ref,
    out_ref, narrow_ref, total_ref,
):
    first = where_ref[4] == 0
    half, whole_rows = near_ref.shape[0], first_ref.shape[0]
    width = input_ref.shape[1]
    columns = width // 4

    def right(start, size):
        here = slice(start, start + size)
        if start < main // 2:
            there = slice(start, start + size)
            apart = jnp.where(first, near_ref[there], far_ref[there])
        else:
            there = slice(start - whole_rows + half, start - whole_rows + half + size)
            apart = jnp.where(first, far_ref[there], near_ref[there])
        return jnp.concatenate([first_ref[here], second_ref[here], third_ref[here], apart, up_ref[here]], axis=1)

    total = part_ref[...] + dot(grad_ref[:, : main // 2], right(0, main // 2))
    total = total + dot(grad_ref[:, main // 2 :], right(main // 2, main // 2))
    extra = whole_rows - main
    total = total + dot(raw_ref[:, :extra], right(main, extra))
    narrow = (total[:, width:] * lane_ref[...]).astype(BF16)
    narrow_ref[...] = narrow
    for place in range(4):
        total_ref[:, pl.ds(aligned(where_ref[place], columns), columns)] = total[:, place * columns : (place + 1) * columns]
    scaled = (total_ref[...] + dot_last(narrow, down_ref[...])) * gain_ref[...]
    inputs = input_ref[...].astype(F32)
    rate = rms_rate(inputs)
    pull = jnp.mean(inputs * scaled, axis=-1, keepdims=True) * rate * rate * rate
    out_ref[...] = (up_stream_ref[...].astype(F32) + rate * scaled - inputs * pull).astype(BF16)


def scan_back_kernel(
    head, heads, state,
    values_ref, grad_ref, bc_ref, step_ref, decay_ref, sig_ref, token_ref, doc_column_ref, doc_row_ref, state_ref,
    grad_state_ref, skip_ref, rate_ref, *rest,
):
    out_values_ref, out_bc_ref, out_raw_ref = rest[-9:-6]
    score_ref, grad_score_ref, pull_ref, direct_ref, grad_in_ref, grad_out_ref = rest[-6:]
    group, groups = pl.program_id(0), pl.num_programs(0)
    width = values_ref.shape[0]
    heads_here = width // head
    in_map, out_map = bc_ref[:, :state], bc_ref[:, state:]

    def same_doc():
        return (doc_column_ref[:, :1] == doc_row_ref[:1]) & lower_ones((SPAN, SPAN))

    @pl.when(group == 0)
    def _():
        score_ref[...] = jnp.where(same_doc(), dot_last(in_map, out_map), 0.0)
        grad_score_ref[...] = jnp.zeros_like(grad_score_ref)
        grad_in_ref[...] = jnp.zeros_like(grad_in_ref)
        grad_out_ref[...] = jnp.zeros_like(grad_out_ref)

    decay, step = decay_ref[...], step_ref[...]
    token = token_ref[0]
    last = decay[:, SPAN - 1 :]
    carry = jnp.exp(decay) * token[:1]
    tail = jnp.exp(last - decay) * token[1:2]
    keep = jnp.exp(last) * token[2:3, :1]
    columns = jnp.concatenate([decay] * (LANES // heads_here), axis=0).T
    at_end = lax.broadcasted_iota(jnp.int32, (1, SPAN), 1) == SPAN - 1
    grads, tails, carried, pulls, directs = [], [], [], [], []
    for place in range(heads_here):
        rows = slice(place * head, (place + 1) * head)
        one = slice(place, place + 1)
        fade = jnp.exp(jnp.minimum(decay[one] - columns[:, one], 0.0))
        kernel = (fade * score_ref[...]).astype(BF16)
        values = values_ref[rows].astype(F32)
        driven = (values * step[one]).astype(BF16)
        grad_low = grad_ref[rows]
        grad = grad_low.astype(F32)
        grad_score_ref[...] += dot_first(driven, grad_low) * fade
        state_here, grad_state = state_ref[rows], grad_state_ref[rows]
        output = dot(driven, kernel) + dot_last(state_here, out_map) * carry[one]
        by_state = dot_last(grad_state, in_map) * tail[one]
        grad_driven = dot_last(grad_low, kernel) + by_state
        driven = driven.astype(F32)
        pull = jnp.sum(grad * output - driven * grad_driven, axis=0, keepdims=True)
        ending = jnp.sum(jnp.sum(driven * by_state, axis=0, keepdims=True), axis=1, keepdims=True)
        kept = jnp.sum(state_here.astype(F32) * grad_state.astype(F32), axis=0, keepdims=True)
        ending = ending + keep[one] * jnp.sum(kept, axis=1, keepdims=True)
        pulls.append(pull + jnp.where(at_end, ending, 0.0))
        directs.append(jnp.sum(values * grad_driven, axis=0, keepdims=True))
        grads.append(step[one] * grad_driven + skip_ref[one, :1] * grad)
        tails.append((driven * tail[one]).astype(BF16))
        carried.append((grad * carry[one]).astype(BF16))
    grad_in_ref[...] += dot_first(jnp.concatenate(tails, axis=0), grad_state_ref[...])
    grad_out_ref[...] += dot_first(jnp.concatenate(carried, axis=0), state_ref[...])
    out_values_ref[...] = jnp.concatenate(grads, axis=0).T.astype(BF16)
    here = pl.ds(pl.multiple_of(group * heads_here, heads_here), heads_here)
    pull_ref[here, :] = jnp.concatenate(pulls, axis=0)
    direct_ref[here, :] = jnp.concatenate(directs, axis=0)

    @pl.when(group == groups - 1)
    def _():
        ones = lower_ones((SPAN, SPAN)).astype(F32)
        summed = lax.dot_general(
            pull_ref[...], ones, (((1,), (1,)), ((), ())), precision=EXACT, preferred_element_type=F32
        )
        grad_step = (direct_ref[...] - rate_ref[:, :1] * summed).astype(BF16).astype(F32)
        grad_raw = grad_step * sig_ref[...]
        padded = jnp.concatenate([grad_raw, jnp.zeros((LANES - heads, SPAN), F32)], axis=0)
        out_raw_ref[...] = padded.T.astype(BF16)
        grad_score = jnp.where(same_doc(), grad_score_ref[...], 0.0).astype(BF16)
        out_bc_ref[:, :state] = (grad_in_ref[...] + dot(grad_score, out_map)).astype(BF16)
        out_bc_ref[:, state:] = (grad_out_ref[...] + dot_first(grad_score, in_map)).astype(BF16)


def conv_back_kernel(
    value_blocks,
    grad_ref, grad_bc_ref, slope_ref, slope_bc_ref, next_ref, weight_ref, valid_ref, next_valid_ref, project_ref,
):
    block = pl.program_id(0)
    length = grad_ref.shape[0]

    def back(grad_low, slope_low):
        grad = grad_low.astype(F32) * slope_low.astype(F32)
        later = next_ref[...].astype(F32)
        weight = weight_ref[...]
        valid, next_valid = valid_ref[:, :1], next_valid_ref[:, :1]
        taps = weight.shape[0]
        total = weight[taps - 1 : taps] * grad
        for ahead in range(1, taps):
            extended = jnp.concatenate(
                [jnp.where(valid >= ahead, grad, 0.0), jnp.where(next_valid >= ahead, later, 0.0)], axis=0
            )
            total = total + weight[taps - 1 - ahead : taps - ahead] * extended[ahead : ahead + length]
        project_ref[...] = total.astype(BF16)

    @pl.when(block < value_blocks)
    def _():
        back(grad_ref[...], slope_ref[...])

    @pl.when(block == value_blocks)
    def _():
        back(grad_bc_ref[...], slope_bc_ref[...])


def spec(shape, index):
    return pl.BlockSpec(shape, index)


def whole(shape):
    return pl.BlockSpec(shape, lambda *_: (0,) * len(shape))


def cost(flops, moved, transcendentals):
    return pl.CostEstimate(flops=int(flops), bytes_accessed=int(moved), transcendentals=int(transcendentals))


class Sizes:
    def __init__(self, rows, inner, heads, state, columns, taps):
        self.rows, self.inner, self.heads, self.state, self.columns, self.taps = rows, inner, heads, state, columns, taps
        self.head = inner // heads
        self.spans = rows // SPAN
        self.mixed = inner + 2 * state
        self.group_heads = 8
        self.groups = heads // self.group_heads
        self.wide = self.group_heads * self.head


def conv_forward(sizes, mixed, raw, rim, level, tokens):
    s = sizes
    rows, wide, heads, state = s.rows, s.wide, s.heads, s.state
    maps = s.inner // (2 * state)
    shapes = [
        ((s.inner, rows), BF16), ((rows, s.inner), BF16), ((rows, 2 * state), BF16), ((rows, 2 * state), BF16),
        ((s.spans, s.inner, state), BF16), ((heads, rows), F32), ((heads, rows), F32), ((heads, rows), F32),
    ]
    return pl.pallas_call(
        functools.partial(conv_kernel, s.spans, s.head, heads, state),
        grid=(s.groups,),
        in_specs=[
            spec((rows, wide), lambda g: (0, g)), spec((rows, 2 * state), lambda g: (0, maps)),
            spec((8, wide), lambda g: (0, g)), spec((8, 2 * state), lambda g: (0, maps)),
            spec((s.taps, wide), lambda g: (0, g)), spec((s.taps, 2 * state), lambda g: (0, maps)),
            spec((1, wide), lambda g: (0, g)), spec((1, 2 * state), lambda g: (0, maps)),
            whole((rows, LANES)), whole((rows, LANES)), whole((1, LANES)), whole((heads, LANES)),
            whole((s.spans, 8, SPAN)),
        ],
        out_specs=[
            spec((wide, rows), lambda g: (g, 0)), spec((rows, wide), lambda g: (0, g)), whole((rows, 2 * state)),
            whole((rows, 2 * state)), spec((s.spans, wide, state), lambda g: (0, g, 0)), whole((heads, rows)),
            whole((heads, rows)), whole((heads, rows)),
        ],
        out_shape=[jax.ShapeDtypeStruct(*one) for one in shapes],
        scratch_shapes=[pltpu.VMEM((heads, rows), F32)],
        compiler_params=PARAMS,
        cost_estimate=cost(2 * rows * s.inner * state, 10 * rows * s.inner, 2 * rows * s.inner),
    )(
        mixed, mixed, rim, rim, level["conv_weight"], level["conv_weight"], level["conv_bias"], level["conv_bias"],
        tokens["valid"], raw, level["dt_bias"], level["rate"], tokens["flags"],
    )


def span_specs(sizes, span):
    s = sizes
    return dict(
        turned=spec((s.wide, SPAN), lambda g: (g, span)),
        maps=spec((SPAN, 2 * s.state), lambda g: (span, 0)),
        rows=spec((s.group_heads, SPAN), lambda g: (g, span)),
        flags=spec((1, 8, SPAN), lambda g: (span, 0, 0)),
        doc_column=spec((SPAN, LANES), lambda g: (span, 0)),
        doc_row=spec((8, SPAN), lambda g: (0, span)),
        state=spec((s.wide, s.state), lambda g: (g, 0)),
        head=spec((s.group_heads, LANES), lambda g: (g, 0)),
        full=spec((SPAN, s.inner), lambda g: (span, 0)),
    )


ANYWHERE = pl.BlockSpec(memory_space=pl.ANY)


def scan_forward(sizes, span, conv, state_in, gate, level, tokens, earlier):
    s = sizes
    at = span_specs(s, span)
    args = [
        conv["values"], conv["maps"], conv["step"], conv["decay"], tokens["flags"], tokens["column"], tokens["row"],
        state_in, level["skip"], gate, level["gate_gain"],
    ]
    in_specs = [
        at["turned"], at["maps"], at["rows"], at["rows"], at["flags"], at["doc_column"], at["doc_row"], at["state"],
        at["head"], at["full"], whole((1, s.inner)),
    ]
    aliases = {}
    if earlier is not None:
        aliases = {len(args): 0, len(args) + 1: 1}
        args, in_specs = args + list(earlier), in_specs + [ANYWHERE] * 2
    shape = jax.ShapeDtypeStruct((s.rows, s.inner), BF16)
    return pl.pallas_call(
        functools.partial(scan_kernel, s.head, s.state),
        grid=(s.groups,),
        in_specs=in_specs,
        out_specs=[at["full"], at["full"]],
        out_shape=[shape, shape],
        scratch_shapes=[pltpu.VMEM((SPAN, SPAN), F32), pltpu.VMEM((SPAN, s.inner), BF16)],
        input_output_aliases=aliases,
        compiler_params=PARAMS,
        cost_estimate=cost(
            2 * SPAN * s.inner * (SPAN * 4 + s.state), 8 * SPAN * s.inner, s.heads * SPAN * SPAN
        ),
    )(*args)


SMALL = pl.BlockSpec(memory_space=pltpu.SMEM)


def shape_of(shape, dtype=BF16):
    return jax.ShapeDtypeStruct(shape, dtype)


def whole_specs(*arrays):
    return [whole(array.shape) for array in arrays]


def project_mixed(sizes, inputs, level, lane_mask):
    s = sizes
    parts = level["mixed"]
    args = [inputs, level["norm_gain"], level["in_down"], lane_mask, level["up_mixed"], *parts]
    width = inputs.shape[1]
    shapes = [(s.rows, width), (s.rows, LANES), (s.rows, s.mixed), (s.rows, LANES)]
    return pl.pallas_call(
        functools.partial(mixed_kernel, s.mixed, LANES),
        grid=(1,),
        in_specs=whole_specs(*args) + [SMALL],
        out_specs=[whole(shape) for shape in shapes],
        out_shape=[shape_of(shape) for shape in shapes],
        compiler_params=PARAMS,
        cost_estimate=cost(2 * s.rows * width * s.mixed, 10 * width * s.mixed, s.rows),
    )(*args, level["where"])


def gate_tile_specs(sizes, tile):
    quarter = spec((tile, sizes.columns), lambda j: (j, 0))
    half = spec((tile, sizes.columns), lambda j: (lax.rem(j, sizes.inner // (2 * tile)), 0))
    return [spec((tile, LANES), lambda j: (j, 0)), quarter, quarter, quarter, half, half, SMALL]


def project_gate(sizes, normed, narrow, level):
    s = sizes
    tile = 512
    return pl.pallas_call(
        gate_kernel,
        grid=(s.inner // tile,),
        in_specs=whole_specs(normed, narrow) + gate_tile_specs(s, tile),
        out_specs=spec((s.rows, tile), lambda j: (0, j)),
        out_shape=shape_of((s.rows, s.inner)),
        compiler_params=PARAMS,
        cost_estimate=cost(2 * s.rows * normed.shape[1] * s.inner, 10 * s.inner * s.rows, 0),
    )(normed, narrow, level["up_gate"], *level["gate"], level["where"])


def project_out(sizes, normed_out, inputs, level, lane_mask):
    s = sizes
    args = [normed_out, inputs, level["out_down"], lane_mask, level["out_up"], *level["out"]]
    shapes = [(s.rows, LANES), inputs.shape]
    return pl.pallas_call(
        out_kernel,
        grid=(1,),
        in_specs=whole_specs(*args) + [SMALL],
        out_specs=[whole(shape) for shape in shapes],
        out_shape=[shape_of(shape) for shape in shapes],
        compiler_params=PARAMS,
        cost_estimate=cost(2 * s.rows * inputs.shape[1] * s.inner, 6 * inputs.shape[1] * s.inner, 0),
    )(*args, level["where"])


def out_backward(sizes, upstream, mixed, gate, conv, level, lane_mask, tokens):
    s = sizes
    full = spec((SPAN, s.inner), lambda k: (k, 0))
    parts = level["out"]
    width = upstream.shape[1]
    return pl.pallas_call(
        functools.partial(out_back_kernel, s.head, s.heads, s.state),
        grid=(s.spans,),
        in_specs=[
            spec((SPAN, width), lambda k: (k, 0)), spec((SPAN, LANES), lambda k: (k, 0)),
            *whole_specs(level["out_up"], level["out_down"], *parts), SMALL,
            full, full, whole((1, s.inner)), spec((s.heads, SPAN), lambda k: (0, k)),
            spec((1, 8, SPAN), lambda k: (k, 0, 0)), spec((SPAN, 2 * s.state), lambda k: (k, 0)),
        ],
        out_specs=[
            full, spec((s.inner, SPAN), lambda k: (0, k)), spec((1, s.inner, s.state), lambda k: (k, 0, 0)),
            spec((SPAN, LANES), lambda k: (k, 0)),
        ],
        out_shape=[
            shape_of((s.rows, s.inner)), shape_of((s.inner, s.rows)), shape_of((s.spans, s.inner, s.state)),
            shape_of((s.rows, LANES)),
        ],
        scratch_shapes=[pltpu.VMEM((SPAN, s.inner), F32), pltpu.VMEM((SPAN, s.inner), BF16)],
        compiler_params=PARAMS,
        cost_estimate=cost(
            2 * s.rows * s.inner * (s.state + width), 14 * s.rows * s.inner, 2 * s.rows * s.inner
        ),
    )(
        upstream, lane_mask, level["out_up"], level["out_down"], *parts, level["where"], mixed, gate,
        level["gate_gain"], conv["decay"], tokens["flags"], conv["maps"],
    )


def gate_in_backward(sizes, grad_gate, level):
    s = sizes
    tile = 512
    width = 4 * s.columns + LANES
    return pl.pallas_call(
        gate_in_back_kernel,
        grid=(s.inner // tile,),
        in_specs=[spec((s.rows, tile), lambda j: (0, j))] + gate_tile_specs(s, tile),
        out_specs=whole((s.rows, width)),
        out_shape=shape_of((s.rows, width), F32),
        compiler_params=PARAMS,
        cost_estimate=cost(2 * s.rows * width * s.inner, 10 * s.inner * s.rows, 0),
    )(grad_gate, level["up_gate"], *level["gate"], level["where"])


def mixed_in_backward(sizes, grad_mixed, raw, part, inputs, upstream, level, lane_mask):
    s = sizes
    width = inputs.shape[1]
    rows = lambda columns: spec((SPAN, columns), lambda k: (k, 0))
    fixed = [level["in_down"], level["up_mixed"], *level["mixed"]]
    return pl.pallas_call(
        functools.partial(mixed_in_back_kernel, s.mixed),
        grid=(s.spans,),
        in_specs=[
            rows(s.mixed), rows(LANES), rows(width + LANES), rows(width), rows(width), whole((1, width)), rows(LANES),
            *whole_specs(*fixed), SMALL,
        ],
        out_specs=[rows(width), rows(LANES)],
        out_shape=[shape_of((s.rows, width)), shape_of((s.rows, LANES))],
        scratch_shapes=[pltpu.VMEM((SPAN, width), F32)],
        compiler_params=PARAMS,
        cost_estimate=cost(2 * s.rows * width * s.mixed, 10 * width * s.mixed, s.rows),
    )(grad_mixed, raw, part, inputs, upstream, level["norm_gain"], lane_mask, *fixed, level["where"])


def scan_backward(sizes, span, conv, grad_turned, state_in, grad_state, level, tokens, earlier):
    s = sizes
    at = span_specs(s, span)
    args = [
        conv["values"], grad_turned, conv["maps"], conv["step"], conv["decay"], conv["sig"], tokens["flags"],
        tokens["column"], tokens["row"], state_in, grad_state, level["skip"], level["rate"],
    ]
    in_specs = [
        at["turned"], at["turned"], at["maps"], at["rows"], at["rows"], spec((s.heads, SPAN), lambda g: (0, span)),
        at["flags"], at["doc_column"], at["doc_row"], at["state"], at["state"], at["head"], whole((s.heads, LANES)),
    ]
    aliases = {}
    if earlier is not None:
        aliases = {len(args) + place: place for place in range(3)}
        args, in_specs = args + list(earlier), in_specs + [ANYWHERE] * 3
    return pl.pallas_call(
        functools.partial(scan_back_kernel, s.head, s.heads, s.state),
        grid=(s.groups,),
        in_specs=in_specs,
        out_specs=[spec((SPAN, s.wide), lambda g: (span, g)), at["maps"], spec((SPAN, LANES), lambda g: (span, 0))],
        out_shape=[
            jax.ShapeDtypeStruct((s.rows, s.inner), BF16), jax.ShapeDtypeStruct((s.rows, 2 * s.state), BF16),
            jax.ShapeDtypeStruct((s.rows, LANES), BF16),
        ],
        scratch_shapes=[
            pltpu.VMEM((SPAN, SPAN), F32), pltpu.VMEM((SPAN, SPAN), F32), pltpu.VMEM((s.heads, SPAN), F32),
            pltpu.VMEM((s.heads, SPAN), F32), pltpu.VMEM((SPAN, s.state), F32), pltpu.VMEM((SPAN, s.state), F32),
        ],
        input_output_aliases=aliases,
        compiler_params=PARAMS,
        cost_estimate=cost(
            2 * SPAN * s.inner * (SPAN * 12 + 4 * s.state), 10 * SPAN * s.inner, s.heads * SPAN * SPAN
        ),
    )(*args)


def conv_backward(sizes, grad_values, grad_maps, conv, later, level, tokens):
    s = sizes
    wide = 2 * s.state
    blocks = s.inner // wide
    values = spec((s.rows, wide), lambda i: (0, jnp.minimum(i, blocks - 1)))
    mixed = lambda i: (0, i)
    return pl.pallas_call(
        functools.partial(conv_back_kernel, blocks),
        grid=(blocks + 1,),
        in_specs=[
            values, whole((s.rows, wide)), values, whole((s.rows, wide)), spec((8, wide), mixed),
            spec((s.taps, wide), mixed), whole((s.rows, LANES)), whole((8, LANES)),
        ],
        out_specs=spec((s.rows, wide), mixed),
        out_shape=shape_of((s.rows, s.mixed)),
        compiler_params=PARAMS,
        cost_estimate=cost(10 * s.rows * s.mixed, 6 * s.rows * s.mixed, 0),
    )(
        grad_values, grad_maps, conv["slope"], conv["slope_maps"], later, level["conv_weight"], tokens["valid"],
        tokens["next_valid"],
    )


def early_grads_kernel(up_ref, narrow_out_ref, normed_out_ref, grad_narrow_ref, grad_gate_ref, narrow_ref, out_ref):
    block = pl.program_id(0)

    @pl.when(block == 0)
    def _():
        out_ref[...] = dot_first(up_ref[...], narrow_out_ref[...]).astype(BF16)

    @pl.when((block == 1) | (block == 2))
    def _():
        out_ref[...] = dot_first(normed_out_ref[...], grad_narrow_ref[...]).astype(BF16)

    @pl.when(block > 2)
    def _():
        out_ref[...] = dot_first(grad_gate_ref[...], narrow_ref[...]).astype(BF16)


def early_grads(sizes, upstream, kept, grad_narrow_out, grad_gate):
    s = sizes
    wide = upstream.shape[1]
    blocks = 1 + 2 * (s.inner // wide)
    args = [upstream, kept["narrow_out"], kept["normed_out"], grad_narrow_out, grad_gate, kept["narrow"]]
    narrow = whole((s.rows, LANES))
    return pl.pallas_call(
        early_grads_kernel,
        grid=(blocks,),
        in_specs=[
            whole((s.rows, wide)), narrow, spec((s.rows, wide), lambda i: (0, jnp.clip(i - 1, 0, 1))), narrow,
            spec((s.rows, wide), lambda i: (0, jnp.clip(i - 3, 0, 1))), narrow,
        ],
        out_specs=spec((wide, LANES), lambda i: (i, 0)),
        out_shape=shape_of((blocks * wide, LANES)),
        compiler_params=PARAMS,
        cost_estimate=cost(2 * s.rows * LANES * blocks * wide, 2 * s.rows * blocks * wide, 0),
    )(*args)


def late_grads_kernel(normed_ref, grad_narrow_ref, mixed_ref, raw_ref, narrow_ref, out_ref):
    first = 0
    for left, right in ((normed_ref, grad_narrow_ref), (mixed_ref, narrow_ref), (raw_ref, narrow_ref)):
        rows = left.shape[1]
        out_ref[first : first + rows, :] = dot_first(left[...], right[...]).astype(BF16)
        first += rows
    out_ref[first:, :] = jnp.zeros((out_ref.shape[0] - first, out_ref.shape[1]), BF16)


def late_grads(sizes, kept, grad_narrow, grad_mixed, raw):
    s = sizes
    args = [kept["normed"], grad_narrow, grad_mixed, raw, kept["narrow"]]
    rows = -(-(kept["normed"].shape[1] + s.mixed + LANES) // 512) * 512
    return pl.pallas_call(
        late_grads_kernel,
        grid=(1,),
        in_specs=whole_specs(*args),
        out_specs=whole((rows, LANES)),
        out_shape=shape_of((rows, LANES)),
        compiler_params=PARAMS,
        cost_estimate=cost(2 * s.rows * LANES * rows, 2 * s.rows * rows, 0),
    )(*args)


def token_tables(doc_ids, block_rows):
    rows = doc_ids.shape[0]
    before = from_behind(doc_ids[rows - 8 :], "seq", 1)
    after = from_behind(doc_ids[:8], "seq", -1)
    extended = jnp.concatenate([before, doc_ids, after])

    def taps_behind(first, count):
        here = extended[first : first + count]
        return sum((extended[first - back : first - back + count] == here).astype(jnp.int32) for back in (1, 2, 3))

    spans = rows // SPAN
    ends = extended[7 + SPAN :: SPAN][:spans]
    starts = extended[7::SPAN][:spans]
    by_span = doc_ids.reshape(spans, SPAN)
    flags = jnp.stack(
        [
            (by_span == starts[:, None]).astype(F32),
            (by_span == ends[:, None]).astype(F32),
            jnp.broadcast_to((starts == ends).astype(F32)[:, None], (spans, SPAN)),
        ]
        + [jnp.zeros((spans, SPAN), F32)] * 5,
        axis=1,
    )
    return dict(
        valid=jnp.broadcast_to(taps_behind(8, rows)[:, None], (rows, LANES)),
        next_valid=jnp.broadcast_to(taps_behind(8 + rows, 8)[:, None], (8, LANES)),
        column=jnp.broadcast_to(doc_ids[:, None], (rows, LANES)),
        row=jnp.broadcast_to(doc_ids[None, :], (8, rows)),
        flags=flags,
        keep=(starts == ends).astype(F32),
    )


def state_hops(rows, block_rows):
    eighth = block_rows // DOCS_PER_BLOCK
    if rows // SPAN > 1 and eighth > SPAN:
        raise ValueError("unsupported block")
    return 1 if rows >= eighth else 2 * eighth // rows - 1


def pass_states(sizes, local, conv, tokens, hops, direction):
    if hops > 1:
        keep = jnp.exp(conv["decay"][:, -1]) * tokens["keep"][0]
        keep = jnp.repeat(keep, sizes.head)[:, None]
        total = local.astype(F32)
        reach = 1
        while reach < hops:
            total = total + keep * from_behind(total.astype(BF16), "seq", direction * reach).astype(F32)
            keep = keep * from_behind(keep, "seq", direction * reach)
            reach *= 2
        local = total.astype(BF16)
    return from_behind(local, "seq", direction)


def layer_forward(sizes, inputs, level, lane_mask, tokens, hops):
    s = sizes
    normed, narrow, mixed, raw = project_mixed(s, inputs, level, lane_mask)
    rim = from_behind(mixed[s.rows - 8 :], "seq", 1)
    gate = project_gate(s, normed, narrow, level)
    values, slope, maps, slope_maps, states, step, decay, sig = conv_forward(s, mixed, raw, rim, level, tokens)
    conv = dict(values=values, slope=slope, maps=maps, slope_maps=slope_maps, step=step, decay=decay, sig=sig)
    states_in = [pass_states(s, states[s.spans - 1], conv, tokens, hops, 1)]
    states_in += [states[span] for span in range(s.spans - 1)]
    outputs = None
    for span in reversed(range(s.spans)):
        outputs = scan_forward(s, span, conv, states_in[span], gate, level, tokens, outputs)
    mixed_out, normed_out = outputs
    narrow_out, result = project_out(s, normed_out, inputs, level, lane_mask)
    kept = dict(
        inputs=inputs, normed=normed, narrow=narrow, gate=gate, conv=conv, states_in=states_in, mixed_out=mixed_out,
        normed_out=normed_out, narrow_out=narrow_out,
    )
    return result, kept


def layer_backward(sizes, upstream, kept, level, lane_mask, tokens, hops):
    s = sizes
    conv = kept["conv"]
    grad_gate, turned, local, grad_narrow_out = out_backward(
        s, upstream, kept["mixed_out"], kept["gate"], conv, level, lane_mask, tokens
    )
    early = early_grads(s, upstream, kept, grad_narrow_out, grad_gate)
    grad_states = [local[span] for span in range(1, s.spans)]
    grad_states.append(pass_states(s, local[0], conv, tokens, hops, -1))
    part = gate_in_backward(s, grad_gate, level)
    outputs = None
    for span in range(s.spans):
        outputs = scan_backward(
            s, span, conv, turned, kept["states_in"][span], grad_states[span], level, tokens, outputs
        )
        if span == 0:
            edge = jnp.concatenate([outputs[0][:8], outputs[1][:8]], axis=1).astype(F32)
            slopes = jnp.concatenate([conv["slope"][:8], conv["slope_maps"][:8]], axis=1).astype(F32)
            later = from_behind((edge * slopes).astype(BF16), "seq", -1)
    grad_values, grad_maps, raw = outputs
    grad_mixed = conv_backward(s, grad_values, grad_maps, conv, later, level, tokens)
    grad_inputs, grad_narrow = mixed_in_backward(
        s, grad_mixed, raw, part, kept["inputs"], upstream, level, lane_mask
    )
    return grad_inputs, early, late_grads(s, kept, grad_narrow, grad_mixed, raw)


def make_level(sizes, weights, section, place):
    s = sizes
    level = dict(weights)
    level["norm_gain"] = weights["norm_gain"][None, :]
    level["gate_gain"] = weights["gate_gain"][None, :]
    level["conv_bias"] = weights["conv_bias"][None, :]
    level["dt_bias"] = jnp.pad(weights["dt_bias"], (0, LANES - s.heads))[None, :]
    level["rate"] = jnp.broadcast_to(jnp.exp(weights["a_log"])[:, None], (s.heads, LANES))
    level["skip"] = jnp.broadcast_to(weights["skip_gain"][:, None], (s.heads, LANES))
    turned = weights["in_up"].T
    level["up_gate"], level["up_mixed"] = turned[: s.inner], turned[s.inner :]
    level["where"] = jnp.stack([place, place ^ (1 + section), place ^ (2 - section), place ^ 3, section]).astype(jnp.int32)
    return level


def swap(value):
    return lax.ppermute(value, "section", [(0, 1), (1, 0)])


def exchange(value, axis, distance):
    count = lax.axis_size(axis)
    return lax.ppermute(value, axis, [(place, place ^ distance) for place in range(count)])


def rows_at(value, index, rows):
    return lax.dynamic_slice_in_dim(value, index * rows, rows, axis=0)


def put_at(buffer, value, *index):
    start = list(index) + [0] * (buffer.ndim - len(index))
    return lax.dynamic_update_slice(buffer, value.reshape((1,) * len(index) + value.shape), start)


def across(value, second):
    count = lax.axis_size("wshard")
    pairs = []
    for section in range(2):
        distance = 2 - section if second else 1 + section
        pairs += [(section * count + place, section * count + (place ^ distance)) for place in range(count)]
    return lax.ppermute(value, ("section", "wshard"), pairs)


def spread(quarters):
    section = lax.axis_index("section")
    others = [swap(matrix) for matrix, _, _ in quarters]
    layers, before = [], None
    for layer in range(2):
        parts = []
        for (matrix, half, step), other in zip(quarters, others, strict=True):
            own = jnp.where(section == layer, matrix, other)
            if before is not None:
                own, _ = lax.optimization_barrier((own, before))
            near = across(own, False)
            before = near
            twin = swap(near)
            apart = across(lax.dynamic_slice_in_dim(near, section * step, half, axis=0), True)
            parts.append((own, near, twin, apart, swap(apart)))
        layers.append(parts)
    return layers


def reduce_rows(value, axis):
    count, place = lax.axis_size(axis), lax.axis_index(axis)
    rows = value.shape[0] // count
    total = rows_at(value, place, rows).astype(F32)
    for distance in range(1, count):
        total = total + exchange(rows_at(value, place ^ distance, rows), axis, distance).astype(F32)
    return total


def collect_rows(value, axis):
    count, place = lax.axis_size(axis), lax.axis_index(axis)
    buffer = jnp.zeros((count,) + value.shape, value.dtype)
    for distance in range(count):
        part = exchange(value, axis, distance) if distance else value
        buffer = put_at(buffer, part, place ^ distance)
    return buffer.reshape((count * value.shape[0],) + value.shape[1:])


def sum_everywhere(packed):
    section = lax.axis_index("section")
    half = packed.shape[0] // 2
    mine = rows_at(packed, section, half).astype(F32) + swap(rows_at(packed, 1 - section, half)).astype(F32)
    mine = mine.astype(BF16)
    if lax.axis_size("seq") == 4:
        part = reduce_rows(mine, "wshard").astype(BF16)
        part = reduce_rows(part, "seq").astype(BF16)
        mine = collect_rows(collect_rows(part, "seq"), "wshard")
    else:
        mine = lax.psum(mine, ("seq", "wshard"))
    other = swap(mine)
    return jnp.concatenate([jnp.where(section == 0, mine, other), jnp.where(section == 0, other, mine)], axis=0)


VECTORS = ("norm_gain", "conv_weight", "conv_bias", "gate_gain", "dt_bias", "a_log", "skip_gain")
ADAPTERS = ("in_down", "in_up", "out_down", "out_up")


def both_layers(own):
    section = lax.axis_index("section")
    other = jax.tree.map(swap, own)
    return [
        jax.tree.map(lambda here, there: jnp.where(section == layer, here, there), own, other) for layer in range(2)
    ]


def on_device(layer_input, out_grad, doc_index, doc_adapter, in_weight, out_weight, *parameters):
    names = ("norm_gain", "conv_weight", "conv_bias", "dt_bias", "a_log", "skip_gain", "gate_gain") + ADAPTERS
    own = {name: value[0] for name, value in zip(names, parameters, strict=True)}
    section = lax.axis_index("section")
    batches, rows, width = layer_input.shape
    heads, inner = own["dt_bias"].shape[0], own["gate_gain"].shape[0]
    taps, mixed = own["conv_weight"].shape
    sizes = Sizes(rows, inner, heads, (mixed - inner) // 2, in_weight.shape[1], taps)
    block_rows = rows * lax.axis_size("seq")
    hops = state_hops(rows, block_rows)

    pick = lambda array: lax.dynamic_index_in_dim(array, section, 0, keepdims=False)
    inputs, grads, doc_ids, table = pick(layer_input), pick(out_grad), pick(doc_index), pick(doc_adapter)[0]
    tokens = token_tables(doc_ids, block_rows)
    adapter = jnp.sum(jnp.where(doc_ids[:, None] == jnp.arange(table.shape[0])[None, :], table[None, :], 0), axis=1)
    lane_mask = (adapter[:, None] == (jnp.arange(own["in_down"].shape[1]) // RANK)[None, :]).astype(F32)

    turned = in_weight[0].T
    main = sizes.mixed // 2
    groups = spread(
        [
            (turned[inner:], main + heads, main),
            (turned[:inner], inner // 2, inner // 2),
            (out_weight[0], out_weight.shape[1] // 2, out_weight.shape[1] // 2),
        ]
    )
    packed = both_layers(jnp.concatenate([own[name].reshape(-1) for name in VECTORS]))
    adapters = both_layers({name: own[name] for name in ADAPTERS})
    levels = []
    for layer in range(2):
        weights, first = dict(adapters[layer]), 0
        for name in VECTORS:
            size = own[name].size
            weights[name] = packed[layer][first : first + size].reshape(own[name].shape)
            first += size
        weights["mixed"], weights["gate"], weights["out"] = groups[layer]
        levels.append(make_level(sizes, weights, section, lax.axis_index("wshard")))

    results, kept = [], []
    rows_now = inputs
    for layer in range(2):
        rows_now, stored = layer_forward(sizes, rows_now, levels[layer], lane_mask, tokens, hops)
        results.append(rows_now)
        kept.append(stored)
    upper_grad, upper_early, upper_late = layer_backward(sizes, grads, kept[1], levels[1], lane_mask, tokens, hops)
    lower_grad, lower_early, lower_late = layer_backward(sizes, upper_grad, kept[0], levels[0], lane_mask, tokens, hops)
    first = sum_everywhere(jnp.concatenate([lower_early, upper_early, upper_late], axis=0))
    early_rows = lower_early.shape[0]
    early = jnp.where(section == 0, first[:early_rows], first[early_rows : 2 * early_rows]).astype(F32)
    late = jnp.where(section == 0, sum_everywhere(lower_late), first[2 * early_rows :]).astype(F32)
    up_out, down_out, up_gate = early[:width], early[width : width + inner], early[width + inner :]
    down_in, up_mixed = late[:width], late[width : width + mixed + heads]

    def placed(pair):
        here = jnp.where(section == 0, pair[0], pair[1])
        there = swap(jnp.where(section == 0, pair[1], pair[0]))
        first, second = jnp.where(section == 0, here, there), jnp.where(section == 0, there, here)
        return jnp.stack([first, second])[None]

    return (
        placed(results),
        placed([lower_grad, upper_grad]),
        down_in[None],
        jnp.concatenate([up_gate, up_mixed], axis=0).T[None],
        down_out[None],
        up_out.T[None],
    )


def solution(mesh):
    tokens, matrix, vector = P(None, ("wshard", "seq"), None), P("section", None, None), P("section", None)
    in_specs = (tokens, tokens, P(None, ("wshard", "seq")), P(None, "wshard", None))
    in_specs += (P("section", "wshard", None),) * 2
    in_specs += (vector, matrix) + (vector,) * 5 + (matrix,) * 4
    out_specs = (P("section", None, ("wshard", "seq"), None),) * 2 + (matrix,) * 4
    return jax.shard_map(on_device, mesh=mesh, in_specs=in_specs, out_specs=out_specs, check_vma=False)
```

```python
import functools

import jax
import jax.numpy as jnp
from jax import lax
from jax.experimental import pallas as pl
from jax.experimental.pallas import tpu as pltpu
from jax.sharding import PartitionSpec as P

SPAN = 256
RANK = 16
LANES = 128
DOCS_PER_BLOCK = 8
EPSILON = 1e-05
EXACT = lax.Precision.HIGHEST
SEQ, WSHARD, SECTION = "seq", "wshard", "section"
BF16 = jnp.bfloat16
F32 = jnp.float32
PARAMS = pltpu.CompilerParams(vmem_limit_bytes=20 * 1024 * 1024)


class Bag:
    def __init__(self, **fields):
        self.__dict__.update(fields)


def tie(value, *others):
    return lax.optimization_barrier((value, *others))[0]


def from_behind(value, axis, steps):
    count = lax.axis_size(axis)
    initial, last = (max(0, -steps), min(count, count - steps))
    return lax.ppermute(value, axis, [(source, source + steps) for source in range(initial, last)])


def dot(left, right):
    return jnp.dot(left, right, preferred_element_type=F32)


def dot_last(left, right):
    return lax.dot_general(left, right, (((1,), (1,)), ((), ())), preferred_element_type=F32)


def dot_first(left, right):
    return lax.dot_general(left, right, (((0,), (0,)), ((), ())), preferred_element_type=F32)


def rms_rate(values):
    return lax.rsqrt(jnp.mean(values * values, axis=-1, keepdims=True) + EPSILON)


def sigmoid(v):
    return 1.0 / (1.0 + jnp.exp(-v))


def lower_ones(shape):
    rows = lax.broadcasted_iota(jnp.int32, shape, 0)
    columns = lax.broadcasted_iota(jnp.int32, shape, 1)
    return rows <= columns


def conv_rows(rows, rim, weight, offset, valid):
    length = rows.shape[0]
    extended = jnp.concatenate([rim, rows], axis=0)
    taps = weight.shape[0]
    total = offset + weight[taps - 1 : taps] * rows
    for back in range(1, taps):
        shifted = extended[8 - back : 8 - back + length]
        total = total + jnp.where(valid >= back, shifted, 0.0) * weight[taps - 1 - back : taps - back]
    gate = sigmoid(total)
    active = total * gate
    return active, gate + active * (1.0 - gate)


def taps_at(vector_ref, places, first, width):
    rows = [vector_ref[:, pl.ds(pl.multiple_of(place + first, LANES), width)] for place in places]
    return jnp.concatenate(rows[:-1], axis=0), rows[-1]


def conv_kernel(
    spans, head, heads, state, places,
    mixed_ref, mixed_bc_ref, rim_ref, rim_bc_ref, vector_ref, valid_ref, raw_ref, head_ref, token_ref,
    values_ref, slope_ref, bc_ref, slope_bc_ref, step_ref, decay_ref, sig_ref, *rest,
):
    state_refs, tail_ref = rest[:-1], rest[-1]
    group = pl.program_id(0)
    valid = valid_ref[:, :1]
    width = mixed_ref.shape[1]
    heads_here = width // head

    @pl.when(group == 0)
    def _():
        weight, offset = taps_at(vector_ref, places, pl.num_programs(0) * width, 2 * state)
        active, slope = conv_rows(
            mixed_bc_ref[...].astype(F32), rim_bc_ref[...].astype(F32), weight, offset, valid
        )
        bc_ref[...] = active.astype(BF16)
        slope_bc_ref[...] = slope.astype(BF16)
        raw = raw_ref[...].astype(F32).T[:heads] + head_ref[:, 2:3]
        step = (jnp.maximum(raw, 0.0) + jnp.log1p(jnp.exp(-jnp.abs(raw)))).astype(BF16).astype(F32)
        step_ref[...] = step
        sig_ref[...] = sigmoid(raw)
        drop = -(step * head_ref[:, :1])
        ones = lower_ones((SPAN, SPAN)).astype(F32)
        for span in range(spans):
            here = slice(span * SPAN, (span + 1) * SPAN)
            decay = jnp.dot(drop[:, here], ones, precision=EXACT, preferred_element_type=F32)
            decay_ref[:, here] = decay
            tail = jnp.exp(decay[:, SPAN - 1 :] - decay) * token_ref[span][1:2]
            tail_ref[:, here] = tail * step[:, here]

    weight, offset = taps_at(vector_ref, places, group * width, width)
    active, slope = conv_rows(
        mixed_ref[...].astype(F32), rim_ref[...].astype(F32), weight, offset, valid
    )
    slope_ref[...] = slope.astype(BF16)
    turned = active.T
    low = turned.astype(BF16)
    values_ref[...] = low
    low = low.astype(F32)
    first = pl.multiple_of(group * heads_here, heads_here)
    tail_rows = tail_ref[pl.ds(first, heads_here), :]
    for span in range(spans):
        here = slice(span * SPAN, (span + 1) * SPAN)
        driven = jnp.concatenate(
            [
                (low[place * head : (place + 1) * head, here] * tail_rows[place : place + 1, here]).astype(BF16)
                for place in range(heads_here)
            ],
            axis=0,
        )
        state_refs[span][...] = dot(driven, bc_ref[here, :state]).astype(BF16)


def scan_kernel(
    head, state, gain,
    values_ref, bc_ref, step_ref, decay_ref, token_ref, doc_column_ref, doc_row_ref, state_ref, head_ref, gate_ref,
    vector_ref, *rest,
):
    mixed_ref, normed_ref, score_ref, scanned_ref = rest[-4:]
    group, groups = pl.program_id(0), pl.num_programs(0)
    width = values_ref.shape[0]
    heads_here = width // head

    @pl.when(group == 0)
    def _():
        score = dot_last(bc_ref[:, :state], bc_ref[:, state:])
        same = (doc_column_ref[:, :1] == doc_row_ref[:1]) & lower_ones((SPAN, SPAN))
        score_ref[...] = jnp.where(same, score, 0.0)

    decay, step = decay_ref[...], step_ref[...]
    carry = jnp.exp(decay) * token_ref[0][:1]
    columns = jnp.concatenate([decay] * (LANES // heads_here), axis=0).T
    out_map = bc_ref[:, state:]
    parts = []
    for place in range(heads_here):
        rows = slice(place * head, (place + 1) * head)
        one = slice(place, place + 1)
        kernel = (jnp.exp(jnp.minimum(decay[one] - columns[:, one], 0.0)) * score_ref[...]).astype(BF16)
        values = values_ref[rows].astype(F32)
        driven = (values * step[one]).astype(BF16)
        before = dot_last(state_ref[rows], out_map) * carry[one]
        parts.append(dot(driven, kernel) + before + head_ref[one, 1:2] * values)
    turned = jnp.concatenate(parts, axis=0).T
    scanned_ref[:, pl.ds(pl.multiple_of(group * width, width), width)] = turned.astype(BF16)

    @pl.when(group == groups - 1)
    def _():
        def rows_at(index, _):
            rows = pl.ds(pl.multiple_of(index * 16, 16), 16)
            mixed = scanned_ref[rows, :]
            mixed_ref[rows, :] = mixed
            gate = gate_ref[rows, :].astype(F32)
            gated = mixed.astype(F32) * (gate * sigmoid(gate))
            normed_ref[rows, :] = (gated * rms_rate(gated) * vector_ref[:, gain : gain + gated.shape[1]]).astype(BF16)
            return 0

        lax.fori_loop(0, SPAN // 16, rows_at, 0)


def out_back_kernel(
    head, heads, state, gain,
    up_ref, lane_ref, up_out_ref, down_out_ref, first_ref, second_ref, third_ref, near_ref, far_ref, where_ref,
    mixed_ref, gate_ref, vector_ref, decay_ref, token_ref, bc_ref,
    project_ref, turned_ref, narrow_ref, *rest,
):
    state_refs, grad_ref, grad_mixed_ref = rest[:-2], rest[-2], rest[-1]
    width = mixed_ref.shape[1]
    up = up_ref[...]
    narrow = (dot_last(up, up_out_ref[...]) * lane_ref[...]).astype(BF16)
    narrow_ref[...] = narrow
    left = jnp.concatenate([up, narrow], axis=1)
    for offset, part in out_places(where_ref, (first_ref, second_ref, third_ref), near_ref, far_ref):
        here = pl.ds(offset, part.shape[0])
        grad_ref[:, here] = dot_last(left, jnp.concatenate([part[...], down_out_ref[here, :]], axis=1))

    def rows_at(index, _):
        rows = pl.ds(pl.multiple_of(index * 16, 16), 16)
        mixed = mixed_ref[rows, :].astype(F32)
        gate = gate_ref[rows, :].astype(F32)
        share = sigmoid(gate)
        silu = gate * share
        gated = mixed * silu
        grad = grad_ref[rows, :] * vector_ref[:, gain : gain + width]
        rate = rms_rate(gated)
        pull = jnp.mean(gated * grad, axis=-1, keepdims=True) * rate * rate * rate
        grad_gated = rate * grad - gated * pull
        project_ref[rows, :] = (grad_gated * mixed * (share + silu * (1.0 - share))).astype(BF16)
        grad_mixed_ref[rows, :] = (grad_gated * silu).astype(BF16)
        return 0

    lax.fori_loop(0, SPAN // 16, rows_at, 0)
    carry = jnp.exp(decay_ref[...]) * token_ref[0][:1]
    out_map = bc_ref[:, state:]
    wide = 512
    for first in range(0, width, wide):
        low = grad_mixed_ref[:, first : first + wide].astype(F32).T
        turned_ref[first : first + wide, :] = low.astype(BF16)
        scaled = [
            (low[place * head : (place + 1) * head] * carry[first // head + place : first // head + place + 1]).astype(BF16)
            for place in range(wide // head)
        ]
        local = dot(jnp.concatenate(scaled, axis=0), out_map).astype(BF16)
        for span, state_ref in enumerate(state_refs):

            @pl.when(pl.program_id(0) == span)
            def _(state_ref=state_ref, first=first, local=local):
                state_ref[first : first + wide, :] = local


def aligned(value, unit):
    return pl.multiple_of(value * unit, unit)


def out_places(where_ref, parts, near, far):
    rows, half = parts[0].shape[0], near.shape[0]
    places = [(aligned(where_ref[place], rows), part) for place, part in enumerate(parts)]
    apart = where_ref[3] * 2
    places.append((aligned(apart + where_ref[4], half), near))
    places.append((aligned(apart + 1 - where_ref[4], half), far))
    return places


def in_columns(ref, where_ref, parts):
    columns = ref.shape[1] // parts
    return [ref[:, pl.ds(aligned(where_ref[place], columns), columns)] for place in range(parts)]


def mixed_kernel(
    main, lanes, gain,
    input_ref, vector_ref, down_ref, lane_ref, up_ref, first_ref, second_ref, third_ref, near_ref, far_ref, where_ref,
    normed_ref, narrow_ref, mixed_ref, raw_ref, rim_ref,
):
    rows = input_ref.shape[0]
    inputs = input_ref[...].astype(F32)
    normed = (inputs * rms_rate(inputs) * vector_ref[:, gain : gain + inputs.shape[1]]).astype(BF16)
    normed_ref[...] = normed
    narrow = (dot(normed, down_ref[...]) * lane_ref[...]).astype(BF16)
    narrow_ref[...] = narrow
    left = jnp.concatenate(in_columns(normed_ref, where_ref, 4) + [narrow], axis=1)
    first = where_ref[4] == 0
    half, whole_rows = near_ref.shape[0], first_ref.shape[0]
    before = up_ref.shape[0] - whole_rows
    step = main // 6

    def product(start, size):
        here = slice(start, start + size)
        if start < main // 2:
            there = slice(start, start + size)
            apart = jnp.where(first, near_ref[there], far_ref[there])
        else:
            there = slice(start - whole_rows + half, start - whole_rows + half + size)
            apart = jnp.where(first, far_ref[there], near_ref[there])
        up = up_ref[before + start : before + start + size]
        parts = [first_ref[here], second_ref[here], third_ref[here], apart, up]
        return dot_last(left, jnp.concatenate(parts, axis=1))

    for start in range(0, main, step):
        low = product(start, step).astype(BF16)
        mixed_ref[:, start : start + step] = low
        rim_ref[:, start : start + step] = low[rows - 8 :]
    extra = whole_rows - main
    raw_ref[...] = jnp.concatenate([product(main, extra), jnp.zeros((rows, lanes - extra), F32)], axis=1).astype(BF16)


def gate_kernel(normed_ref, narrow_ref, up_ref, first_ref, second_ref, third_ref, near_ref, far_ref, where_ref, gate_ref):
    tile, tiles = pl.program_id(0), pl.num_programs(0)
    near = (where_ref[4] == 0) == (tile < tiles // 2)
    left = jnp.concatenate(in_columns(normed_ref, where_ref, 4) + [narrow_ref[...]], axis=1)
    apart = jnp.where(near, near_ref[...], far_ref[...])
    right = jnp.concatenate([first_ref[...], second_ref[...], third_ref[...], apart, up_ref[...]], axis=1)
    gate_ref[...] = dot_last(left, right).astype(BF16)


def out_kernel(
    normed_ref, input_ref, down_ref, lane_ref, up_ref, first_ref, second_ref, third_ref, near_ref, far_ref, where_ref,
    narrow_ref, out_ref,
):
    narrow = (dot(normed_ref[...], down_ref[...]) * lane_ref[...]).astype(BF16)
    narrow_ref[...] = narrow
    places = out_places(where_ref, (first_ref, second_ref, third_ref), near_ref, far_ref)
    left = [normed_ref[:, pl.ds(offset, part.shape[0])] for offset, part in places]
    left = jnp.concatenate(left + [narrow], axis=1)
    wide = 256
    for start in range(0, out_ref.shape[1], wide):
        here = slice(start, start + wide)
        right = jnp.concatenate([part[:, here] for _, part in places] + [up_ref[:, here]], axis=0)
        out_ref[:, here] = (input_ref[:, here].astype(F32) + dot(left, right)).astype(BF16)


def gate_in_back_kernel(
    grad_ref, up_ref, first_ref, second_ref, third_ref, near_ref, far_ref, where_ref, out_ref
):
    tile, tiles = pl.program_id(0), pl.num_programs(0)
    near = (where_ref[4] == 0) == (tile < tiles // 2)
    apart = jnp.where(near, near_ref[...], far_ref[...])
    right = jnp.concatenate([first_ref[...], second_ref[...], third_ref[...], apart, up_ref[...]], axis=1)
    product = dot(grad_ref[...], right)

    @pl.when(tile == 0)
    def _():
        out_ref[...] = product

    @pl.when(tile > 0)
    def _():
        out_ref[...] += product


def mixed_in_back_kernel(
    main, gain,
    grad_ref, raw_ref, part_ref, input_ref, up_stream_ref, vector_ref, lane_ref, down_ref, up_ref,
    first_ref, second_ref, third_ref, near_ref, far_ref, where_ref,
    out_ref, narrow_ref, total_ref,
):
    first = where_ref[4] == 0
    half, whole_rows = near_ref.shape[0], first_ref.shape[0]
    before = up_ref.shape[0] - whole_rows
    width = input_ref.shape[1]
    columns = width // 4

    def right(start, size):
        here = slice(start, start + size)
        if start < main // 2:
            there = slice(start, start + size)
            apart = jnp.where(first, near_ref[there], far_ref[there])
        else:
            there = slice(start - whole_rows + half, start - whole_rows + half + size)
            apart = jnp.where(first, far_ref[there], near_ref[there])
        up = up_ref[before + start : before + start + size]
        return jnp.concatenate([first_ref[here], second_ref[here], third_ref[here], apart, up], axis=1)

    total = part_ref[...] + dot(grad_ref[:, : main // 2], right(0, main // 2))
    total = total + dot(grad_ref[:, main // 2 :], right(main // 2, main // 2))
    extra = whole_rows - main
    total = total + dot(raw_ref[:, :extra], right(main, extra))
    narrow = (total[:, width:] * lane_ref[...]).astype(BF16)
    narrow_ref[...] = narrow
    for place in range(4):
        total_ref[:, pl.ds(aligned(where_ref[place], columns), columns)] = total[:, place * columns : (place + 1) * columns]
    scaled = (total_ref[...] + dot_last(narrow, down_ref[...])) * vector_ref[:, gain : gain + width]
    inputs = input_ref[...].astype(F32)
    rate = rms_rate(inputs)
    pull = jnp.mean(inputs * scaled, axis=-1, keepdims=True) * rate * rate * rate
    out_ref[...] = (up_stream_ref[...].astype(F32) + rate * scaled - inputs * pull).astype(BF16)


def scan_back_kernel(
    head, heads, state, edge,
    values_ref, grad_ref, bc_ref, step_ref, decay_ref, sig_ref, token_ref, doc_column_ref, doc_row_ref, state_ref,
    grad_state_ref, head_ref, rate_ref, slope_ref, slope_bc_ref, *rest,
):
    outputs = rest[:-6]
    if edge:
        outputs, edge_ref = outputs[:-1], outputs[-1]
    out_values_ref, out_bc_ref, out_raw_ref = outputs[-3:]
    score_ref, grad_score_ref, pull_ref, direct_ref, grad_in_ref, grad_out_ref = rest[-6:]
    group, groups = pl.program_id(0), pl.num_programs(0)
    width = values_ref.shape[0]
    heads_here = width // head
    in_map, out_map = bc_ref[:, :state], bc_ref[:, state:]

    def same_doc():
        return (doc_column_ref[:, :1] == doc_row_ref[:1]) & lower_ones((SPAN, SPAN))

    @pl.when(group == 0)
    def _():
        score_ref[...] = jnp.where(same_doc(), dot_last(in_map, out_map), 0.0)
        grad_score_ref[...] = jnp.zeros_like(grad_score_ref)
        grad_in_ref[...] = jnp.zeros_like(grad_in_ref)
        grad_out_ref[...] = jnp.zeros_like(grad_out_ref)

    decay, step = decay_ref[...], step_ref[...]
    token = token_ref[0]
    last = decay[:, SPAN - 1 :]
    carry = jnp.exp(decay) * token[:1]
    tail = jnp.exp(last - decay) * token[1:2]
    keep = jnp.exp(last) * token[2:3, :1]
    columns = jnp.concatenate([decay] * (LANES // heads_here), axis=0).T
    at_end = lax.broadcasted_iota(jnp.int32, (1, SPAN), 1) == SPAN - 1
    grads, tails, carried, pulls, directs = [], [], [], [], []
    for place in range(heads_here):
        rows = slice(place * head, (place + 1) * head)
        one = slice(place, place + 1)
        fade = jnp.exp(jnp.minimum(decay[one] - columns[:, one], 0.0))
        kernel = (fade * score_ref[...]).astype(BF16)
        values = values_ref[rows].astype(F32)
        driven = (values * step[one]).astype(BF16)
        grad_low = grad_ref[rows]
        grad = grad_low.astype(F32)
        grad_score_ref[...] += dot_first(driven, grad_low) * fade
        state_here, grad_state = state_ref[rows], grad_state_ref[rows]
        output = dot(driven, kernel) + dot_last(state_here, out_map) * carry[one]
        by_state = dot_last(grad_state, in_map) * tail[one]
        grad_driven = dot_last(grad_low, kernel) + by_state
        driven = driven.astype(F32)
        pull = jnp.sum(grad * output - driven * grad_driven, axis=0, keepdims=True)
        ending = jnp.sum(jnp.sum(driven * by_state, axis=0, keepdims=True), axis=1, keepdims=True)
        kept = jnp.sum(state_here.astype(F32) * grad_state.astype(F32), axis=0, keepdims=True)
        ending = ending + keep[one] * jnp.sum(kept, axis=1, keepdims=True)
        pulls.append(pull + jnp.where(at_end, ending, 0.0))
        directs.append(jnp.sum(values * grad_driven, axis=0, keepdims=True))
        grads.append(step[one] * grad_driven + head_ref[one, 1:2] * grad)
        tails.append((driven * tail[one]).astype(BF16))
        carried.append((grad * carry[one]).astype(BF16))
    grad_in_ref[...] += dot_first(jnp.concatenate(tails, axis=0), grad_state_ref[...])
    grad_out_ref[...] += dot_first(jnp.concatenate(carried, axis=0), state_ref[...])
    grads = jnp.concatenate(grads, axis=0).T.astype(BF16)
    out_values_ref[...] = grads
    if edge:
        product = grads[:8].astype(F32) * slope_ref[...][:8].astype(F32)
        edge_ref[:, pl.ds(pl.multiple_of(group * width, width), width)] = product.astype(BF16)
    here = pl.ds(pl.multiple_of(group * heads_here, heads_here), heads_here)
    pull_ref[here, :] = jnp.concatenate(pulls, axis=0)
    direct_ref[here, :] = jnp.concatenate(directs, axis=0)

    @pl.when(group == groups - 1)
    def _():
        ones = lower_ones((SPAN, SPAN)).astype(F32)
        summed = lax.dot_general(
            pull_ref[...], ones, (((1,), (1,)), ((), ())), precision=EXACT, preferred_element_type=F32
        )
        grad_step = (direct_ref[...] - rate_ref[:, :1] * summed).astype(BF16).astype(F32)
        grad_raw = grad_step * sig_ref[...]
        padded = jnp.concatenate([grad_raw, jnp.zeros((LANES - heads, SPAN), F32)], axis=0)
        out_raw_ref[...] = padded.T.astype(BF16)
        grad_score = jnp.where(same_doc(), grad_score_ref[...], 0.0).astype(BF16)
        grad_in = grad_in_ref[...] + dot(grad_score, out_map)
        grad_out = grad_out_ref[...] + dot_first(grad_score, in_map)
        low = jnp.concatenate([grad_in, grad_out], axis=1).astype(BF16)
        out_bc_ref[...] = low
        if edge:
            product = low[:8].astype(F32) * slope_bc_ref[...][:8].astype(F32)
            edge_ref[:, groups * width :] = product.astype(BF16)


def conv_back_kernel(
    value_blocks, places,
    grad_ref, grad_bc_ref, slope_ref, slope_bc_ref, next_ref, vector_ref, valid_ref, next_valid_ref, project_ref,
):
    block = pl.program_id(0)
    length = grad_ref.shape[0]

    def back(grad_low, slope_low):
        grad = grad_low.astype(F32) * slope_low.astype(F32)
        later = next_ref[...].astype(F32)
        weight, _ = taps_at(vector_ref, places, block * grad.shape[1], grad.shape[1])
        valid, next_valid = valid_ref[:, :1], next_valid_ref[:, :1]
        taps = weight.shape[0]
        total = weight[taps - 1 : taps] * grad
        for ahead in range(1, taps):
            extended = jnp.concatenate(
                [jnp.where(valid >= ahead, grad, 0.0), jnp.where(next_valid >= ahead, later, 0.0)], axis=0
            )
            total = total + weight[taps - 1 - ahead : taps - ahead] * extended[ahead : ahead + length]
        project_ref[...] = total.astype(BF16)

    @pl.when(block < value_blocks)
    def _():
        back(grad_ref[...], slope_ref[...])

    @pl.when(block == value_blocks)
    def _():
        back(grad_bc_ref[...], slope_bc_ref[...])


def spec(shape, index):
    return pl.BlockSpec(shape, index)


def whole(shape):
    return pl.BlockSpec(shape, lambda *_: (0,) * len(shape))


def cost(flops, moved, transcendentals):
    return pl.CostEstimate(flops=int(flops), bytes_accessed=int(moved), transcendentals=int(transcendentals))


class Sizes:
    def __init__(self, rows, inner, heads, state, columns, taps):
        self.rows, self.inner, self.heads, self.state, self.columns, self.taps = rows, inner, heads, state, columns, taps
        self.head = inner // heads
        self.spans = rows // SPAN
        self.mixed = inner + 2 * state
        self.group_heads = 8
        self.groups = heads // self.group_heads
        self.wide = self.group_heads * self.head
        self.places = tuple(tap * self.mixed for tap in range(taps + 1))
        self.gate_gain = (taps + 1) * self.mixed
        self.norm_gain = self.gate_gain + inner


def conv_forward(sizes, mixed, raw, rim, level, tokens):
    s = sizes
    rows, wide, heads, state = s.rows, s.wide, s.heads, s.state
    maps = s.inner // (2 * state)
    shapes = [
        ((s.inner, rows), BF16), ((rows, s.inner), BF16), ((rows, 2 * state), BF16), ((rows, 2 * state), BF16),
        ((heads, rows), F32), ((heads, rows), F32), ((heads, rows), F32),
    ] + [((s.inner, state), BF16)] * s.spans
    args = [level.vector, tokens.valid, raw, level.heads, tokens.flags]
    outputs = pl.pallas_call(
        functools.partial(conv_kernel, s.spans, s.head, heads, state, s.places),
        grid=(s.groups,),
        in_specs=[
            spec((rows, wide), lambda g: (0, g)), spec((rows, 2 * state), lambda g: (0, maps)),
            spec((8, wide), lambda g: (0, g)), spec((8, 2 * state), lambda g: (0, maps)), *whole_specs(*args),
        ],
        out_specs=[
            spec((wide, rows), lambda g: (g, 0)), spec((rows, wide), lambda g: (0, g)), whole((rows, 2 * state)),
            whole((rows, 2 * state)), whole((heads, rows)), whole((heads, rows)), whole((heads, rows)),
        ] + [spec((wide, state), lambda g: (g, 0))] * s.spans,
        out_shape=[jax.ShapeDtypeStruct(*one) for one in shapes],
        scratch_shapes=[pltpu.VMEM((heads, rows), F32)],
        compiler_params=PARAMS,
        cost_estimate=cost(2 * rows * s.inner * state, 10 * rows * s.inner, 2 * rows * s.inner),
    )(mixed, mixed, rim, rim, *args)
    return outputs[:7], outputs[7:]


def span_specs(sizes, span):
    s = sizes
    return Bag(
        turned=spec((s.wide, SPAN), lambda g: (g, span)),
        maps=spec((SPAN, 2 * s.state), lambda g: (span, 0)),
        rows=spec((s.group_heads, SPAN), lambda g: (g, span)),
        flags=spec((1, 8, SPAN), lambda g: (span, 0, 0)),
        doc_column=spec((SPAN, LANES), lambda g: (span, 0)),
        doc_row=spec((8, SPAN), lambda g: (0, span)),
        state=spec((s.wide, s.state), lambda g: (g, 0)),
        head=spec((s.group_heads, LANES), lambda g: (g, 0)),
        full=spec((SPAN, s.inner), lambda g: (span, 0)),
    )


ANYWHERE = pl.BlockSpec(memory_space=pl.ANY)


def scan_forward(sizes, span, conv, state_in, gate, level, tokens, earlier):
    s = sizes
    at = span_specs(s, span)
    args = [
        conv.values, conv.maps, conv.step, conv.decay, tokens.flags, tokens.column, tokens.row,
        state_in, level.heads, gate, level.vector,
    ]
    in_specs = [
        at.turned, at.maps, at.rows, at.rows, at.flags, at.doc_column, at.doc_row, at.state,
        at.head, at.full, whole(level.vector.shape),
    ]
    aliases = {}
    if earlier is not None:
        aliases = {len(args): 0, len(args) + 1: 1}
        args, in_specs = args + list(earlier), in_specs + [ANYWHERE] * 2
    shape = jax.ShapeDtypeStruct((s.rows, s.inner), BF16)
    return pl.pallas_call(
        functools.partial(scan_kernel, s.head, s.state, s.gate_gain),
        grid=(s.groups,),
        in_specs=in_specs,
        out_specs=[at.full, at.full],
        out_shape=[shape, shape],
        scratch_shapes=[pltpu.VMEM((SPAN, SPAN), F32), pltpu.VMEM((SPAN, s.inner), BF16)],
        input_output_aliases=aliases,
        compiler_params=PARAMS,
        cost_estimate=cost(
            2 * SPAN * s.inner * (SPAN * 4 + s.state), 8 * SPAN * s.inner, s.heads * SPAN * SPAN
        ),
    )(*args)


SMALL = pl.BlockSpec(memory_space=pltpu.SMEM)


def shape_of(shape, dtype=BF16):
    return jax.ShapeDtypeStruct(shape, dtype)


def whole_specs(*arrays):
    return [whole(array.shape) for array in arrays]


def project_mixed(sizes, inputs, level, lane_mask):
    s = sizes
    parts = level.mixed
    args = [inputs, level.vector, level.in_down, lane_mask, level.in_up, *parts]
    width = inputs.shape[1]
    shapes = [(s.rows, width), (s.rows, LANES), (s.rows, s.mixed), (s.rows, LANES), (8, s.mixed)]
    return pl.pallas_call(
        functools.partial(mixed_kernel, s.mixed, LANES, s.norm_gain),
        grid=(1,),
        in_specs=whole_specs(*args) + [SMALL],
        out_specs=[whole(shape) for shape in shapes],
        out_shape=[shape_of(shape) for shape in shapes],
        compiler_params=PARAMS,
        cost_estimate=cost(2 * s.rows * width * s.mixed, 10 * width * s.mixed, s.rows),
    )(*args, level.where)


def gate_tile_specs(sizes, tile):
    quarter = spec((tile, sizes.columns), lambda j: (j, 0))
    half = spec((tile, sizes.columns), lambda j: (lax.rem(j, sizes.inner // (2 * tile)), 0))
    return [spec((tile, LANES), lambda j: (j, 0)), quarter, quarter, quarter, half, half, SMALL]


def project_gate(sizes, normed, narrow, level):
    s = sizes
    tile = 512
    return pl.pallas_call(
        gate_kernel,
        grid=(s.inner // tile,),
        in_specs=whole_specs(normed, narrow) + gate_tile_specs(s, tile),
        out_specs=spec((s.rows, tile), lambda j: (0, j)),
        out_shape=shape_of((s.rows, s.inner)),
        compiler_params=PARAMS,
        cost_estimate=cost(2 * s.rows * normed.shape[1] * s.inner, 10 * s.inner * s.rows, 0),
    )(normed, narrow, level.in_up, *level.gate, level.where)


def project_out(sizes, normed_out, inputs, level, lane_mask):
    s = sizes
    args = [normed_out, inputs, level.out_down, lane_mask, level.out_up, *level.out]
    shapes = [(s.rows, LANES), inputs.shape]
    return pl.pallas_call(
        out_kernel,
        grid=(1,),
        in_specs=whole_specs(*args) + [SMALL],
        out_specs=[whole(shape) for shape in shapes],
        out_shape=[shape_of(shape) for shape in shapes],
        compiler_params=PARAMS,
        cost_estimate=cost(2 * s.rows * inputs.shape[1] * s.inner, 6 * inputs.shape[1] * s.inner, 0),
    )(*args, level.where)


def out_backward(sizes, upstream, mixed, gate, conv, level, lane_mask, tokens):
    s = sizes
    full = spec((SPAN, s.inner), lambda k: (k, 0))
    parts = level.out
    width = upstream.shape[1]
    return pl.pallas_call(
        functools.partial(out_back_kernel, s.head, s.heads, s.state, s.gate_gain),
        grid=(s.spans,),
        in_specs=[
            spec((SPAN, width), lambda k: (k, 0)), spec((SPAN, LANES), lambda k: (k, 0)),
            *whole_specs(level.out_up, level.out_down, *parts), SMALL,
            full, full, whole(level.vector.shape), spec((s.heads, SPAN), lambda k: (0, k)),
            spec((1, 8, SPAN), lambda k: (k, 0, 0)), spec((SPAN, 2 * s.state), lambda k: (k, 0)),
        ],
        out_specs=[
            full, spec((s.inner, SPAN), lambda k: (0, k)), spec((SPAN, LANES), lambda k: (k, 0)),
        ] + [whole((s.inner, s.state))] * s.spans,
        out_shape=[
            shape_of((s.rows, s.inner)), shape_of((s.inner, s.rows)), shape_of((s.rows, LANES)),
        ] + [shape_of((s.inner, s.state))] * s.spans,
        scratch_shapes=[pltpu.VMEM((SPAN, s.inner), F32), pltpu.VMEM((SPAN, s.inner), BF16)],
        compiler_params=PARAMS,
        cost_estimate=cost(
            2 * s.rows * s.inner * (s.state + width), 14 * s.rows * s.inner, 2 * s.rows * s.inner
        ),
    )(
        upstream, lane_mask, level.out_up, level.out_down, *parts, level.where, mixed, gate,
        level.vector, conv.decay, tokens.flags, conv.maps,
    )


def gate_in_backward(sizes, grad_gate, level):
    s = sizes
    tile = 512
    width = 4 * s.columns + LANES
    return pl.pallas_call(
        gate_in_back_kernel,
        grid=(s.inner // tile,),
        in_specs=[spec((s.rows, tile), lambda j: (0, j))] + gate_tile_specs(s, tile),
        out_specs=whole((s.rows, width)),
        out_shape=shape_of((s.rows, width), F32),
        compiler_params=PARAMS,
        cost_estimate=cost(2 * s.rows * width * s.inner, 10 * s.inner * s.rows, 0),
    )(grad_gate, level.in_up, *level.gate, level.where)


def mixed_in_backward(sizes, grad_mixed, raw, part, inputs, upstream, level, lane_mask):
    s = sizes
    width = inputs.shape[1]
    rows = lambda columns: spec((SPAN, columns), lambda k: (k, 0))
    fixed = [level.in_down, level.in_up, *level.mixed]
    return pl.pallas_call(
        functools.partial(mixed_in_back_kernel, s.mixed, s.norm_gain),
        grid=(s.spans,),
        in_specs=[
            rows(s.mixed), rows(LANES), rows(width + LANES), rows(width), rows(width), whole(level.vector.shape), rows(LANES),
            *whole_specs(*fixed), SMALL,
        ],
        out_specs=[rows(width), rows(LANES)],
        out_shape=[shape_of((s.rows, width)), shape_of((s.rows, LANES))],
        scratch_shapes=[pltpu.VMEM((SPAN, width), F32)],
        compiler_params=PARAMS,
        cost_estimate=cost(2 * s.rows * width * s.mixed, 10 * width * s.mixed, s.rows),
    )(grad_mixed, raw, part, inputs, upstream, level.vector, lane_mask, *fixed, level.where)


def scan_backward(sizes, span, conv, grad_turned, state_in, grad_state, level, tokens, earlier):
    s = sizes
    at = span_specs(s, span)
    args = [
        conv.values, grad_turned, conv.maps, conv.step, conv.decay, conv.sig, tokens.flags, tokens.column, tokens.row,
        state_in, grad_state, level.heads, level.heads, conv.slope, conv.slope_maps,
    ]
    in_specs = [
        at.turned, at.turned, at.maps, at.rows, at.rows, spec((s.heads, SPAN), lambda g: (0, span)), at.flags,
        at.doc_column, at.doc_row, at.state, at.state, at.head, whole((s.heads, LANES)),
        spec((16, s.wide), lambda g: (0, g)), spec((16, 2 * s.state), lambda g: (0, 0)),
    ]
    aliases = {}
    if earlier is not None:
        aliases = {len(args) + place: place for place in range(3)}
        args, in_specs = args + list(earlier[:3]), in_specs + [ANYWHERE] * 3
    out_specs = [spec((SPAN, s.wide), lambda g: (span, g)), at.maps, spec((SPAN, LANES), lambda g: (span, 0))]
    out_shape = [shape_of((s.rows, s.inner)), shape_of((s.rows, 2 * s.state)), shape_of((s.rows, LANES))]
    if span == 0:
        out_specs, out_shape = out_specs + [whole((8, s.mixed))], out_shape + [shape_of((8, s.mixed))]
    return pl.pallas_call(
        functools.partial(scan_back_kernel, s.head, s.heads, s.state, span == 0),
        grid=(s.groups,),
        in_specs=in_specs,
        out_specs=out_specs,
        out_shape=out_shape,
        scratch_shapes=[
            pltpu.VMEM((SPAN, SPAN), F32), pltpu.VMEM((SPAN, SPAN), F32), pltpu.VMEM((s.heads, SPAN), F32),
            pltpu.VMEM((s.heads, SPAN), F32), pltpu.VMEM((SPAN, s.state), F32), pltpu.VMEM((SPAN, s.state), F32),
        ],
        input_output_aliases=aliases,
        compiler_params=PARAMS,
        cost_estimate=cost(
            2 * SPAN * s.inner * (SPAN * 12 + 4 * s.state), 10 * SPAN * s.inner, s.heads * SPAN * SPAN
        ),
    )(*args)


def conv_backward(sizes, grad_values, grad_maps, conv, later, level, tokens):
    s = sizes
    wide = 2 * s.state
    blocks = s.inner // wide
    values = spec((s.rows, wide), lambda i: (0, jnp.minimum(i, blocks - 1)))
    maps = whole((s.rows, wide))
    fixed = [level.vector, tokens.valid, tokens.next_valid]
    return pl.pallas_call(
        functools.partial(conv_back_kernel, blocks, s.places),
        grid=(blocks + 1,),
        in_specs=[values, maps, values, maps, spec((8, wide), lambda i: (0, i)), *whole_specs(*fixed)],
        out_specs=spec((s.rows, wide), lambda i: (0, i)),
        out_shape=shape_of((s.rows, s.mixed)),
        compiler_params=PARAMS,
        cost_estimate=cost(10 * s.rows * s.mixed, 6 * s.rows * s.mixed, 0),
    )(grad_values, grad_maps, conv.slope, conv.slope_maps, later, *fixed)


GRAD_ROWS = 512


def early_grads_kernel(
    up_blocks, out_blocks, up_ref, narrow_out_ref, normed_out_ref, grad_narrow_ref, grad_gate_ref, narrow_ref, *rest
):
    out_ref = rest[-1]
    block = pl.program_id(0)

    @pl.when(block < up_blocks)
    def _():
        out_ref[...] = dot_first(up_ref[...], narrow_out_ref[...]).astype(BF16)

    @pl.when((block >= up_blocks) & (block < up_blocks + out_blocks))
    def _():
        out_ref[...] = dot_first(normed_out_ref[...], grad_narrow_ref[...]).astype(BF16)

    @pl.when(block >= up_blocks + out_blocks)
    def _():
        out_ref[...] = dot_first(grad_gate_ref[...], narrow_ref[...]).astype(BF16)


def grad_blocks(sizes, width):
    late = -(-(width + sizes.mixed + LANES) // GRAD_ROWS)
    return (width + 2 * sizes.inner) // GRAD_ROWS, late


def early_grads(sizes, upstream, kept, grad_narrow_out, grad_gate, rows, first, buffer):
    s = sizes
    wide = GRAD_ROWS
    up_blocks, out_blocks = upstream.shape[1] // wide, s.inner // wide
    args = [upstream, kept.narrow_out, kept.normed_out, grad_narrow_out, grad_gate, kept.narrow]
    narrow = whole((s.rows, LANES))
    at = lambda start, count: spec((s.rows, wide), lambda i: (0, jnp.clip(i - start, 0, count - 1)))
    in_specs = [
        at(0, up_blocks), narrow, at(up_blocks, out_blocks), narrow, at(up_blocks + out_blocks, out_blocks), narrow
    ]
    aliases = {}
    if buffer is not None:
        aliases = {len(args): 0}
        args, in_specs = args + [buffer], in_specs + [ANYWHERE]
    blocks = up_blocks + 2 * out_blocks
    return pl.pallas_call(
        functools.partial(early_grads_kernel, up_blocks, out_blocks),
        grid=(blocks,),
        in_specs=in_specs,
        out_specs=spec((wide, LANES), lambda i: (first + i, 0)),
        out_shape=shape_of((rows, LANES)),
        input_output_aliases=aliases,
        compiler_params=PARAMS,
        cost_estimate=cost(2 * s.rows * LANES * blocks * wide, 2 * s.rows * blocks * wide, 0),
    )(*args)


def late_grads_kernel(normed_ref, grad_narrow_ref, mixed_ref, raw_ref, narrow_ref, *rest):
    out_ref = rest[-1]
    first = 0
    for left, right in ((normed_ref, grad_narrow_ref), (mixed_ref, narrow_ref), (raw_ref, narrow_ref)):
        rows = left.shape[1]
        out_ref[first : first + rows, :] = dot_first(left[...], right[...]).astype(BF16)
        first += rows
    out_ref[first:, :] = jnp.zeros((out_ref.shape[0] - first, out_ref.shape[1]), BF16)


def late_grads(sizes, kept, grad_narrow, grad_mixed, raw, buffer):
    s = sizes
    args = [kept.normed, grad_narrow, grad_mixed, raw, kept.narrow]
    in_specs = whole_specs(*args)
    rows = grad_blocks(s, kept.normed.shape[1])[1] * GRAD_ROWS
    all_rows, aliases = rows, {}
    if buffer is not None:
        all_rows, aliases = buffer.shape[0], {len(args): 0}
        args, in_specs = args + [buffer], in_specs + [ANYWHERE]
    return pl.pallas_call(
        late_grads_kernel,
        grid=(1,),
        in_specs=in_specs,
        out_specs=whole((rows, LANES)),
        out_shape=shape_of((all_rows, LANES)),
        input_output_aliases=aliases,
        compiler_params=PARAMS,
        cost_estimate=cost(2 * s.rows * LANES * rows, 2 * s.rows * rows, 0),
    )(*args)


def token_tables(doc_ids, block_rows):
    rows = doc_ids.shape[0]
    before = from_behind(doc_ids[rows - 8 :], SEQ, 1)
    after = from_behind(doc_ids[:8], SEQ, -1)
    extended = jnp.concatenate([before, doc_ids, after])

    def taps_behind(first, count):
        here = extended[first : first + count]
        return sum((extended[first - back : first - back + count] == here).astype(jnp.int32) for back in (1, 2, 3))

    spans = rows // SPAN
    ends = extended[7 + SPAN :: SPAN][:spans]
    starts = extended[7::SPAN][:spans]
    by_span = doc_ids.reshape(spans, SPAN)
    flags = jnp.stack(
        [
            (by_span == starts[:, None]).astype(F32),
            (by_span == ends[:, None]).astype(F32),
            jnp.broadcast_to((starts == ends).astype(F32)[:, None], (spans, SPAN)),
        ]
        + [jnp.zeros((spans, SPAN), F32)] * 5,
        axis=1,
    )
    return Bag(
        valid=jnp.broadcast_to(taps_behind(8, rows)[:, None], (rows, LANES)),
        next_valid=jnp.broadcast_to(taps_behind(8 + rows, 8)[:, None], (8, LANES)),
        column=jnp.broadcast_to(doc_ids[:, None], (rows, LANES)),
        row=jnp.broadcast_to(doc_ids[None, :], (8, rows)),
        flags=flags,
        keep=(starts == ends).astype(F32),
    )


def state_hops(rows, block_rows):
    eighth = block_rows // DOCS_PER_BLOCK
    if rows // SPAN > 1 and eighth > SPAN:
        raise ValueError("unsupported block")
    return 1 if rows >= eighth else 2 * eighth // rows - 1


def pass_states(sizes, local, conv, tokens, hops, direction):
    if hops > 1:
        keep = jnp.exp(conv.decay[:, -1]) * tokens.keep[0]
        keep = jnp.repeat(keep, sizes.head)[:, None]
        total = local.astype(F32)
        reach = 1
        while reach < hops:
            total = total + keep * from_behind(total.astype(BF16), SEQ, direction * reach).astype(F32)
            keep = keep * from_behind(keep, SEQ, direction * reach)
            reach *= 2
        local = total.astype(BF16)
    return from_behind(local, SEQ, direction)


def layer_forward(sizes, inputs, level, lane_mask, tokens, hops):
    s = sizes
    normed, narrow, mixed, raw, rim = project_mixed(s, inputs, level, lane_mask)
    rim = from_behind(rim, SEQ, 1)
    outputs, states = conv_forward(s, mixed, raw, rim, level, tokens)
    values, slope, maps, slope_maps, step, decay, sig = outputs
    conv = Bag(values=values, slope=slope, maps=maps, slope_maps=slope_maps, step=step, decay=decay, sig=sig)
    states_in = [pass_states(s, states[-1], conv, tokens, hops, 1)] + list(states[:-1])
    gate = project_gate(s, normed, narrow, level)
    outputs = None
    for span in reversed(range(s.spans)):
        outputs = scan_forward(s, span, conv, states_in[span], gate, level, tokens, outputs)
    mixed_out, normed_out = outputs
    narrow_out, result = project_out(s, normed_out, inputs, level, lane_mask)
    kept = Bag(
        inputs=inputs, normed=normed, narrow=narrow, gate=gate, conv=conv, states_in=states_in, mixed_out=mixed_out,
        normed_out=normed_out, narrow_out=narrow_out,
    )
    return result, kept


def layer_backward(sizes, upstream, kept, level, lane_mask, tokens, hops, buffer, rows, first, last):
    s = sizes
    conv = kept.conv
    grad_gate, turned, grad_narrow_out, *local = out_backward(
        s, upstream, kept.mixed_out, kept.gate, conv, level, lane_mask, tokens
    )
    grad_states = list(local[1:]) + [pass_states(s, local[0], conv, tokens, hops, -1)]
    buffer = early_grads(s, upstream, kept, grad_narrow_out, grad_gate, rows, first, buffer)
    part = gate_in_backward(s, grad_gate, level)
    outputs = None
    for span in range(s.spans):
        outputs = scan_backward(
            s, span, conv, turned, kept.states_in[span], grad_states[span], level, tokens, outputs
        )
        if span == 0:
            later = from_behind(outputs[3], SEQ, -1)
    grad_values, grad_maps, raw = outputs[:3]
    grad_mixed = conv_backward(s, grad_values, grad_maps, conv, later, level, tokens)
    grad_inputs, grad_narrow = mixed_in_backward(s, grad_mixed, raw, part, kept.inputs, upstream, level, lane_mask)
    late = late_grads(s, kept, grad_narrow, grad_mixed, raw, None if last else buffer)
    return grad_inputs, buffer, late


def make_level(sizes, vector, numbers, adapters, section, place):
    s = sizes
    in_down, in_up, out_down, out_up = adapters
    dt_bias, a_log, skip_gain = numbers
    table = jnp.stack([jnp.exp(a_log), skip_gain, dt_bias], axis=1)
    where = jnp.stack([place, place ^ (1 + section), place ^ (2 - section), place ^ 3, section]).astype(jnp.int32)
    return Bag(
        vector=vector, heads=jnp.pad(table, ((0, 0), (0, LANES - 3))), in_down=in_down, in_up=in_up, out_down=out_down,
        out_up=out_up, where=where,
    )


def swap(value):
    return lax.ppermute(value, SECTION, [(0, 1), (1, 0)])


def exchange(value, axis, distance):
    count = lax.axis_size(axis)
    return lax.ppermute(value, axis, [(place, place ^ distance) for place in range(count)])


def rows_at(value, index, rows):
    return lax.dynamic_slice_in_dim(value, index * rows, rows, axis=0)


def put_at(buffer, value, *index):
    start = list(index) + [0] * (buffer.ndim - len(index))
    return lax.dynamic_update_slice(buffer, value.reshape((1,) * len(index) + value.shape), start)


def across(value, second):
    count = lax.axis_size(WSHARD)
    pairs = []
    for section in range(2):
        distance = 2 - section if second else 1 + section
        pairs += [(section * count + place, section * count + (place ^ distance)) for place in range(count)]
    return lax.ppermute(value, (SECTION, WSHARD), pairs)


def spread(quarters):
    section = lax.axis_index(SECTION)
    layers, before, others = [], None, []
    for layer in range(2):
        parts = []
        for index, (matrix, half, step) in enumerate(quarters):
            if layer == 0:
                others.append(swap(matrix if before is None else tie(matrix, before.own)))
            own = jnp.where(section == layer, matrix, others[index])
            ready = own
            if before is not None:
                ready = tie(own, before.apart if before.first else before.near)
            near = across(ready, False)
            pass_on = near if before is None else tie(near, before.apart)
            apart = across(lax.dynamic_slice_in_dim(pass_on, section * step, half, axis=0), True)
            parts.append((own, near, swap(pass_on), apart, swap(apart)))
            before = Bag(own=own, near=near, apart=apart, first=before is None)
        layers.append(parts)
    return layers


def reduce_rows(value, axis):
    count, place = lax.axis_size(axis), lax.axis_index(axis)
    rows = value.shape[0] // count
    total = rows_at(value, place, rows).astype(F32)
    for distance in range(1, count):
        total = total + exchange(rows_at(value, place ^ distance, rows), axis, distance).astype(F32)
    return total


def collect_rows(value, axis):
    count, place = lax.axis_size(axis), lax.axis_index(axis)
    buffer = jnp.zeros((count,) + value.shape, value.dtype)
    for distance in range(count):
        part = exchange(value, axis, distance) if distance else value
        buffer = put_at(buffer, part, place ^ distance)
    return buffer.reshape((count * value.shape[0],) + value.shape[1:])


def sum_everywhere(packed):
    section = lax.axis_index(SECTION)
    half = packed.shape[0] // 2
    mine = rows_at(packed, section, half).astype(F32) + swap(rows_at(packed, 1 - section, half)).astype(F32)
    mine = mine.astype(BF16)
    if lax.axis_size(SEQ) == 4:
        part = reduce_rows(mine, WSHARD).astype(BF16)
        part = reduce_rows(part, SEQ).astype(BF16)
        mine = collect_rows(collect_rows(part, SEQ), WSHARD)
    else:
        mine = lax.psum(mine, (SEQ, WSHARD))
    other = swap(mine)
    return jnp.concatenate([jnp.where(section == 0, mine, other), jnp.where(section == 0, other, mine)], axis=0)


def both_layers(own):
    section = lax.axis_index(SECTION)
    other = swap(own)
    return [jnp.where(section == layer, own, other) for layer in range(2)]


def on_device(
    layer_input, out_grad, doc_index, doc_adapter, in_weight, out_weight, norm_gain, conv_weight, conv_bias, dt_bias,
    a_log, skip_gain, gate_gain, *adapters,
):
    section, place = lax.axis_index(SECTION), lax.axis_index(WSHARD)
    batches, rows, width = layer_input.shape
    heads, inner = dt_bias.shape[1], gate_gain.shape[1]
    taps, mixed = conv_weight.shape[1:]
    sizes = Sizes(rows, inner, heads, (mixed - inner) // 2, in_weight.shape[1], taps)
    block_rows = rows * lax.axis_size(SEQ)
    hops = state_hops(rows, block_rows)

    pick = lambda array: lax.dynamic_index_in_dim(array, section, 0, keepdims=False)
    inputs, grads, doc_ids, table = pick(layer_input), pick(out_grad), pick(doc_index), pick(doc_adapter)[0]
    turned = in_weight[0].T
    main = mixed // 2
    groups = spread(
        [
            (turned[inner:], main + heads, main),
            (turned[:inner], inner // 2, inner // 2),
            (out_weight[0], out_weight.shape[1] // 2, out_weight.shape[1] // 2),
        ]
    )
    tokens = token_tables(doc_ids, block_rows)
    adapter = jnp.sum(jnp.where(doc_ids[:, None] == jnp.arange(table.shape[0])[None, :], table[None, :], 0), axis=1)
    lane_mask = (adapter[:, None] == (jnp.arange(LANES) // RANK)[None, :]).astype(F32)
    vectors = both_layers(jnp.concatenate([conv_weight[0].reshape(1, -1), conv_bias, gate_gain, norm_gain], axis=1))
    numbers = both_layers(jnp.concatenate([dt_bias, a_log, skip_gain], axis=0))
    in_down, in_up, out_down, out_up = adapters
    both = [both_layers(array) for array in (in_down[0], in_up[0].T, out_down[0], out_up[0])]
    levels = [
        make_level(sizes, vectors[layer], numbers[layer], [pair[layer] for pair in both], section, place)
        for layer in range(2)
    ]
    small = [inputs, grads, lane_mask, tokens.__dict__] + [level.__dict__ for level in levels]
    first_parts = groups[0][0]
    (inputs, grads, lane_mask, token_fields, *level_fields), first_parts = lax.optimization_barrier((small, first_parts))
    tokens, levels = Bag(**token_fields), [Bag(**fields) for fields in level_fields]
    groups[0][0] = first_parts
    for layer in range(2):
        levels[layer].mixed, levels[layer].gate, levels[layer].out = groups[layer]

    results, kept = [], []
    rows_now = inputs
    for layer in range(2):
        rows_now, stored = layer_forward(sizes, rows_now, levels[layer], lane_mask, tokens, hops)
        results.append(rows_now)
        kept.append(stored)
    early_blocks, late_blocks = grad_blocks(sizes, width)
    early_rows, late_rows = early_blocks * GRAD_ROWS, late_blocks * GRAD_ROWS
    all_rows = late_rows + 2 * early_rows
    upper_grad, _, buffer = layer_backward(
        sizes, grads, kept[1], levels[1], lane_mask, tokens, hops, None, all_rows, late_blocks, False
    )
    lower_grad, buffer, lower_late = layer_backward(
        sizes, upper_grad, kept[0], levels[0], lane_mask, tokens, hops, buffer, all_rows, late_blocks + early_blocks, True
    )
    first = sum_everywhere(buffer)
    upper_early, lower_early = first[late_rows : late_rows + early_rows], first[late_rows + early_rows :]
    early = jnp.where(section == 0, lower_early, upper_early).astype(F32)
    late = jnp.where(section == 0, sum_everywhere(lower_late), first[:late_rows]).astype(F32)
    up_out, down_out, up_gate = early[:width], early[width : width + inner], early[width + inner :]
    down_in, up_mixed = late[:width], late[width : width + mixed + heads]

    def placed(pair):
        here = jnp.where(section == 0, pair[0], pair[1])
        there = swap(jnp.where(section == 0, pair[1], pair[0]))
        first, second = jnp.where(section == 0, here, there), jnp.where(section == 0, there, here)
        return jnp.stack([first, second])[None]

    return (
        placed(results),
        placed([lower_grad, upper_grad]),
        down_in[None],
        jnp.concatenate([up_gate, up_mixed], axis=0).T[None],
        down_out[None],
        up_out.T[None],
    )


def solution(mesh):
    tokens, matrix, vector = P(None, (WSHARD, SEQ), None), P(SECTION, None, None), P(SECTION, None)
    in_specs = (tokens, tokens, P(None, (WSHARD, SEQ)), P(None, WSHARD, None))
    in_specs += (P(SECTION, WSHARD, None),) * 2
    in_specs += (vector, matrix) + (vector,) * 5 + (matrix,) * 4
    out_specs = (P(SECTION, None, (WSHARD, SEQ), None),) * 2 + (matrix,) * 4
    return jax.shard_map(on_device, mesh=mesh, in_specs=in_specs, out_specs=out_specs, check_vma=False)
```

```python
import functools

import jax
import jax.numpy as jnp
from jax import lax
from jax.experimental import pallas as pl
from jax.experimental.pallas import tpu as pltpu
from jax.sharding import PartitionSpec as P

SPAN = 256
RANK = 16
LANES = 128
DOCS_PER_BLOCK = 8
EPSILON = 1e-05
LOG2E = 1.4426950408889634
EXACT = lax.Precision.HIGHEST
SEQ, WSHARD, SECTION = "seq", "wshard", "section"
BF16 = jnp.bfloat16
F32 = jnp.float32
PARAMS = pltpu.CompilerParams(vmem_limit_bytes=20 * 1024 * 1024)


class Bag:
    def __init__(self, **fields):
        self.__dict__.update(fields)


def tie(value, *others):
    return lax.optimization_barrier((value, *others))[0]


def from_behind(value, axis, steps):
    count = lax.axis_size(axis)
    initial, last = (max(0, -steps), min(count, count - steps))
    return lax.ppermute(value, axis, [(source, source + steps) for source in range(initial, last)])


def dot(left, right):
    return jnp.dot(left, right, preferred_element_type=F32)


def dot_last(left, right):
    return lax.dot_general(left, right, (((1,), (1,)), ((), ())), preferred_element_type=F32)


def dot_first(left, right):
    return lax.dot_general(left, right, (((0,), (0,)), ((), ())), preferred_element_type=F32)


def rms_rate(values):
    return lax.rsqrt(jnp.mean(values * values, axis=-1, keepdims=True) + EPSILON)


def sigmoid(v):
    return 0.5 + 0.5 * jnp.tanh(0.5 * v)


def lower_ones(shape):
    rows = lax.broadcasted_iota(jnp.int32, shape, 0)
    columns = lax.broadcasted_iota(jnp.int32, shape, 1)
    return rows <= columns


def conv_rows(rows, rim, weight, offset, valid):
    length = rows.shape[0]
    valid = jnp.concatenate([valid] * (rows.shape[1] // LANES), axis=1)
    extended = jnp.concatenate([rim, rows], axis=0)
    taps = weight.shape[0]
    total = offset + weight[taps - 1 : taps] * rows
    for back in range(1, taps):
        shifted = extended[8 - back : 8 - back + length]
        total = total + jnp.where(valid >= back, shifted, 0.0) * weight[taps - 1 - back : taps - back]
    gate = sigmoid(total)
    active = total * gate
    return active, gate + active * (1.0 - gate)


def taps_at(vector_ref, places, first, width):
    rows = [vector_ref[:, pl.ds(pl.multiple_of(place + first, LANES), width)] for place in places]
    return jnp.concatenate(rows[:-1], axis=0), rows[-1]


def conv_kernel(
    spans, head, heads, state, places,
    mixed_ref, mixed_bc_ref, rim_ref, rim_bc_ref, vector_ref, valid_ref, raw_ref, head_ref, token_ref,
    values_ref, slope_ref, bc_ref, step_ref, *rest,
):
    state_refs, tail_ref = rest[:-1], rest[-1]
    group = pl.program_id(0)
    valid = valid_ref[...]
    width = mixed_ref.shape[1]
    heads_here = width // head

    @pl.when(group == 0)
    def _():
        weight, offset = taps_at(vector_ref, places, pl.num_programs(0) * width, 2 * state)
        active, slope = conv_rows(
            mixed_bc_ref[...].astype(F32), rim_bc_ref[...].astype(F32), weight, offset, valid
        )
        bc_ref[...] = jnp.concatenate([active, slope], axis=1).astype(BF16)
        raw = raw_ref[...].astype(F32).T[:heads] + head_ref[:, 2:3]
        step = (jnp.maximum(raw, 0.0) + jnp.log1p(jnp.exp(-jnp.abs(raw)))).astype(BF16).astype(F32)
        step_ref[:heads, :] = step
        step_ref[2 * heads :, :] = sigmoid(raw)
        drop = step * head_ref[:, :1]
        ones = lower_ones((SPAN, SPAN)).astype(F32)
        for span in range(spans):
            here = slice(span * SPAN, (span + 1) * SPAN)
            decay = jnp.dot(drop[:, here], ones, precision=EXACT, preferred_element_type=F32)
            step_ref[heads : 2 * heads, here] = decay
            tail = jnp.exp2(decay[:, SPAN - 1 :] - decay) * token_ref[span][1:2]
            tail_ref[:, here] = tail * step[:, here]

    weight, offset = taps_at(vector_ref, places, group * width, width)
    active, slope = conv_rows(
        mixed_ref[...].astype(F32), rim_ref[...].astype(F32), weight, offset, valid
    )
    slope_ref[...] = slope.astype(BF16)
    low = active.T.astype(BF16)
    values_ref[...] = low
    low = low.astype(F32)
    first = pl.multiple_of(group * heads_here, heads_here)
    tail_rows = tail_ref[pl.ds(first, heads_here), :]
    for span in range(spans):
        here = slice(span * SPAN, (span + 1) * SPAN)
        driven = jnp.concatenate(
            [
                (low[place * head : (place + 1) * head, here] * tail_rows[place : place + 1, here]).astype(BF16)
                for place in range(heads_here)
            ],
            axis=0,
        )
        state_refs[span][...] = dot(driven, bc_ref[here, :state]).astype(BF16)


def faded(row, column, score_ref):
    half = SPAN // 2
    upper = jnp.exp2(jnp.minimum(row - column[:half], 0.0))
    lower = jnp.exp2(jnp.minimum(row[:, half:] - column[half:], 0.0))
    lower = jnp.concatenate([jnp.zeros_like(lower), lower], axis=1)
    return (upper, lower), (upper * score_ref[:half, :], lower * score_ref[half:, :])


def scan_kernel(
    head, state, gain,
    values_ref, bc_ref, step_ref, decay_ref, token_ref, doc_column_ref, doc_row_ref, state_ref, head_ref, gate_ref,
    vector_ref, *rest,
):
    mixed_ref, normed_ref, score_ref, scanned_ref = rest[-4:]
    group, groups = pl.program_id(0), pl.num_programs(0)
    width = values_ref.shape[0]
    heads_here = width // head

    @pl.when(group == 0)
    def _():
        score = dot_last(bc_ref[:, :state], bc_ref[:, state:])
        same = (jnp.concatenate([doc_column_ref[...]] * (SPAN // LANES), axis=1) == doc_row_ref[:1]) & lower_ones((SPAN, SPAN))
        score_ref[...] = jnp.where(same, score, 0.0)

    decay, step = decay_ref[...], step_ref[...]
    carry = jnp.exp2(decay) * token_ref[0][:1]
    columns = jnp.concatenate([decay] * (LANES // heads_here), axis=0).T
    out_map = bc_ref[:, state:]
    parts = []
    for place in range(heads_here):
        rows = slice(place * head, (place + 1) * head)
        one = slice(place, place + 1)
        kernel = jnp.concatenate([part.astype(BF16) for part in faded(decay[one], columns[:, one], score_ref)[1]], axis=0)
        values = values_ref[rows].astype(F32)
        driven = (values * step[one]).astype(BF16)
        before = dot_last(state_ref[rows], out_map) * carry[one]
        parts.append(dot(driven, kernel) + before + head_ref[one, 1:2] * values)
    turned = jnp.concatenate(parts, axis=0).T
    low = turned.astype(BF16)
    mixed_ref[...] = low
    scanned_ref[:, pl.ds(pl.multiple_of(group * width, width), width)] = low

    @pl.when(group == groups - 1)
    def _():
        def rows_at(index, _):
            rows = pl.ds(pl.multiple_of(index * 16, 16), 16)
            mixed = scanned_ref[rows, :]
            gate = gate_ref[rows, :].astype(F32)
            gated = mixed.astype(F32) * (gate * sigmoid(gate))
            normed_ref[rows, :] = (gated * rms_rate(gated) * vector_ref[:, gain : gain + gated.shape[1]]).astype(BF16)
            return 0

        lax.fori_loop(0, SPAN // 16, rows_at, 0)


def out_back_kernel(
    head, heads, state, gain, count,
    up_ref, lane_ref, up_out_ref, down_out_ref, mixed_ref, gate_ref, vector_ref, decay_ref, token_ref, bc_ref, where_ref,
    *rest,
):
    parts, rest = rest[:count], rest[count:]
    (project_ref, turned_ref, narrow_ref), state_refs, (grad_ref, grad_mixed_ref) = rest[:3], rest[3:-2], rest[-2:]
    width = mixed_ref.shape[1]
    up = up_ref[...]
    narrow = (dot_last(up, up_out_ref[...]) * lane_ref[...]).astype(BF16)
    narrow_ref[...] = narrow
    left = jnp.concatenate([up, narrow], axis=1)
    for offset, part in out_places(where_ref, parts):
        here = pl.ds(offset, part.shape[0])
        grad_ref[:, here] = dot_last(left, jnp.concatenate([part[...], down_out_ref[here, :]], axis=1))

    def rows_at(index, _):
        rows = pl.ds(pl.multiple_of(index * 16, 16), 16)
        mixed = mixed_ref[rows, :].astype(F32)
        gate = gate_ref[rows, :].astype(F32)
        share = sigmoid(gate)
        silu = gate * share
        gated = mixed * silu
        grad = grad_ref[rows, :] * vector_ref[:, gain : gain + width]
        rate = rms_rate(gated)
        pull = jnp.mean(gated * grad, axis=-1, keepdims=True) * rate * rate * rate
        grad_gated = rate * grad - gated * pull
        project_ref[rows, :] = (grad_gated * mixed * (share + silu * (1.0 - share))).astype(BF16)
        grad_mixed_ref[rows, :] = (grad_gated * silu).astype(BF16)
        return 0

    lax.fori_loop(0, SPAN // 16, rows_at, 0)
    carry = jnp.exp2(decay_ref[...]) * token_ref[0][:1]
    out_map = bc_ref[:, state:]
    wide = 512
    for first in range(0, width, wide):
        low = grad_mixed_ref[:, first : first + wide].astype(F32).T
        turned_ref[first : first + wide, :] = low.astype(BF16)
        scaled = [
            (low[place * head : (place + 1) * head] * carry[first // head + place : first // head + place + 1]).astype(BF16)
            for place in range(wide // head)
        ]
        local = dot(jnp.concatenate(scaled, axis=0), out_map).astype(BF16)
        for span, state_ref in enumerate(state_refs):

            @pl.when(pl.program_id(0) == span)
            def _(state_ref=state_ref, first=first, local=local):
                state_ref[first : first + wide, :] = local


def aligned(value, unit):
    return pl.multiple_of(value * unit, unit)


def out_places(where_ref, parts):
    if len(parts) == 1:
        half = parts[0].shape[1]
        return [((2 * place + side) * half, parts[0].at[4 * side + place]) for place in range(4) for side in range(2)]
    rows, half = parts[0].shape[0], parts[3].shape[0]
    places = [(aligned(where_ref[place], rows), part) for place, part in enumerate(parts[:3])]
    apart = where_ref[3] * 2
    places.append((aligned(apart + where_ref[4], half), parts[3]))
    places.append((aligned(apart + 1 - where_ref[4], half), parts[4]))
    return places


def in_rows(where_ref, parts, step, start, size):
    side = int(start >= step)
    there = slice(start - side * step, start - side * step + size)
    if len(parts) == 1:
        return [parts[0][4 * side + place, there, :] for place in range(4)]
    pair = (parts[3][there], parts[4][there])
    apart = jnp.where(where_ref[4] == 0, pair[side], pair[1 - side])
    return [part[start : start + size] for part in parts[:3]] + [apart]


def in_columns(ref, where_ref, parts):
    columns = (ref.shape[1] - LANES) // parts
    places = [pl.ds(aligned(where_ref[place], columns), columns) for place in range(parts)]
    return jnp.concatenate([ref[:, here] for here in places + [pl.ds(parts * columns, LANES)]], axis=1)


def mixed_kernel(
    main, lanes, gain, count, input_ref, vector_ref, down_ref, lane_ref, up_ref, where_ref, *rest
):
    parts, (normed_ref, mixed_ref, raw_ref, rim_ref) = rest[:count], rest[count:]
    rows = input_ref.shape[0]
    inputs = input_ref[...].astype(F32)
    normed = (inputs * rms_rate(inputs) * vector_ref[:, gain : gain + inputs.shape[1]]).astype(BF16)
    narrow = (dot(normed, down_ref[...]) * lane_ref[...]).astype(BF16)
    normed_ref[...] = jnp.concatenate([normed, narrow], axis=1)
    left = in_columns(normed_ref, where_ref, 4)
    step, extra = main // 6, raw_ref.shape[1] // 4
    before = up_ref.shape[0] - main - extra

    def product(start, size):
        right = in_rows(where_ref, parts, main // 2, start, size)
        right.append(up_ref[before + start : before + start + size])
        return dot_last(left, jnp.concatenate(right, axis=1))

    for start in range(0, main, step):
        low = product(start, step).astype(BF16)
        mixed_ref[:, start : start + step] = low
        rim_ref[:, start : start + step] = low[rows - 8 :]
    raw_ref[...] = jnp.concatenate([product(main, extra), jnp.zeros((rows, lanes - extra), F32)], axis=1).astype(BF16)


def gate_kernel(count, normed_ref, up_ref, where_ref, *rest):
    parts, gate_ref = rest[:count], rest[count]
    left = in_columns(normed_ref, where_ref, 4)
    wide = 512
    inner = gate_ref.shape[1]
    for start in range(0, inner, wide):
        right = in_rows(where_ref, parts, inner // 2, start, wide) + [up_ref[start : start + wide]]
        gate_ref[:, start : start + wide] = dot_last(left, jnp.concatenate(right, axis=1)).astype(BF16)


def out_kernel(count, normed_ref, input_ref, down_ref, lane_ref, up_ref, where_ref, *rest):
    parts, (narrow_ref, out_ref) = rest[:count], rest[count:]
    narrow = (dot(normed_ref[...], down_ref[...]) * lane_ref[...]).astype(BF16)
    narrow_ref[...] = narrow
    places = out_places(where_ref, parts)
    left = [normed_ref[:, pl.ds(offset, part.shape[0])] for offset, part in places]
    left = jnp.concatenate(left + [narrow], axis=1)
    wide = 256
    for start in range(0, out_ref.shape[1], wide):
        here = slice(start, start + wide)
        right = jnp.concatenate([part[:, here] for _, part in places] + [up_ref[:, here]], axis=0)
        out_ref[:, here] = (input_ref[:, here].astype(F32) + dot(left, right)).astype(BF16)


def gate_in_back_kernel(count, grad_ref, up_ref, where_ref, *rest):
    parts, out_ref = rest[:count], rest[count]
    grad = grad_ref[...]
    half = grad.shape[1] // 2
    lower, upper = [in_rows(where_ref, parts, half, side * half, half) for side in range(2)]
    columns = lower[0].shape[1]
    for place in range(4):
        product = dot(grad[:, :half], lower[place]) + dot(grad[:, half:], upper[place])
        out_ref[:, place * columns : (place + 1) * columns] = product
    out_ref[:, 4 * columns :] = dot(grad, up_ref[...])


def narrow_back_kernel(main, extra, grad_ref, raw_ref, part_ref, lane_ref, up_ref, narrow_ref):
    before = up_ref.shape[0] - main - extra
    total = part_ref[...] + dot(grad_ref[...], up_ref[before : before + main])
    total = total + dot(raw_ref[...][:, :extra], up_ref[before + main :])
    narrow_ref[...] = (total * lane_ref[...]).astype(BF16)


def mixed_in_back_kernel(
    main, extra, gain, count,
    grad_ref, raw_ref, part_ref, input_ref, up_stream_ref, vector_ref, narrow_ref, down_ref, where_ref, *rest
):
    parts, (out_ref, total_ref) = rest[:count], rest[count:]
    width = input_ref.shape[1]
    columns = width // 4
    half = main // 2
    left = jnp.concatenate([grad_ref[...], raw_ref[...][:, :extra]], axis=1)
    lower = in_rows(where_ref, parts, half, 0, half)
    upper = in_rows(where_ref, parts, half, half, half + extra)
    for place in range(4):
        product = dot(left[:, :half], lower[place]) + dot(left[:, half:], upper[place])
        here = slice(place * columns, (place + 1) * columns)
        total_ref[:, pl.ds(aligned(where_ref[place], columns), columns)] = part_ref[:, here] + product
    scaled = (total_ref[...] + dot_last(narrow_ref[...], down_ref[...])) * vector_ref[:, gain : gain + width]
    inputs = input_ref[...].astype(F32)
    rate = rms_rate(inputs)
    pull = jnp.mean(inputs * scaled, axis=-1, keepdims=True) * rate * rate * rate
    out_ref[...] = (up_stream_ref[...].astype(F32) + rate * scaled - inputs * pull).astype(BF16)


def scan_back_kernel(
    head, heads, state, edge,
    values_ref, grad_ref, bc_ref, step_ref, decay_ref, sig_ref, token_ref, doc_column_ref, doc_row_ref, state_ref,
    grad_state_ref, head_ref, rate_ref, slope_ref, slope_bc_ref, *rest,
):
    outputs = rest[:-6]
    if edge:
        outputs, edge_ref = outputs[:-1], outputs[-1]
    out_values_ref, out_bc_ref, out_raw_ref = outputs[-3:]
    score_ref, grad_score_ref, pull_ref, direct_ref, grad_in_ref, grad_out_ref = rest[-6:]
    group, groups = pl.program_id(0), pl.num_programs(0)
    width = values_ref.shape[0]
    heads_here = width // head
    in_map, out_map = bc_ref[:, :state], bc_ref[:, state:]

    def same_doc():
        return (jnp.concatenate([doc_column_ref[...]] * (SPAN // LANES), axis=1) == doc_row_ref[:1]) & lower_ones((SPAN, SPAN))

    @pl.when(group == 0)
    def _():
        score_ref[...] = jnp.where(same_doc(), dot_last(in_map, out_map), 0.0)
        grad_score_ref[...] = jnp.zeros_like(grad_score_ref)
        grad_in_ref[...] = jnp.zeros_like(grad_in_ref)
        grad_out_ref[...] = jnp.zeros_like(grad_out_ref)

    decay, step = decay_ref[...], step_ref[...]
    token = token_ref[0]
    last = decay[:, SPAN - 1 :]
    carry = jnp.exp2(decay) * token[:1]
    tail = jnp.exp2(last - decay) * token[1:2]
    keep = jnp.exp2(last) * token[2:3, :1]
    columns = jnp.concatenate([decay] * (LANES // heads_here), axis=0).T
    at_end = lax.broadcasted_iota(jnp.int32, (1, SPAN), 1) == SPAN - 1
    grads, tails, carried, pulls, directs = [], [], [], [], []
    for place in range(heads_here):
        rows = slice(place * head, (place + 1) * head)
        one = slice(place, place + 1)
        fade, kernel = faded(decay[one], columns[:, one], score_ref)
        kernel = jnp.concatenate([part.astype(BF16) for part in kernel], axis=0)
        values = values_ref[rows].astype(F32)
        driven = (values * step[one]).astype(BF16)
        grad_low = grad_ref[rows]
        grad = grad_low.astype(F32)
        grad_kernel = dot_first(driven, grad_low)
        half = SPAN // 2
        grad_score_ref[:half, :] += grad_kernel[:half] * fade[0]
        grad_score_ref[half:, half:] += grad_kernel[half:, half:] * fade[1][:, half:]
        state_here, grad_state = state_ref[rows], grad_state_ref[rows]
        output = dot(driven, kernel) + dot_last(state_here, out_map) * carry[one]
        by_state = dot_last(grad_state, in_map) * tail[one]
        grad_driven = dot_last(grad_low, kernel) + by_state
        driven = driven.astype(F32)
        pull = jnp.sum(grad * output - driven * grad_driven, axis=0, keepdims=True)
        ending = jnp.sum(jnp.sum(driven * by_state, axis=0, keepdims=True), axis=1, keepdims=True)
        kept = jnp.sum(state_here.astype(F32) * grad_state.astype(F32), axis=0, keepdims=True)
        ending = ending + keep[one] * jnp.sum(kept, axis=1, keepdims=True)
        pulls.append(pull + jnp.where(at_end, ending, 0.0))
        directs.append(jnp.sum(values * grad_driven, axis=0, keepdims=True))
        grads.append(step[one] * grad_driven + head_ref[one, 1:2] * grad)
        tails.append((driven * tail[one]).astype(BF16))
        carried.append((grad * carry[one]).astype(BF16))
    grad_in_ref[...] += dot_first(jnp.concatenate(tails, axis=0), grad_state_ref[...])
    grad_out_ref[...] += dot_first(jnp.concatenate(carried, axis=0), state_ref[...])
    grads = jnp.concatenate(grads, axis=0).T.astype(BF16)
    out_values_ref[...] = grads
    if edge:
        product = grads[:8].astype(F32) * slope_ref[...][:8].astype(F32)
        edge_ref[:, pl.ds(pl.multiple_of(group * width, width), width)] = product.astype(BF16)
    here = pl.ds(pl.multiple_of(group * heads_here, heads_here), heads_here)
    pull_ref[here, :] = jnp.concatenate(pulls, axis=0)
    direct_ref[here, :] = jnp.concatenate(directs, axis=0)

    @pl.when(group == groups - 1)
    def _():
        ones = lower_ones((SPAN, SPAN)).astype(F32)
        summed = lax.dot_general(
            pull_ref[...], ones, (((1,), (1,)), ((), ())), precision=EXACT, preferred_element_type=F32
        )
        grad_step = (direct_ref[...] + rate_ref[:, 3:4] * summed).astype(BF16).astype(F32)
        grad_raw = grad_step * sig_ref[...]
        padded = jnp.concatenate([grad_raw, jnp.zeros((LANES - heads, SPAN), F32)], axis=0)
        out_raw_ref[...] = padded.T.astype(BF16)
        grad_score = jnp.where(same_doc(), grad_score_ref[...], 0.0).astype(BF16)
        grad_in = grad_in_ref[...] + dot(grad_score, out_map)
        grad_out = grad_out_ref[...] + dot_first(grad_score, in_map)
        low = jnp.concatenate([grad_in, grad_out], axis=1).astype(BF16)
        out_bc_ref[...] = low
        if edge:
            product = low[:8].astype(F32) * slope_bc_ref[...][:8].astype(F32)
            edge_ref[:, groups * width :] = product.astype(BF16)


def conv_back_kernel(
    value_blocks, places,
    grad_ref, grad_bc_ref, slope_ref, slope_bc_ref, next_ref, vector_ref, valid_ref, next_valid_ref, project_ref,
):
    block = pl.program_id(0)
    length = grad_ref.shape[0]

    def back(grad_low, slope_low):
        grad = grad_low.astype(F32) * slope_low.astype(F32)
        later = next_ref[...].astype(F32)
        weight, _ = taps_at(vector_ref, places, block * grad.shape[1], grad.shape[1])
        valid, next_valid = [jnp.concatenate([ref[...]] * (grad.shape[1] // LANES), axis=1) for ref in (valid_ref, next_valid_ref)]
        taps = weight.shape[0]
        total = weight[taps - 1 : taps] * grad
        for ahead in range(1, taps):
            extended = jnp.concatenate(
                [jnp.where(valid >= ahead, grad, 0.0), jnp.where(next_valid >= ahead, later, 0.0)], axis=0
            )
            total = total + weight[taps - 1 - ahead : taps - ahead] * extended[ahead : ahead + length]
        project_ref[...] = total.astype(BF16)

    @pl.when(block < value_blocks)
    def _():
        back(grad_ref[...], slope_ref[...])

    @pl.when(block == value_blocks)
    def _():
        back(grad_bc_ref[...], slope_bc_ref[...])


def spec(shape, index):
    return pl.BlockSpec(shape, index)


def whole(shape):
    return pl.BlockSpec(shape, lambda *_: (0,) * len(shape))


def cost(microseconds):
    return pl.CostEstimate(flops=int(microseconds * 1.15e9), bytes_accessed=1 << 16, transcendentals=0)


class Sizes:
    def __init__(self, rows, inner, heads, state, columns, taps):
        self.rows, self.inner, self.heads, self.state, self.columns, self.taps = rows, inner, heads, state, columns, taps
        self.head = inner // heads
        self.spans = rows // SPAN
        self.mixed = inner + 2 * state
        self.group_heads = 8
        self.groups = heads // self.group_heads
        self.wide = self.group_heads * self.head
        self.places = tuple(tap * self.mixed for tap in range(taps + 1))
        self.gate_gain = (taps + 1) * self.mixed
        self.norm_gain = self.gate_gain + inner


def conv_forward(sizes, mixed, raw, rim, level, tokens):
    s = sizes
    rows, wide, heads, state = s.rows, s.wide, s.heads, s.state
    maps = s.inner // (2 * state)
    shapes = [(s.inner, rows), (rows, s.inner), (rows, 4 * state)]
    args = [level.vector, tokens.valid, raw, level.heads, tokens.flags]
    outputs = pl.pallas_call(
        functools.partial(conv_kernel, s.spans, s.head, heads, state, s.places),
        grid=(s.groups,),
        in_specs=[
            spec((rows, wide), lambda g: (0, g)), spec((rows, 2 * state), lambda g: (0, maps)),
            spec((8, wide), lambda g: (0, g)), spec((8, 2 * state), lambda g: (0, maps)), *whole_specs(*args),
        ],
        out_specs=[
            spec((wide, rows), lambda g: (g, 0)), spec((rows, wide), lambda g: (0, g)), whole(shapes[2]),
            whole((3 * heads, rows)),
        ] + [spec((wide, state), lambda g: (g, 0))] * s.spans,
        out_shape=[shape_of(shapes[0]), far_shape(shapes[1]), shape_of(shapes[2]), shape_of((3 * heads, rows), F32)]
        + [shape_of((s.inner, state))] * s.spans,
        scratch_shapes=[pltpu.VMEM((heads, rows), F32)],
        compiler_params=PARAMS,
        cost_estimate=cost(8.5),
    )(mixed, mixed, rim, rim, *args)
    return outputs[:4], outputs[4:]


def span_specs(sizes, span):
    s = sizes
    return Bag(
        turned=spec((s.wide, SPAN), lambda g: (g, span)),
        maps=spec((SPAN, 2 * s.state), lambda g: (span, 0)),
        rows=spec((s.group_heads, SPAN), lambda g: (g, span)),
        decay=spec((s.group_heads, SPAN), lambda g: (s.groups + g, span)),
        flags=spec((1, 8, SPAN), lambda g: (span, 0, 0)),
        doc_column=spec((SPAN, LANES), lambda g: (span, 0)),
        doc_row=spec((8, SPAN), lambda g: (0, span)),
        state=spec((s.wide, s.state), lambda g: (g, 0)),
        head=spec((s.group_heads, LANES), lambda g: (g, 0)),
        full=spec((SPAN, s.inner), lambda g: (span, 0)),
    )


ANYWHERE = pl.BlockSpec(memory_space=pl.ANY)


def scan_forward(sizes, span, conv, state_in, gate, level, tokens, earlier):
    s = sizes
    at = span_specs(s, span)
    args = [
        conv.values, conv.maps, conv.step, conv.step, tokens.flags, tokens.column, tokens.row, state_in, level.heads,
        gate, level.vector,
    ]
    in_specs = [
        at.turned, at.maps, at.rows, at.decay, at.flags, at.doc_column, at.doc_row, at.state,
        at.head, at.full, whole(level.vector.shape),
    ]
    aliases = {}
    if earlier is not None:
        aliases = {len(args): 0, len(args) + 1: 1}
        args, in_specs = args + list(earlier), in_specs + [ANYWHERE] * 2
    shape = (s.rows, s.inner)
    return pl.pallas_call(
        functools.partial(scan_kernel, s.head, s.state, s.gate_gain),
        grid=(s.groups,),
        in_specs=in_specs,
        out_specs=[spec((SPAN, s.wide), lambda g: (span, g)), at.full],
        out_shape=[shape_of(shape), shape_of(shape)],
        scratch_shapes=[pltpu.VMEM((SPAN, SPAN), F32), pltpu.VMEM((SPAN, s.inner), BF16)],
        input_output_aliases=aliases,
        compiler_params=PARAMS,
        cost_estimate=cost(6.5),
    )(*args)


SMALL = pl.BlockSpec(memory_space=pltpu.SMEM)


def shape_of(shape, dtype=BF16):
    return jax.ShapeDtypeStruct(shape, dtype)


def far_shape(shape, dtype=BF16):
    return pltpu.HBM(shape, dtype)


def whole_specs(*arrays):
    return [whole(array.shape) for array in arrays]


def project_mixed(sizes, inputs, level, lane_mask):
    s = sizes
    args = [inputs, level.vector, level.in_down, lane_mask, level.in_up]
    width = inputs.shape[1]
    shapes = [(s.rows, width + LANES), (s.rows, s.mixed), (s.rows, LANES), (8, s.mixed)]
    return pl.pallas_call(
        functools.partial(mixed_kernel, s.mixed, LANES, s.norm_gain, len(level.mixed)),
        grid=(1,),
        in_specs=whole_specs(*args) + [SMALL] + whole_specs(*level.mixed),
        out_specs=[whole(shape) for shape in shapes],
        out_shape=[shape_of(shape) for shape in shapes],
        compiler_params=PARAMS,
        cost_estimate=cost(6),
    )(*args, level.mixed_where, *level.mixed)


def gate_specs(sizes, level):
    return [whole((sizes.inner, LANES)), SMALL] + whole_specs(*level.gate)


def project_gate(sizes, normed, level):
    s = sizes
    return pl.pallas_call(
        functools.partial(gate_kernel, len(level.gate)),
        grid=(1,),
        in_specs=whole_specs(normed) + gate_specs(s, level),
        out_specs=whole((s.rows, s.inner)),
        out_shape=shape_of((s.rows, s.inner)),
        compiler_params=PARAMS,
        cost_estimate=cost(3.6),
    )(normed, level.in_up, level.where, *level.gate)


def project_out(sizes, normed_out, inputs, level, lane_mask):
    s = sizes
    args = [normed_out, inputs, level.out_down, lane_mask, level.out_up]
    shapes = [(s.rows, LANES), inputs.shape]
    return pl.pallas_call(
        functools.partial(out_kernel, len(level.out)),
        grid=(1,),
        in_specs=whole_specs(*args) + [SMALL] + whole_specs(*level.out),
        out_specs=[whole(shape) for shape in shapes],
        out_shape=[shape_of(shape) for shape in shapes],
        compiler_params=PARAMS,
        cost_estimate=cost(4),
    )(*args, level.where, *level.out)


def out_backward(sizes, upstream, mixed, gate, conv, level, lane_mask, tokens):
    s = sizes
    full = spec((SPAN, s.inner), lambda k: (k, 0))
    width = upstream.shape[1]
    return pl.pallas_call(
        functools.partial(out_back_kernel, s.head, s.heads, s.state, s.gate_gain, len(level.out)),
        grid=(s.spans,),
        in_specs=[
            spec((SPAN, width), lambda k: (k, 0)), spec((SPAN, LANES), lambda k: (k, 0)),
            *whole_specs(level.out_up, level.out_down), full, full, whole(level.vector.shape),
            spec((s.heads, SPAN), lambda k: (1, k)), spec((1, 8, SPAN), lambda k: (k, 0, 0)),
            spec((SPAN, 2 * s.state), lambda k: (k, 0)), SMALL, *whole_specs(*level.out),
        ],
        out_specs=[
            full, spec((s.inner, SPAN), lambda k: (0, k)), spec((SPAN, LANES), lambda k: (k, 0)),
        ] + [whole((s.inner, s.state))] * s.spans,
        out_shape=[
            shape_of((s.rows, s.inner)), shape_of((s.inner, s.rows)), shape_of((s.rows, LANES)),
        ] + [shape_of((s.inner, s.state))] * s.spans,
        scratch_shapes=[pltpu.VMEM((SPAN, s.inner), F32), pltpu.VMEM((SPAN, s.inner), BF16)],
        compiler_params=PARAMS,
        cost_estimate=cost(13.5),
    )(
        upstream, lane_mask, level.out_up, level.out_down, mixed, gate, level.vector, conv.step, tokens.flags, conv.maps,
        level.where, *level.out,
    )


def gate_in_backward(sizes, grad_gate, level):
    s = sizes
    width = 4 * s.columns + LANES
    return pl.pallas_call(
        functools.partial(gate_in_back_kernel, len(level.gate)),
        grid=(1,),
        in_specs=whole_specs(grad_gate) + gate_specs(s, level),
        out_specs=whole((s.rows, width)),
        out_shape=shape_of((s.rows, width), F32),
        compiler_params=PARAMS,
        cost_estimate=cost(3.5),
    )(grad_gate, level.in_up, level.where, *level.gate)


def narrow_backward(sizes, grad_mixed, raw, part, level, lane_mask):
    s = sizes
    args = [grad_mixed, raw, part, lane_mask, level.in_up]
    in_specs = whole_specs(*args)
    in_specs[2] = spec((s.rows, LANES), lambda _: (0, part.shape[1] // LANES - 1))
    return pl.pallas_call(
        functools.partial(narrow_back_kernel, s.mixed, s.heads),
        grid=(1,),
        in_specs=in_specs,
        out_specs=whole((s.rows, LANES)),
        out_shape=shape_of((s.rows, LANES)),
        compiler_params=PARAMS,
        cost_estimate=cost(0.9),
    )(*args)


def mixed_in_backward(sizes, grad_mixed, raw, part, inputs, upstream, narrow, level):
    s = sizes
    width = inputs.shape[1]
    rows = lambda columns: spec((SPAN, columns), lambda k: (k, 0))
    return pl.pallas_call(
        functools.partial(mixed_in_back_kernel, s.mixed, s.heads, s.norm_gain, len(level.mixed)),
        grid=(s.spans,),
        in_specs=[
            rows(s.mixed), rows(LANES), rows(width + LANES), rows(width), rows(width), whole(level.vector.shape),
            rows(LANES), *whole_specs(level.in_down), SMALL, *whole_specs(*level.mixed),
        ],
        out_specs=rows(width),
        out_shape=shape_of((s.rows, width)),
        scratch_shapes=[pltpu.VMEM((SPAN, width), F32)],
        compiler_params=PARAMS,
        cost_estimate=cost(4.7),
    )(grad_mixed, raw, part, inputs, upstream, level.vector, narrow, level.in_down, level.mixed_where, *level.mixed)


def scan_backward(sizes, span, conv, grad_turned, state_in, grad_state, level, tokens, earlier):
    s = sizes
    at = span_specs(s, span)
    args = [
        conv.values, grad_turned, conv.maps, conv.step, conv.step, conv.step, tokens.flags, tokens.column, tokens.row,
        state_in, grad_state, level.heads, level.heads, conv.slope, conv.maps,
    ]
    in_specs = [
        at.turned, at.turned, at.maps, at.rows, at.decay, spec((s.heads, SPAN), lambda g: (2, span)), at.flags,
        at.doc_column, at.doc_row, at.state, at.state, at.head, whole((s.heads, LANES)),
        spec((16, s.wide), lambda g: (0, g)), spec((16, 2 * s.state), lambda g: (0, 1)),
    ]
    aliases = {}
    if earlier is not None:
        aliases = {len(args) + place: place for place in range(3)}
        args, in_specs = args + list(earlier[:3]), in_specs + [ANYWHERE] * 3
    out_specs = [spec((SPAN, s.wide), lambda g: (span, g)), at.maps, spec((SPAN, LANES), lambda g: (span, 0))]
    out_shape = [shape_of((s.rows, s.inner)), shape_of((s.rows, 2 * s.state)), shape_of((s.rows, LANES))]
    if span == 0:
        out_specs, out_shape = out_specs + [whole((8, s.mixed))], out_shape + [shape_of((8, s.mixed))]
    return pl.pallas_call(
        functools.partial(scan_back_kernel, s.head, s.heads, s.state, span == 0),
        grid=(s.groups,),
        in_specs=in_specs,
        out_specs=out_specs,
        out_shape=out_shape,
        scratch_shapes=[
            pltpu.VMEM((SPAN, SPAN), F32), pltpu.VMEM((SPAN, SPAN), F32), pltpu.VMEM((s.heads, SPAN), F32),
            pltpu.VMEM((s.heads, SPAN), F32), pltpu.VMEM((SPAN, s.state), F32), pltpu.VMEM((SPAN, s.state), F32),
        ],
        input_output_aliases=aliases,
        compiler_params=PARAMS,
        cost_estimate=cost(8.5),
    )(*args)


def conv_backward(sizes, grad_values, grad_maps, conv, later, level, tokens):
    s = sizes
    wide = 2 * s.state
    blocks = s.inner // wide
    values = spec((s.rows, wide), lambda i: (0, jnp.minimum(i, blocks - 1)))
    maps, slopes = whole((s.rows, wide)), spec((s.rows, wide), lambda i: (0, 1))
    fixed = [level.vector, tokens.valid, tokens.next_valid]
    return pl.pallas_call(
        functools.partial(conv_back_kernel, blocks, s.places),
        grid=(blocks + 1,),
        in_specs=[values, maps, values, slopes, spec((8, wide), lambda i: (0, i)), *whole_specs(*fixed)],
        out_specs=spec((s.rows, wide), lambda i: (0, i)),
        out_shape=shape_of((s.rows, s.mixed)),
        compiler_params=PARAMS,
        cost_estimate=cost(4.4),
    )(grad_values, grad_maps, conv.slope, conv.maps, later, *fixed)


def stacked_kernel(places, *refs):
    out_ref = refs[-1]
    first = 0
    for left, right in places:
        rows = refs[left].shape[1]
        out_ref[first : first + rows, :] = dot_first(refs[left][...], refs[right][...]).astype(BF16)
        first += rows
    if first < out_ref.shape[0]:
        out_ref[first:, :] = jnp.zeros((out_ref.shape[0] - first, out_ref.shape[1]), BF16)


def stacked(sizes, args, places, columns, rows, first, buffer, all_rows):
    s = sizes
    in_specs = [spec((s.rows, width), functools.partial(lambda at, _: (0, at), at)) for at, width in columns]
    aliases = {}
    if buffer is not None:
        aliases = {len(args): 0}
        args, in_specs = args + [buffer], in_specs + [ANYWHERE]
    return pl.pallas_call(
        functools.partial(stacked_kernel, places),
        grid=(1,),
        in_specs=in_specs,
        out_specs=pl.BlockSpec((pl.Element(rows), pl.Element(LANES)), lambda _: (first, 0)),
        out_shape=shape_of((all_rows, LANES)),
        input_output_aliases=aliases,
        compiler_params=PARAMS,
        cost_estimate=cost(1.6),
    )(*args)


def grad_rows(sizes, width):
    return width + 2 * sizes.inner, -(-(width + sizes.mixed + LANES) // 512) * 512


def early_grads(sizes, upstream, kept, grad_narrow_out, grad_gate, first, buffer, all_rows):
    s = sizes
    width = upstream.shape[1]
    args = [upstream, kept.narrow_out, kept.normed_out, grad_narrow_out, grad_gate, kept.normed]
    columns = [(0, width), (0, LANES), (0, s.inner), (0, LANES), (0, s.inner), (width // LANES, LANES)]
    return stacked(
        s, args, ((0, 1), (2, 3), (4, 5)), columns, grad_rows(s, width)[0], first, buffer, all_rows
    )


def late_grads(sizes, kept, grad_narrow, grad_mixed, raw, first, buffer, all_rows):
    s = sizes
    width = kept.inputs.shape[1]
    args = [kept.normed, grad_narrow, grad_mixed, raw, kept.normed]
    columns = [(0, width), (0, LANES), (0, s.mixed), (0, LANES), (width // LANES, LANES)]
    return stacked(s, args, ((0, 1), (2, 4), (3, 4)), columns, grad_rows(s, width)[1], first, buffer, all_rows)


def final_kernel(width, inner, where_ref, *refs):
    upper, upper_other, lower, lower_other, down_in_ref, in_up_ref, down_out_ref, out_up_ref = refs
    first = where_ref[0] == 0
    half = upper.shape[0]

    def rows(start, stop):
        pieces = []
        for side, (mine, yours) in enumerate(((lower, upper_other), (lower_other, upper))):
            low, high = max(start - side * half, 0), min(stop - side * half, half)
            if low < high:
                pieces.append(jnp.where(first, mine[low:high], yours[low:high]).astype(F32))
        return pieces

    def put(ref, at, start, stop):
        for piece in rows(start, stop):
            ref[at : at + piece.shape[0], :] = piece
            at += piece.shape[0]

    out_up_ref[...] = jnp.concatenate(rows(0, width), axis=0).T
    put(down_out_ref, 0, width, width + inner)
    put(in_up_ref, 0, width + inner, width + 2 * inner)
    late = width + 2 * inner
    put(down_in_ref, 0, late, late + width)
    put(in_up_ref, inner, late + width, late + width + in_up_ref.shape[0] - inner)


def final_sums(sizes, width, section, *sums):
    s = sizes
    shapes = [(width, LANES), (s.inner + s.mixed + s.heads, LANES), (s.inner, LANES), (LANES, width)]
    return pl.pallas_call(
        functools.partial(final_kernel, width, s.inner),
        grid=(1,),
        in_specs=[SMALL] + whole_specs(*sums),
        out_specs=[whole(shape) for shape in shapes],
        out_shape=[shape_of(shape, F32) for shape in shapes],
        compiler_params=PARAMS,
    )(section[None], *sums)


def token_kernel(spans, row_ref, before_ref, after_ref, table_ref, valid_ref, next_ref, column_ref, mask_ref, flags_ref):
    length = row_ref.shape[1]
    row = row_ref[...].astype(F32)
    ids = jnp.concatenate([before_ref[...].astype(F32), row, after_ref[...].astype(F32)], axis=1)
    behind = jnp.zeros((1, length + LANES), F32)
    for back in (1, 2, 3):
        same = ids[:, LANES - back : 2 * LANES - back + length] == ids[:, LANES : 2 * LANES + length]
        behind = behind + jnp.where(same, 1.0, 0.0)
    adapter = jnp.zeros_like(row)
    for document in range(table_ref.shape[0]):
        adapter = jnp.where(row == document, table_ref[document].astype(F32), adapter)
    rows = jnp.concatenate([behind[:, :length], row, adapter, jnp.zeros((5, length), F32)], axis=0).T
    wide = (length, LANES)
    valid_ref[...] = jnp.broadcast_to(rows[:, :1], wide).astype(jnp.int32)
    column_ref[...] = jnp.broadcast_to(rows[:, 1:2], wide).astype(jnp.int32)
    lanes = lax.broadcasted_iota(jnp.int32, wide, 1) // RANK
    mask_ref[...] = jnp.where(lanes == jnp.broadcast_to(rows[:, 2:3], wide).astype(jnp.int32), 1.0, 0.0)
    last = jnp.concatenate([behind[:, length:], jnp.zeros((7, LANES), F32)], axis=0).T
    next_ref[...] = jnp.broadcast_to(last[:8, :1], (8, LANES)).astype(jnp.int32)
    zeros = jnp.zeros((5, SPAN), F32)
    for span in range(spans):
        here = row[:, span * SPAN : (span + 1) * SPAN]
        start = ids[:, LANES + span * SPAN - 1 : LANES + span * SPAN]
        end = here[:, SPAN - 1 :]
        keep = jnp.broadcast_to(jnp.where(start == end, 1.0, 0.0), here.shape)
        flags_ref[span] = jnp.concatenate(
            [jnp.where(here == start, 1.0, 0.0), jnp.where(here == end, 1.0, 0.0), keep, zeros], axis=0
        )


def token_tables(doc_ids, table):
    rows = doc_ids.shape[1]
    before = from_behind(doc_ids[:, rows - LANES :], SEQ, 1)
    after = from_behind(doc_ids[:, :LANES], SEQ, -1)
    shapes = [((rows, LANES), jnp.int32), ((8, LANES), jnp.int32), ((rows, LANES), jnp.int32), ((rows, LANES), F32)]
    shapes.append(((rows // SPAN, 8, SPAN), F32))
    valid, next_valid, column, mask, flags = pl.pallas_call(
        functools.partial(token_kernel, rows // SPAN),
        grid=(1,),
        in_specs=whole_specs(doc_ids, before, after) + [SMALL],
        out_specs=[whole(shape) for shape, _ in shapes],
        out_shape=[jax.ShapeDtypeStruct(*one) for one in shapes],
        compiler_params=PARAMS,
    )(doc_ids, before, after, table)
    row = jnp.broadcast_to(doc_ids, (8, rows))
    return Bag(valid=valid, next_valid=next_valid, column=column, row=row, flags=flags), mask


def state_hops(rows, block_rows):
    eighth = block_rows // DOCS_PER_BLOCK
    if rows // SPAN > 1 and eighth > SPAN:
        raise ValueError("unsupported block")
    return 1 if rows >= eighth else 2 * eighth // rows - 1


def pass_states(sizes, local, conv, tokens, hops, direction):
    if hops > 1:
        keep = jnp.exp2(conv.step[sizes.heads : 2 * sizes.heads, -1]) * tokens.flags[0, 2, 0]
        keep = jnp.repeat(keep, sizes.head)[:, None]
        total = local.astype(F32)
        reach = 1
        while reach < hops:
            total = total + keep * from_behind(total.astype(BF16), SEQ, direction * reach).astype(F32)
            keep = keep * from_behind(keep, SEQ, direction * reach)
            reach *= 2
        local = total.astype(BF16)
    return from_behind(local, SEQ, direction)


def layer_forward(sizes, inputs, level, lane_mask, tokens, hops):
    s = sizes
    normed, mixed, raw, rim = project_mixed(s, inputs, level, lane_mask)
    rim = from_behind(rim, SEQ, 1)
    yield mixed
    gate = None
    if level.gate_first:
        gate = project_gate(s, normed, level)
        rim = tie(rim, gate)
    (values, slope, maps, step), states = conv_forward(s, mixed, raw, rim, level, tokens)
    conv = Bag(values=values, slope=slope, maps=maps, step=step)
    states_in = [pass_states(s, states[-1], conv, tokens, hops, 1)] + list(states[:-1])
    yield values
    if gate is None:
        gate = project_gate(s, normed, level)
    outputs = None
    for span in reversed(range(s.spans)):
        outputs = scan_forward(s, span, conv, states_in[span], gate, level, tokens, outputs)
        if span == s.spans - 1:
            yield outputs[0]
    mixed_out, normed_out = outputs
    narrow_out, result = project_out(s, normed_out, inputs, level, lane_mask)
    yield result
    kept = Bag(
        inputs=inputs, normed=normed, gate=gate, conv=conv, states_in=states_in, mixed_out=mixed_out,
        normed_out=normed_out, narrow_out=narrow_out,
    )
    return result, kept


def layer_backward(sizes, upstream, kept, level, lane_mask, tokens, hops):
    s = sizes
    conv = kept.conv
    early_rows, late_rows = grad_rows(s, upstream.shape[1])
    all_rows = early_rows + late_rows
    grad_gate, turned, grad_narrow_out, *local = out_backward(
        s, upstream, kept.mixed_out, kept.gate, conv, level, lane_mask, tokens
    )
    grad_states = list(local[1:]) + [pass_states(s, local[0], conv, tokens, hops, -1)]
    buffer = early_grads(s, upstream, kept, grad_narrow_out, grad_gate, 0, None, all_rows)
    outputs = None
    for span in range(s.spans):
        outputs = scan_backward(
            s, span, conv, turned, kept.states_in[span], grad_states[span], level, tokens, outputs
        )
        if span == 0:
            later = from_behind(outputs[3], SEQ, -1)
            turned = yield outputs[0], turned
    grad_values, grad_maps, raw = outputs[:3]
    grad_values = yield grad_values, grad_values
    grad_mixed = conv_backward(s, grad_values, grad_maps, conv, later, level, tokens)
    part = gate_in_backward(s, grad_gate, level)
    grad_mixed = yield grad_mixed, grad_mixed
    narrow = narrow_backward(s, grad_mixed, raw, part, level, lane_mask)
    buffer = late_grads(s, kept, narrow, grad_mixed, raw, early_rows, buffer, all_rows)
    grad_mixed = yield buffer, grad_mixed
    return mixed_in_backward(s, grad_mixed, raw, part, kept.inputs, upstream, narrow, level)


def make_level(sizes, vector, numbers, adapters, where):
    s = sizes
    in_down, in_up, out_down, out_up = adapters
    dt_bias, a_log, skip_gain = numbers
    rate = -jnp.exp(a_log)[:, None]
    lane = jnp.arange(LANES)[None, :]
    table = jnp.where(lane == 1, skip_gain[:, None], jnp.where(lane == 2, dt_bias[:, None], rate))
    table = jnp.where(lane == 0, rate * LOG2E, table)
    return Bag(
        vector=vector, heads=table, in_down=in_down, in_up=in_up, out_down=out_down,
        out_up=out_up, where=where, mixed_where=where,
    )


def swap(value):
    return lax.ppermute(value, SECTION, [(0, 1), (1, 0)])


def exchange(value, axis, distance):
    count = lax.axis_size(axis)
    return lax.ppermute(value, axis, [(place, place ^ distance) for place in range(count)])


def rows_at(value, index, rows):
    return lax.dynamic_slice_in_dim(value, index * rows, rows, axis=0)


def put_at(buffer, value, *index):
    start = list(index) + [0] * (buffer.ndim - len(index))
    return lax.dynamic_update_slice(buffer, value.reshape((1,) * len(index) + value.shape), start)


def across(value, second):
    count = lax.axis_size(WSHARD)
    pairs = []
    for section in range(2):
        distance = 2 - section if second else 1 + section
        pairs += [(section * count + place, section * count + (place ^ distance)) for place in range(count)]
    return lax.ppermute(value, (SECTION, WSHARD), pairs)


class Parts:
    def __init__(self, quarters):
        self.section = lax.axis_index(SECTION)
        self.quarters, self.near, self.parts = quarters, {}, {}
        other = swap(quarters[0][0])
        self.own = [jnp.where(self.section == 0, quarters[0][0], other)]
        others = [other] + [swap(tie(matrix, self.own[0])) for matrix, _, _ in quarters[1:]]
        for layer in range(2):
            for (matrix, _, _), other in list(zip(quarters, others, strict=True))[1 - layer :]:
                self.own.append(jnp.where(self.section == layer, matrix, other))

    def start(self, index, *after):
        self.near[index] = across(tie(self.own[index], *after), False)

    def forward(self, index, *after):
        _, half, step = self.quarters[index % len(self.quarters)]
        near = tie(self.near[index], *after)
        apart = across(lax.dynamic_slice_in_dim(near, self.section * step, half, axis=0), True)
        self.parts[index] = (self.own[index], near, swap(near), apart, swap(apart))


def scatter_start(value, axis):
    count, place = lax.axis_size(axis), lax.axis_index(axis)
    rows = value.shape[0] // count
    sent = [exchange(rows_at(value, place ^ away, rows), axis, away) for away in range(1, count)]
    return rows_at(value, place, rows), sent


def scatter_done(parts, *after):
    own, received = parts
    total = own.astype(F32)
    for part in tie(received, *after):
        total = total + part.astype(F32)
    return total.astype(BF16)


def gather_start(value, axis):
    return value, [exchange(value, axis, away) for away in range(1, lax.axis_size(axis))]


def gather_done(parts, axis, *after):
    own, received = parts
    count, place = lax.axis_size(axis), lax.axis_index(axis)
    buffer = jnp.zeros((count,) + own.shape, own.dtype)
    for away, part in enumerate([own] + tie(received, *after)):
        buffer = put_at(buffer, part, place ^ away)
    return buffer.reshape((count * own.shape[0],) + own.shape[1:])


def chip_start(packed):
    section = lax.axis_index(SECTION)
    half = packed.shape[0] // 2
    return rows_at(packed, section, half), [swap(rows_at(packed, 1 - section, half))]


def both_layers(own):
    section = lax.axis_index(SECTION)
    other = swap(own)
    return [jnp.where(section == layer, own, other) for layer in range(2)]


def on_device(
    layer_input, out_grad, doc_index, doc_adapter, in_weight, out_weight, norm_gain, conv_weight, conv_bias, dt_bias,
    a_log, skip_gain, gate_gain, *adapters,
):
    section, place = lax.axis_index(SECTION), lax.axis_index(WSHARD)
    batches, rows, width = layer_input.shape
    heads, inner = dt_bias.shape[1], gate_gain.shape[1]
    taps, mixed = conv_weight.shape[1:]
    sizes = Sizes(rows, inner, heads, (mixed - inner) // 2, in_weight.shape[1], taps)
    block_rows = rows * lax.axis_size(SEQ)
    hops = state_hops(rows, block_rows)

    pick = lambda array: lax.dynamic_index_in_dim(array, section, 0, keepdims=False)
    turned = in_weight[0].T
    main = mixed // 2
    weights = Parts(
        [
            (turned[inner:], main + heads, main),
            (turned[:inner], inner // 2, inner // 2),
            (out_weight[0], out_weight.shape[1] // 2, out_weight.shape[1] // 2),
        ]
    )
    weights.start(0)
    weights.forward(0)
    weights.start(1, weights.parts[0][3])
    rest = (layer_input, out_grad, doc_index, doc_adapter, norm_gain, conv_weight, conv_bias, dt_bias, a_log, skip_gain)
    rest, gate_gain, adapters = tie((rest, gate_gain, adapters), weights.own[0])
    layer_input, out_grad, doc_index, doc_adapter, norm_gain, conv_weight, conv_bias, dt_bias, a_log, skip_gain = rest
    inputs, grads, doc_ids, table = pick(layer_input), pick(out_grad), pick(doc_index), pick(doc_adapter)[0]
    tokens, lane_mask = token_tables(doc_ids[None, :], table)
    vectors = both_layers(jnp.concatenate([conv_weight[0].reshape(1, -1), conv_bias, gate_gain, norm_gain], axis=1))
    numbers = both_layers(jnp.concatenate([dt_bias, a_log, skip_gain], axis=0))
    in_down, in_up, out_down, out_up = adapters
    both = [both_layers(array) for array in (in_down[0], in_up[0].T, out_down[0], out_up[0])]
    where = jnp.stack([place, place ^ (1 + section), place ^ (2 - section), place ^ 3, section]).astype(jnp.int32)
    levels = [
        make_level(sizes, vectors[layer], numbers[layer], [pair[layer] for pair in both], where)
        for layer in range(2)
    ]
    small = [inputs, grads, lane_mask, tokens.__dict__, weights.own[1:]] + [level.__dict__ for level in levels]
    small, weights.parts[0] = lax.optimization_barrier((small, weights.parts[0]))
    inputs, grads, lane_mask, token_fields, weights.own[1:], *level_fields = small
    tokens, levels = Bag(**token_fields), [Bag(**fields) for fields in level_fields]
    levels[0].mixed = weights.parts[0]
    levels[0].gate_first = levels[1].gate_first = False

    moves = {(0, 0): 1, (0, 1): 2, (0, 2): 3, (0, 4): 4, (1, 1): 5}
    results, kept = [], []
    rows_now = inputs
    for layer in range(2):
        stages = layer_forward(sizes, rows_now, levels[layer], lane_mask, tokens, hops)
        for stage in range(5):
            try:
                token = next(stages)
            except StopIteration as end:
                rows_now, stored = end.value
            move = moves.get((layer, stage))
            if move is not None:
                weights.forward(move, token)
                owner, parts = levels[move // 3], weights.parts[move]
                if move % 3 == 0:
                    owner.mixed = parts
                elif move % 3 == 1:
                    owner.gate = parts
                else:
                    owner.out = parts
                if move < 5:
                    weights.start(move + 1, weights.near[move], token)
        results.append(rows_now)
        kept.append(stored)

    direct = lax.axis_size(SEQ) == 4
    both_axes = (WSHARD, SEQ)

    def finish(stages, value):
        try:
            stages.send(value)
        except StopIteration as end:
            return end.value

    stages = layer_backward(sizes, tie(grads, rows_now), kept[1], levels[1], lane_mask, tokens, hops)
    _, pending = next(stages)
    for _ in range(2):
        _, pending = stages.send(pending)
    upper, pending = stages.send(pending)
    upper = chip_start(upper)
    upper_grad = finish(stages, pending)
    upper = scatter_done(upper, upper_grad)
    upper_grad = tie(upper_grad, upper)
    upper = scatter_start(upper, WSHARD) if direct else lax.psum(upper, both_axes)

    stages = layer_backward(sizes, upper_grad, kept[0], levels[0], lane_mask, tokens, hops)
    token, pending = next(stages)
    if direct:
        upper = scatter_start(scatter_done(upper, token), SEQ)
    token, pending = stages.send(tie(pending, upper[0]))
    if direct:
        upper = gather_start(scatter_done(upper, token), SEQ)
    token, pending = stages.send(tie(pending, upper[0]))
    if direct:
        upper = gather_start(gather_done(upper, SEQ, token), WSHARD)
    lower, pending = stages.send(tie(pending, upper[0]))
    lower = chip_start(lower)
    if direct:
        upper = gather_done(upper, WSHARD, lower[0])
    lower = scatter_done(lower, upper)
    if direct:
        lower = scatter_start(lower, WSHARD)
    lower_grad = finish(stages, tie(pending, lower[0]))
    if direct:
        lower = scatter_start(scatter_done(lower, lower_grad), SEQ)
        lower = gather_start(scatter_done(lower), SEQ)
        lower = gather_start(gather_done(lower, SEQ), WSHARD)
        lower = gather_done(lower, WSHARD)
    else:
        lower = lax.psum(lower, both_axes)
    sums = final_sums(sizes, width, section, upper, swap(upper), lower, swap(lower))
    def placed(pair):
        here = jnp.where(section == 0, pair[0], pair[1])
        there = swap(jnp.where(section == 0, pair[1], pair[0]))
        first, second = jnp.where(section == 0, here, there), jnp.where(section == 0, there, here)
        return jnp.stack([first, second])[None]

    down_in, in_up, down_out, out_up = sums
    return (
        placed(results), placed([lower_grad, upper_grad]), down_in[None], in_up.T[None], down_out[None], out_up[None],
    )


def solution(mesh):
    tokens, matrix, vector = P(None, (WSHARD, SEQ), None), P(SECTION, None, None), P(SECTION, None)
    in_specs = (tokens, tokens, P(None, (WSHARD, SEQ)), P(None, WSHARD, None))
    in_specs += (P(SECTION, WSHARD, None),) * 2
    in_specs += (vector, matrix) + (vector,) * 5 + (matrix,) * 4
    out_specs = (P(SECTION, None, (WSHARD, SEQ), None),) * 2 + (matrix,) * 4
    return jax.shard_map(on_device, mesh=mesh, in_specs=in_specs, out_specs=out_specs, check_vma=False)
```

```python
import functools

import jax
import jax.numpy as jnp
from jax import lax
from jax.experimental import pallas as pl
from jax.experimental.pallas import tpu as pltpu
from jax.sharding import PartitionSpec as P

SPAN = 256
RANK = 16
LANES = 128
DOCS_PER_BLOCK = 8
EPSILON = 1e-05
LOG2E = 1.4426950408889634
EXACT = lax.Precision.HIGHEST
SEQ, WSHARD, SECTION = "seq", "wshard", "section"
BF16 = jnp.bfloat16
F32 = jnp.float32
PARAMS = pltpu.CompilerParams(vmem_limit_bytes=20 * 1024 * 1024)


class Bag:
    def __init__(self, **fields):
        self.__dict__.update(fields)


def tie(value, *others):
    return lax.optimization_barrier((value, *others))[0]


def from_behind(value, axis, steps):
    count = lax.axis_size(axis)
    initial, last = (max(0, -steps), min(count, count - steps))
    return lax.ppermute(value, axis, [(source, source + steps) for source in range(initial, last)])


def dot(left, right):
    return jnp.dot(left, right, preferred_element_type=F32)


def dot_last(left, right):
    return lax.dot_general(left, right, (((1,), (1,)), ((), ())), preferred_element_type=F32)


def dot_first(left, right):
    return lax.dot_general(left, right, (((0,), (0,)), ((), ())), preferred_element_type=F32)


def rms_rate(values):
    return lax.rsqrt(jnp.mean(values * values, axis=-1, keepdims=True) + EPSILON)


def sigmoid(v):
    return 0.5 + 0.5 * jnp.tanh(0.5 * v)


def lower_ones(shape):
    rows = lax.broadcasted_iota(jnp.int32, shape, 0)
    columns = lax.broadcasted_iota(jnp.int32, shape, 1)
    return rows <= columns


def conv_rows(rows, rim, weight, offset, valid):
    length = rows.shape[0]
    valid = jnp.concatenate([valid] * (rows.shape[1] // LANES), axis=1)
    extended = jnp.concatenate([rim, rows], axis=0)
    taps = weight.shape[0]
    total = offset + weight[taps - 1 : taps] * rows
    for back in range(1, taps):
        shifted = extended[8 - back : 8 - back + length]
        total = total + jnp.where(valid >= back, shifted, 0.0) * weight[taps - 1 - back : taps - back]
    gate = sigmoid(total)
    active = total * gate
    return active, gate + active * (1.0 - gate)


def taps_at(vector_ref, places, first, width):
    rows = [vector_ref[:, pl.ds(pl.multiple_of(place + first, LANES), width)] for place in places]
    return jnp.concatenate(rows[:-1], axis=0), rows[-1]


def conv_kernel(
    spans, head, heads, state, places,
    mixed_ref, mixed_bc_ref, rim_ref, rim_bc_ref, vector_ref, valid_ref, raw_ref, head_ref, token_ref,
    values_ref, slope_ref, bc_ref, step_ref, *rest,
):
    state_refs, tail_ref = rest[:-1], rest[-1]
    group = pl.program_id(0)
    valid = valid_ref[...]
    width = mixed_ref.shape[1]
    heads_here = width // head

    @pl.when(group == 0)
    def _():
        weight, offset = taps_at(vector_ref, places, pl.num_programs(0) * width, 2 * state)
        active, slope = conv_rows(
            mixed_bc_ref[...].astype(F32), rim_bc_ref[...].astype(F32), weight, offset, valid
        )
        bc_ref[...] = jnp.concatenate([active, slope], axis=1).astype(BF16)
        raw = raw_ref[...].astype(F32).T[:heads] + head_ref[:, 2:3]
        step = (jnp.maximum(raw, 0.0) + jnp.log1p(jnp.exp(-jnp.abs(raw)))).astype(BF16).astype(F32)
        step_ref[:heads, :] = step
        step_ref[2 * heads :, :] = sigmoid(raw)
        drop = step * head_ref[:, :1]
        ones = lower_ones((SPAN, SPAN)).astype(F32)
        for span in range(spans):
            here = slice(span * SPAN, (span + 1) * SPAN)
            decay = jnp.dot(drop[:, here], ones, precision=EXACT, preferred_element_type=F32)
            step_ref[heads : 2 * heads, here] = decay
            tail = jnp.exp2(decay[:, SPAN - 1 :] - decay) * token_ref[span][1:2]
            tail_ref[:, here] = tail * step[:, here]

    weight, offset = taps_at(vector_ref, places, group * width, width)
    active, slope = conv_rows(
        mixed_ref[...].astype(F32), rim_ref[...].astype(F32), weight, offset, valid
    )
    slope_ref[...] = slope.astype(BF16)
    low = active.T.astype(BF16)
    values_ref[...] = low
    low = low.astype(F32)
    first = pl.multiple_of(group * heads_here, heads_here)
    tail_rows = tail_ref[pl.ds(first, heads_here), :]
    for span in range(spans):
        here = slice(span * SPAN, (span + 1) * SPAN)
        driven = jnp.concatenate(
            [
                (low[place * head : (place + 1) * head, here] * tail_rows[place : place + 1, here]).astype(BF16)
                for place in range(heads_here)
            ],
            axis=0,
        )
        state_refs[span][...] = dot(driven, bc_ref[here, :state]).astype(BF16)


def faded(row, column, score_ref):
    half = SPAN // 2
    upper = jnp.exp2(jnp.minimum(row - column[:half], 0.0))
    lower = jnp.exp2(jnp.minimum(row[:, half:] - column[half:], 0.0))
    lower = jnp.concatenate([jnp.zeros_like(lower), lower], axis=1)
    return (upper, lower), (upper * score_ref[:half, :], lower * score_ref[half:, :])


def scan_kernel(
    head, state, gain,
    values_ref, bc_ref, step_ref, decay_ref, token_ref, doc_column_ref, doc_row_ref, state_ref, head_ref, gate_ref,
    vector_ref, *rest,
):
    mixed_ref, normed_ref, score_ref, scanned_ref = rest[-4:]
    group, groups = pl.program_id(0), pl.num_programs(0)
    width = values_ref.shape[0]
    heads_here = width // head

    @pl.when(group == 0)
    def _():
        score = dot_last(bc_ref[:, :state], bc_ref[:, state:])
        same = (jnp.concatenate([doc_column_ref[...]] * (SPAN // LANES), axis=1) == doc_row_ref[:1]) & lower_ones((SPAN, SPAN))
        score_ref[...] = jnp.where(same, score, 0.0)

    decay, step = decay_ref[...], step_ref[...]
    carry = jnp.exp2(decay) * token_ref[0][:1]
    columns = jnp.concatenate([decay] * (LANES // heads_here), axis=0).T
    out_map = bc_ref[:, state:]
    parts = []
    for place in range(heads_here):
        rows = slice(place * head, (place + 1) * head)
        one = slice(place, place + 1)
        kernel = jnp.concatenate([part.astype(BF16) for part in faded(decay[one], columns[:, one], score_ref)[1]], axis=0)
        values = values_ref[rows].astype(F32)
        driven = (values * step[one]).astype(BF16)
        before = dot_last(state_ref[rows], out_map) * carry[one]
        parts.append(dot(driven, kernel) + before + head_ref[one, 1:2] * values)
    low = jnp.concatenate(parts, axis=0).astype(BF16).T
    mixed_ref[...] = low
    scanned_ref[:, pl.ds(pl.multiple_of(group * width, width), width)] = low

    @pl.when(group == groups - 1)
    def _():
        def rows_at(index, _):
            rows = pl.ds(pl.multiple_of(index * 16, 16), 16)
            mixed = scanned_ref[rows, :]
            gate = gate_ref[rows, :].astype(F32)
            gated = mixed.astype(F32) * (gate * sigmoid(gate))
            normed_ref[rows, :] = (gated * rms_rate(gated) * vector_ref[:, gain : gain + gated.shape[1]]).astype(BF16)
            return 0

        lax.fori_loop(0, SPAN // 16, rows_at, 0, unroll=4)


def out_back_kernel(
    head, heads, state, gain, count,
    up_ref, lane_ref, up_out_ref, down_out_ref, mixed_ref, gate_ref, vector_ref, decay_ref, token_ref, bc_ref, where_ref,
    *rest,
):
    parts, rest = rest[:count], rest[count:]
    (project_ref, turned_ref, narrow_ref), state_refs, (grad_ref, grad_mixed_ref) = rest[:3], rest[3:-2], rest[-2:]
    width = mixed_ref.shape[1]
    up = up_ref[...]
    narrow = (dot_last(up, up_out_ref[...]) * lane_ref[...]).astype(BF16)
    narrow_ref[...] = narrow
    left = jnp.concatenate([up, narrow], axis=1)
    for offset, part in out_places(where_ref, parts):
        here = pl.ds(offset, part.shape[0])
        grad_ref[:, here] = dot_last(left, jnp.concatenate([part[...], down_out_ref[here, :]], axis=1))

    def rows_at(index, _):
        rows = pl.ds(pl.multiple_of(index * 16, 16), 16)
        mixed = mixed_ref[rows, :].astype(F32)
        gate = gate_ref[rows, :].astype(F32)
        share = sigmoid(gate)
        silu = gate * share
        gated = mixed * silu
        grad = grad_ref[rows, :] * vector_ref[:, gain : gain + width]
        rate = rms_rate(gated)
        pull = jnp.mean(gated * grad, axis=-1, keepdims=True) * rate * rate * rate
        grad_gated = rate * grad - gated * pull
        project_ref[rows, :] = (grad_gated * mixed * (share + silu * (1.0 - share))).astype(BF16)
        grad_mixed_ref[rows, :] = (grad_gated * silu).astype(BF16)
        return 0

    lax.fori_loop(0, SPAN // 16, rows_at, 0, unroll=4)
    carry = jnp.exp2(decay_ref[...]) * token_ref[0][:1]
    out_map = bc_ref[:, state:]
    wide = 512
    for first in range(0, width, wide):
        low = grad_mixed_ref[:, first : first + wide].astype(F32).T
        turned_ref[first : first + wide, :] = low.astype(BF16)
        scaled = [
            (low[place * head : (place + 1) * head] * carry[first // head + place : first // head + place + 1]).astype(BF16)
            for place in range(wide // head)
        ]
        local = dot(jnp.concatenate(scaled, axis=0), out_map).astype(BF16)
        for span, state_ref in enumerate(state_refs):

            @pl.when(pl.program_id(0) == span)
            def _(state_ref=state_ref, first=first, local=local):
                state_ref[first : first + wide, :] = local


def aligned(value, unit):
    return pl.multiple_of(value * unit, unit)


def out_places(where_ref, parts):
    if len(parts) == 1:
        half = parts[0].shape[1]
        return [((2 * place + side) * half, parts[0].at[4 * side + place]) for place in range(4) for side in range(2)]
    rows, half = parts[0].shape[0], parts[3].shape[0]
    places = [(aligned(where_ref[place], rows), part) for place, part in enumerate(parts[:3])]
    apart = where_ref[3] * 2
    places.append((aligned(apart + where_ref[4], half), parts[3]))
    places.append((aligned(apart + 1 - where_ref[4], half), parts[4]))
    return places


def in_rows(where_ref, parts, step, start, size):
    side = int(start >= step)
    there = slice(start - side * step, start - side * step + size)
    if len(parts) == 1:
        return [parts[0][4 * side + place, there, :] for place in range(4)]
    pair = (parts[3][there], parts[4][there])
    apart = jnp.where(where_ref[4] == 0, pair[side], pair[1 - side])
    return [part[start : start + size] for part in parts[:3]] + [apart]


def in_columns(ref, where_ref, parts):
    columns = (ref.shape[1] - LANES) // parts
    places = [pl.ds(aligned(where_ref[place], columns), columns) for place in range(parts)]
    return jnp.concatenate([ref[:, here] for here in places + [pl.ds(parts * columns, LANES)]], axis=1)


def mixed_kernel(
    main, lanes, gain, count, input_ref, vector_ref, down_ref, lane_ref, up_ref, where_ref, *rest
):
    parts, (normed_ref, mixed_ref, raw_ref, rim_ref) = rest[:count], rest[count:]
    rows = input_ref.shape[0]
    inputs = input_ref[...].astype(F32)
    normed = (inputs * rms_rate(inputs) * vector_ref[:, gain : gain + inputs.shape[1]]).astype(BF16)
    narrow = (dot(normed, down_ref[...]) * lane_ref[...]).astype(BF16)
    normed_ref[...] = jnp.concatenate([normed, narrow], axis=1)
    left = in_columns(normed_ref, where_ref, 4)
    step, extra = main // 6, raw_ref.shape[1] // 4
    before = up_ref.shape[0] - main - extra

    def product(start, size):
        right = in_rows(where_ref, parts, main // 2, start, size)
        right.append(up_ref[before + start : before + start + size])
        return dot_last(left, jnp.concatenate(right, axis=1))

    for start in range(0, main, step):
        low = product(start, step).astype(BF16)
        mixed_ref[:, start : start + step] = low
        rim_ref[:, start : start + step] = low[rows - 8 :]
    raw_ref[...] = jnp.concatenate([product(main, extra), jnp.zeros((rows, lanes - extra), F32)], axis=1).astype(BF16)


def gate_kernel(count, normed_ref, up_ref, where_ref, *rest):
    parts, gate_ref = rest[:count], rest[count]
    left = in_columns(normed_ref, where_ref, 4)
    wide = 512
    inner = gate_ref.shape[1]
    for start in range(0, inner, wide):
        right = in_rows(where_ref, parts, inner // 2, start, wide) + [up_ref[start : start + wide]]
        gate_ref[:, start : start + wide] = dot_last(left, jnp.concatenate(right, axis=1)).astype(BF16)


def out_kernel(count, normed_ref, input_ref, down_ref, lane_ref, up_ref, where_ref, *rest):
    parts, (narrow_ref, out_ref) = rest[:count], rest[count:]
    narrow = (dot(normed_ref[...], down_ref[...]) * lane_ref[...]).astype(BF16)
    narrow_ref[...] = narrow
    places = out_places(where_ref, parts)
    left = [normed_ref[:, pl.ds(offset, part.shape[0])] for offset, part in places]
    left = jnp.concatenate(left + [narrow], axis=1)
    wide = 256
    for start in range(0, out_ref.shape[1], wide):
        here = slice(start, start + wide)
        right = jnp.concatenate([part[:, here] for _, part in places] + [up_ref[:, here]], axis=0)
        out_ref[:, here] = (input_ref[:, here].astype(F32) + dot(left, right)).astype(BF16)


def gate_in_back_kernel(count, grad_ref, up_ref, where_ref, *rest):
    parts, out_ref = rest[:count], rest[count]
    grad = grad_ref[...]
    half = grad.shape[1] // 2
    lower, upper = [in_rows(where_ref, parts, half, side * half, half) for side in range(2)]
    columns = lower[0].shape[1]
    for place in range(4):
        product = dot(grad[:, :half], lower[place]) + dot(grad[:, half:], upper[place])
        out_ref[:, place * columns : (place + 1) * columns] = product
    out_ref[:, 4 * columns :] = dot(grad, up_ref[...])


def narrow_back_kernel(main, extra, grad_ref, raw_ref, part_ref, lane_ref, up_ref, narrow_ref):
    before = up_ref.shape[0] - main - extra
    total = part_ref[...] + dot(grad_ref[...], up_ref[before : before + main])
    total = total + dot(raw_ref[...][:, :extra], up_ref[before + main :])
    narrow_ref[...] = (total * lane_ref[...]).astype(BF16)


def mixed_in_back_kernel(
    main, extra, gain, count,
    grad_ref, raw_ref, part_ref, input_ref, up_stream_ref, vector_ref, narrow_ref, down_ref, where_ref, *rest
):
    parts, (out_ref, total_ref) = rest[:count], rest[count:]
    width = input_ref.shape[1]
    columns = width // 4
    half = main // 2
    left = jnp.concatenate([grad_ref[...], raw_ref[...][:, :extra]], axis=1)
    lower = in_rows(where_ref, parts, half, 0, half)
    upper = in_rows(where_ref, parts, half, half, half + extra)
    for place in range(4):
        product = dot(left[:, :half], lower[place]) + dot(left[:, half:], upper[place])
        here = slice(place * columns, (place + 1) * columns)
        total_ref[:, pl.ds(aligned(where_ref[place], columns), columns)] = part_ref[:, here] + product
    scaled = (total_ref[...] + dot_last(narrow_ref[...], down_ref[...])) * vector_ref[:, gain : gain + width]
    inputs = input_ref[...].astype(F32)
    rate = rms_rate(inputs)
    pull = jnp.mean(inputs * scaled, axis=-1, keepdims=True) * rate * rate * rate
    out_ref[...] = (up_stream_ref[...].astype(F32) + rate * scaled - inputs * pull).astype(BF16)


def scan_back_kernel(
    head, heads, state, edge,
    values_ref, grad_ref, bc_ref, step_ref, decay_ref, sig_ref, token_ref, doc_column_ref, doc_row_ref, state_ref,
    grad_state_ref, head_ref, rate_ref, slope_ref, slope_bc_ref, *rest,
):
    outputs = rest[:-6]
    if edge:
        outputs, edge_ref = outputs[:-1], outputs[-1]
    out_values_ref, out_bc_ref, out_raw_ref = outputs[-3:]
    score_ref, grad_score_ref, pull_ref, direct_ref, grad_in_ref, grad_out_ref = rest[-6:]
    group, groups = pl.program_id(0), pl.num_programs(0)
    width = values_ref.shape[0]
    heads_here = width // head
    in_map, out_map = bc_ref[:, :state], bc_ref[:, state:]

    def same_doc():
        return (jnp.concatenate([doc_column_ref[...]] * (SPAN // LANES), axis=1) == doc_row_ref[:1]) & lower_ones((SPAN, SPAN))

    @pl.when(group == 0)
    def _():
        score_ref[...] = jnp.where(same_doc(), dot_last(in_map, out_map), 0.0)
        grad_score_ref[...] = jnp.zeros_like(grad_score_ref)
        grad_in_ref[...] = jnp.zeros_like(grad_in_ref)
        grad_out_ref[...] = jnp.zeros_like(grad_out_ref)

    decay, step = decay_ref[...], step_ref[...]
    token = token_ref[0]
    last = decay[:, SPAN - 1 :]
    carry = jnp.exp2(decay) * token[:1]
    tail = jnp.exp2(last - decay) * token[1:2]
    keep = jnp.exp2(last) * token[2:3, :1]
    columns = jnp.concatenate([decay] * (LANES // heads_here), axis=0).T
    at_end = lax.broadcasted_iota(jnp.int32, (1, SPAN), 1) == SPAN - 1
    grads, tails, carried, pulls, directs = [], [], [], [], []
    for place in range(heads_here):
        rows = slice(place * head, (place + 1) * head)
        one = slice(place, place + 1)
        fade, kernel = faded(decay[one], columns[:, one], score_ref)
        kernel = jnp.concatenate([part.astype(BF16) for part in kernel], axis=0)
        values = values_ref[rows].astype(F32)
        driven = (values * step[one]).astype(BF16)
        grad_low = grad_ref[rows]
        grad = grad_low.astype(F32)
        grad_kernel = dot_first(driven, grad_low)
        half = SPAN // 2
        grad_score_ref[:half, :] += grad_kernel[:half] * fade[0]
        grad_score_ref[half:, half:] += grad_kernel[half:, half:] * fade[1][:, half:]
        state_here, grad_state = state_ref[rows], grad_state_ref[rows]
        output = dot(driven, kernel) + dot_last(state_here, out_map) * carry[one]
        by_state = dot_last(grad_state, in_map) * tail[one]
        grad_driven = dot_last(grad_low, kernel) + by_state
        driven = driven.astype(F32)
        pull = jnp.sum(grad * output - driven * grad_driven, axis=0, keepdims=True)
        ending = jnp.sum(jnp.sum(driven * by_state, axis=0, keepdims=True), axis=1, keepdims=True)
        kept = jnp.sum(state_here.astype(F32) * grad_state.astype(F32), axis=0, keepdims=True)
        ending = ending + keep[one] * jnp.sum(kept, axis=1, keepdims=True)
        pulls.append(pull + jnp.where(at_end, ending, 0.0))
        directs.append(jnp.sum(values * grad_driven, axis=0, keepdims=True))
        grads.append(step[one] * grad_driven + head_ref[one, 1:2] * grad)
        tails.append((driven * tail[one]).astype(BF16))
        carried.append((grad * carry[one]).astype(BF16))
    grad_in_ref[...] += dot_first(jnp.concatenate(tails, axis=0), grad_state_ref[...])
    grad_out_ref[...] += dot_first(jnp.concatenate(carried, axis=0), state_ref[...])
    grads = jnp.concatenate(grads, axis=0).T.astype(BF16)
    out_values_ref[...] = grads
    if edge:
        product = grads[:8].astype(F32) * slope_ref[...][:8].astype(F32)
        edge_ref[:, pl.ds(pl.multiple_of(group * width, width), width)] = product.astype(BF16)
    here = pl.ds(pl.multiple_of(group * heads_here, heads_here), heads_here)
    pull_ref[here, :] = jnp.concatenate(pulls, axis=0)
    direct_ref[here, :] = jnp.concatenate(directs, axis=0)

    @pl.when(group == groups - 1)
    def _():
        ones = lower_ones((SPAN, SPAN)).astype(F32)
        summed = lax.dot_general(
            pull_ref[...], ones, (((1,), (1,)), ((), ())), precision=EXACT, preferred_element_type=F32
        )
        grad_step = (direct_ref[...] + rate_ref[:, 3:4] * summed).astype(BF16).astype(F32)
        grad_raw = grad_step * sig_ref[...]
        padded = jnp.concatenate([grad_raw, jnp.zeros((LANES - heads, SPAN), F32)], axis=0)
        out_raw_ref[...] = padded.T.astype(BF16)
        grad_score = jnp.where(same_doc(), grad_score_ref[...], 0.0).astype(BF16)
        grad_in = grad_in_ref[...] + dot(grad_score, out_map)
        grad_out = grad_out_ref[...] + dot_first(grad_score, in_map)
        low = jnp.concatenate([grad_in, grad_out], axis=1).astype(BF16)
        out_bc_ref[...] = low
        if edge:
            product = low[:8].astype(F32) * slope_bc_ref[...][:8].astype(F32)
            edge_ref[:, groups * width :] = product.astype(BF16)


def conv_back_kernel(
    value_blocks, places,
    grad_ref, grad_bc_ref, slope_ref, slope_bc_ref, next_ref, vector_ref, valid_ref, next_valid_ref, project_ref,
):
    block = pl.program_id(0)
    length = grad_ref.shape[0]

    def back(grad_low, slope_low):
        grad = grad_low.astype(F32) * slope_low.astype(F32)
        later = next_ref[...].astype(F32)
        weight, _ = taps_at(vector_ref, places, block * grad.shape[1], grad.shape[1])
        valid, next_valid = [jnp.concatenate([ref[...]] * (grad.shape[1] // LANES), axis=1) for ref in (valid_ref, next_valid_ref)]
        taps = weight.shape[0]
        total = weight[taps - 1 : taps] * grad
        for ahead in range(1, taps):
            extended = jnp.concatenate(
                [jnp.where(valid >= ahead, grad, 0.0), jnp.where(next_valid >= ahead, later, 0.0)], axis=0
            )
            total = total + weight[taps - 1 - ahead : taps - ahead] * extended[ahead : ahead + length]
        project_ref[...] = total.astype(BF16)

    @pl.when(block < value_blocks)
    def _():
        back(grad_ref[...], slope_ref[...])

    @pl.when(block == value_blocks)
    def _():
        back(grad_bc_ref[...], slope_bc_ref[...])


def spec(shape, index):
    return pl.BlockSpec(shape, index)


def whole(shape):
    return pl.BlockSpec(shape, lambda *_: (0,) * len(shape))


def cost(microseconds):
    return pl.CostEstimate(flops=int(microseconds * 3.45e+09), bytes_accessed=1 << 16, transcendentals=0)


class Sizes:
    def __init__(self, rows, inner, heads, state, columns, taps):
        self.rows, self.inner, self.heads, self.state, self.columns, self.taps = rows, inner, heads, state, columns, taps
        self.head = inner // heads
        self.spans = rows // SPAN
        self.mixed = inner + 2 * state
        self.group_heads = 8
        self.groups = heads // self.group_heads
        self.wide = self.group_heads * self.head
        self.places = tuple(tap * self.mixed for tap in range(taps + 1))
        self.gate_gain = (taps + 1) * self.mixed
        self.norm_gain = self.gate_gain + inner


def conv_forward(sizes, mixed, raw, rim, level, tokens):
    s = sizes
    rows, wide, heads, state = s.rows, s.wide, s.heads, s.state
    maps = s.inner // (2 * state)
    shapes = [(s.inner, rows), (rows, s.inner), (rows, 4 * state)]
    args = [level.vector, tokens.valid, raw, level.heads, tokens.flags]
    outputs = pl.pallas_call(
        functools.partial(conv_kernel, s.spans, s.head, heads, state, s.places),
        grid=(s.groups,),
        in_specs=[
            spec((rows, wide), lambda g: (0, g)), spec((rows, 2 * state), lambda g: (0, maps)),
            spec((8, wide), lambda g: (0, g)), spec((8, 2 * state), lambda g: (0, maps)), *whole_specs(*args),
        ],
        out_specs=[
            spec((wide, rows), lambda g: (g, 0)), spec((rows, wide), lambda g: (0, g)), whole(shapes[2]),
            whole((3 * heads, rows)),
        ] + [spec((wide, state), lambda g: (g, 0))] * s.spans,
        out_shape=[shape_of(shapes[0]), far_shape(shapes[1]), shape_of(shapes[2]), shape_of((3 * heads, rows), F32)]
        + [shape_of((s.inner, state))] * s.spans,
        scratch_shapes=[pltpu.VMEM((heads, rows), F32)],
        compiler_params=PARAMS,
        cost_estimate=cost(8.5),
    )(mixed, mixed, rim, rim, *args)
    return outputs[:4], outputs[4:]


def span_specs(sizes, span):
    s = sizes
    return Bag(
        turned=spec((s.wide, SPAN), lambda g: (g, span)),
        maps=spec((SPAN, 2 * s.state), lambda g: (span, 0)),
        rows=spec((s.group_heads, SPAN), lambda g: (g, span)),
        decay=spec((s.group_heads, SPAN), lambda g: (s.groups + g, span)),
        flags=spec((1, 8, SPAN), lambda g: (span, 0, 0)),
        doc_column=spec((SPAN, LANES), lambda g: (span, 0)),
        doc_row=spec((8, SPAN), lambda g: (0, span)),
        state=spec((s.wide, s.state), lambda g: (g, 0)),
        head=spec((s.group_heads, LANES), lambda g: (g, 0)),
        full=spec((SPAN, s.inner), lambda g: (span, 0)),
    )


ANYWHERE = pl.BlockSpec(memory_space=pl.ANY)


def scan_forward(sizes, span, conv, state_in, gate, level, tokens, earlier):
    s = sizes
    at = span_specs(s, span)
    args = [
        conv.values, conv.maps, conv.step, conv.step, tokens.flags, tokens.column, tokens.row, state_in, level.heads,
        gate, level.vector,
    ]
    in_specs = [
        at.turned, at.maps, at.rows, at.decay, at.flags, at.doc_column, at.doc_row, at.state,
        at.head, at.full, whole(level.vector.shape),
    ]
    aliases = {}
    if earlier is not None:
        aliases = {len(args): 0, len(args) + 1: 1}
        args, in_specs = args + list(earlier), in_specs + [ANYWHERE] * 2
    shape = (s.rows, s.inner)
    return pl.pallas_call(
        functools.partial(scan_kernel, s.head, s.state, s.gate_gain),
        grid=(s.groups,),
        in_specs=in_specs,
        out_specs=[spec((SPAN, s.wide), lambda g: (span, g)), at.full],
        out_shape=[shape_of(shape), shape_of(shape)],
        scratch_shapes=[pltpu.VMEM((SPAN, SPAN), F32), pltpu.VMEM((SPAN, s.inner), BF16)],
        input_output_aliases=aliases,
        compiler_params=PARAMS,
        cost_estimate=cost(6.5),
    )(*args)


SMALL = pl.BlockSpec(memory_space=pltpu.SMEM)


def shape_of(shape, dtype=BF16):
    return jax.ShapeDtypeStruct(shape, dtype)


def far_shape(shape, dtype=BF16):
    return pltpu.HBM(shape, dtype)


def whole_specs(*arrays):
    return [whole(array.shape) for array in arrays]


def project_mixed(sizes, inputs, level, lane_mask):
    s = sizes
    args = [inputs, level.vector, level.in_down, lane_mask, level.in_up]
    width = inputs.shape[1]
    shapes = [(s.rows, width + LANES), (s.rows, s.mixed), (s.rows, LANES), (8, s.mixed)]
    return pl.pallas_call(
        functools.partial(mixed_kernel, s.mixed, LANES, s.norm_gain, len(level.mixed)),
        grid=(1,),
        in_specs=whole_specs(*args) + [SMALL] + whole_specs(*level.mixed),
        out_specs=[whole(shape) for shape in shapes],
        out_shape=[shape_of(shape) for shape in shapes],
        compiler_params=PARAMS,
        cost_estimate=cost(6),
    )(*args, level.mixed_where, *level.mixed)


def gate_specs(sizes, level):
    return [whole((sizes.inner, LANES)), SMALL] + whole_specs(*level.gate)


def project_gate(sizes, normed, level):
    s = sizes
    return pl.pallas_call(
        functools.partial(gate_kernel, len(level.gate)),
        grid=(1,),
        in_specs=whole_specs(normed) + gate_specs(s, level),
        out_specs=whole((s.rows, s.inner)),
        out_shape=shape_of((s.rows, s.inner)),
        compiler_params=PARAMS,
        cost_estimate=cost(3.6),
    )(normed, level.in_up, level.where, *level.gate)


def project_out(sizes, normed_out, inputs, level, lane_mask):
    s = sizes
    args = [normed_out, inputs, level.out_down, lane_mask, level.out_up]
    shapes = [(s.rows, LANES), inputs.shape]
    return pl.pallas_call(
        functools.partial(out_kernel, len(level.out)),
        grid=(1,),
        in_specs=whole_specs(*args) + [SMALL] + whole_specs(*level.out),
        out_specs=[whole(shape) for shape in shapes],
        out_shape=[shape_of(shape) for shape in shapes],
        compiler_params=PARAMS,
        cost_estimate=cost(4),
    )(*args, level.where, *level.out)


def out_backward(sizes, upstream, mixed, gate, conv, level, lane_mask, tokens):
    s = sizes
    full = spec((SPAN, s.inner), lambda k: (k, 0))
    width = upstream.shape[1]
    return pl.pallas_call(
        functools.partial(out_back_kernel, s.head, s.heads, s.state, s.gate_gain, len(level.out)),
        grid=(s.spans,),
        in_specs=[
            spec((SPAN, width), lambda k: (k, 0)), spec((SPAN, LANES), lambda k: (k, 0)),
            *whole_specs(level.out_up, level.out_down), full, full, whole(level.vector.shape),
            spec((s.heads, SPAN), lambda k: (1, k)), spec((1, 8, SPAN), lambda k: (k, 0, 0)),
            spec((SPAN, 2 * s.state), lambda k: (k, 0)), SMALL, *whole_specs(*level.out),
        ],
        out_specs=[
            full, spec((s.inner, SPAN), lambda k: (0, k)), spec((SPAN, LANES), lambda k: (k, 0)),
        ] + [whole((s.inner, s.state))] * s.spans,
        out_shape=[
            shape_of((s.rows, s.inner)), shape_of((s.inner, s.rows)), shape_of((s.rows, LANES)),
        ] + [shape_of((s.inner, s.state))] * s.spans,
        scratch_shapes=[pltpu.VMEM((SPAN, s.inner), F32), pltpu.VMEM((SPAN, s.inner), BF16)],
        compiler_params=PARAMS,
        cost_estimate=cost(13.5),
    )(
        upstream, lane_mask, level.out_up, level.out_down, mixed, gate, level.vector, conv.step, tokens.flags, conv.maps,
        level.where, *level.out,
    )


def gate_in_backward(sizes, grad_gate, level):
    s = sizes
    width = 4 * s.columns + LANES
    return pl.pallas_call(
        functools.partial(gate_in_back_kernel, len(level.gate)),
        grid=(1,),
        in_specs=whole_specs(grad_gate) + gate_specs(s, level),
        out_specs=whole((s.rows, width)),
        out_shape=shape_of((s.rows, width), F32),
        compiler_params=PARAMS,
        cost_estimate=cost(3.5),
    )(grad_gate, level.in_up, level.where, *level.gate)


def narrow_backward(sizes, grad_mixed, raw, part, level, lane_mask):
    s = sizes
    args = [grad_mixed, raw, part, lane_mask, level.in_up]
    in_specs = whole_specs(*args)
    in_specs[2] = spec((s.rows, LANES), lambda _: (0, part.shape[1] // LANES - 1))
    return pl.pallas_call(
        functools.partial(narrow_back_kernel, s.mixed, s.heads),
        grid=(1,),
        in_specs=in_specs,
        out_specs=whole((s.rows, LANES)),
        out_shape=shape_of((s.rows, LANES)),
        compiler_params=PARAMS,
        cost_estimate=cost(0.9),
    )(*args)


def mixed_in_backward(sizes, grad_mixed, raw, part, inputs, upstream, narrow, level):
    s = sizes
    width = inputs.shape[1]
    rows = lambda columns: spec((SPAN, columns), lambda k: (k, 0))
    return pl.pallas_call(
        functools.partial(mixed_in_back_kernel, s.mixed, s.heads, s.norm_gain, len(level.mixed)),
        grid=(s.spans,),
        in_specs=[
            rows(s.mixed), rows(LANES), rows(width + LANES), rows(width), rows(width), whole(level.vector.shape),
            rows(LANES), *whole_specs(level.in_down), SMALL, *whole_specs(*level.mixed),
        ],
        out_specs=rows(width),
        out_shape=shape_of((s.rows, width)),
        scratch_shapes=[pltpu.VMEM((SPAN, width), F32)],
        compiler_params=PARAMS,
        cost_estimate=cost(4.7),
    )(grad_mixed, raw, part, inputs, upstream, level.vector, narrow, level.in_down, level.mixed_where, *level.mixed)


def scan_backward(sizes, span, conv, grad_turned, state_in, grad_state, level, tokens, earlier):
    s = sizes
    at = span_specs(s, span)
    args = [
        conv.values, grad_turned, conv.maps, conv.step, conv.step, conv.step, tokens.flags, tokens.column, tokens.row,
        state_in, grad_state, level.heads, level.heads, conv.slope, conv.maps,
    ]
    in_specs = [
        at.turned, at.turned, at.maps, at.rows, at.decay, spec((s.heads, SPAN), lambda g: (2, span)), at.flags,
        at.doc_column, at.doc_row, at.state, at.state, at.head, whole((s.heads, LANES)),
        spec((16, s.wide), lambda g: (0, g)), spec((16, 2 * s.state), lambda g: (0, 1)),
    ]
    aliases = {}
    if earlier is not None:
        aliases = {len(args) + place: place for place in range(3)}
        args, in_specs = args + list(earlier[:3]), in_specs + [ANYWHERE] * 3
    out_specs = [spec((SPAN, s.wide), lambda g: (span, g)), at.maps, spec((SPAN, LANES), lambda g: (span, 0))]
    out_shape = [shape_of((s.rows, s.inner)), shape_of((s.rows, 2 * s.state)), shape_of((s.rows, LANES))]
    if span == 0:
        out_specs, out_shape = out_specs + [whole((8, s.mixed))], out_shape + [shape_of((8, s.mixed))]
    return pl.pallas_call(
        functools.partial(scan_back_kernel, s.head, s.heads, s.state, span == 0),
        grid=(s.groups,),
        in_specs=in_specs,
        out_specs=out_specs,
        out_shape=out_shape,
        scratch_shapes=[
            pltpu.VMEM((SPAN, SPAN), F32), pltpu.VMEM((SPAN, SPAN), F32), pltpu.VMEM((s.heads, SPAN), F32),
            pltpu.VMEM((s.heads, SPAN), F32), pltpu.VMEM((SPAN, s.state), F32), pltpu.VMEM((SPAN, s.state), F32),
        ],
        input_output_aliases=aliases,
        compiler_params=PARAMS,
        cost_estimate=cost(8.5),
    )(*args)


def conv_backward(sizes, grad_values, grad_maps, conv, later, level, tokens):
    s = sizes
    wide = 2 * s.state
    blocks = s.inner // wide
    values = spec((s.rows, wide), lambda i: (0, jnp.minimum(i, blocks - 1)))
    maps, slopes = whole((s.rows, wide)), spec((s.rows, wide), lambda i: (0, 1))
    fixed = [level.vector, tokens.valid, tokens.next_valid]
    return pl.pallas_call(
        functools.partial(conv_back_kernel, blocks, s.places),
        grid=(blocks + 1,),
        in_specs=[values, maps, values, slopes, spec((8, wide), lambda i: (0, i)), *whole_specs(*fixed)],
        out_specs=spec((s.rows, wide), lambda i: (0, i)),
        out_shape=shape_of((s.rows, s.mixed)),
        compiler_params=PARAMS,
        cost_estimate=cost(4.4),
    )(grad_values, grad_maps, conv.slope, conv.maps, later, *fixed)


def stacked_kernel(places, *refs):
    out_ref = refs[-1]
    first = 0
    for left, right in places:
        rows = refs[left].shape[1]
        out_ref[first : first + rows, :] = dot_first(refs[left][...], refs[right][...]).astype(BF16)
        first += rows
    if first < out_ref.shape[0]:
        out_ref[first:, :] = jnp.zeros((out_ref.shape[0] - first, out_ref.shape[1]), BF16)


def stacked(sizes, args, places, columns, rows, first, buffer, all_rows):
    s = sizes
    in_specs = [spec((s.rows, width), functools.partial(lambda at, _: (0, at), at)) for at, width in columns]
    aliases = {}
    if buffer is not None:
        aliases = {len(args): 0}
        args, in_specs = args + [buffer], in_specs + [ANYWHERE]
    return pl.pallas_call(
        functools.partial(stacked_kernel, places),
        grid=(1,),
        in_specs=in_specs,
        out_specs=pl.BlockSpec((pl.Element(rows), pl.Element(LANES)), lambda _: (first, 0)),
        out_shape=shape_of((all_rows, LANES)),
        input_output_aliases=aliases,
        compiler_params=PARAMS,
        cost_estimate=cost(1.6),
    )(*args)


def grad_rows(sizes, width):
    return width + 2 * sizes.inner, -(-(width + sizes.mixed + LANES) // 512) * 512


def early_grads(sizes, upstream, kept, grad_narrow_out, grad_gate, first, buffer, all_rows):
    s = sizes
    width = upstream.shape[1]
    args = [upstream, kept.narrow_out, kept.normed_out, grad_narrow_out, grad_gate, kept.normed]
    columns = [(0, width), (0, LANES), (0, s.inner), (0, LANES), (0, s.inner), (width // LANES, LANES)]
    return stacked(
        s, args, ((0, 1), (2, 3), (4, 5)), columns, grad_rows(s, width)[0], first, buffer, all_rows
    )


def late_grads(sizes, kept, grad_narrow, grad_mixed, raw, first, buffer, all_rows):
    s = sizes
    width = kept.inputs.shape[1]
    args = [kept.normed, grad_narrow, grad_mixed, raw, kept.normed]
    columns = [(0, width), (0, LANES), (0, s.mixed), (0, LANES), (width // LANES, LANES)]
    return stacked(s, args, ((0, 1), (2, 4), (3, 4)), columns, grad_rows(s, width)[1], first, buffer, all_rows)


def final_kernel(width, inner, where_ref, *refs):
    upper, upper_other, lower, lower_other, down_in_ref, in_up_ref, down_out_ref, out_up_ref = refs
    first = where_ref[0] == 0
    half = upper.shape[0]

    def rows(start, stop):
        pieces = []
        for side, (mine, yours) in enumerate(((lower, upper_other), (lower_other, upper))):
            low, high = max(start - side * half, 0), min(stop - side * half, half)
            if low < high:
                pieces.append(jnp.where(first, mine[low:high], yours[low:high]).astype(F32))
        return pieces

    def put(ref, at, start, stop):
        for piece in rows(start, stop):
            ref[at : at + piece.shape[0], :] = piece
            at += piece.shape[0]

    out_up_ref[...] = jnp.concatenate(rows(0, width), axis=0).T
    put(down_out_ref, 0, width, width + inner)
    put(in_up_ref, 0, width + inner, width + 2 * inner)
    late = width + 2 * inner
    put(down_in_ref, 0, late, late + width)
    put(in_up_ref, inner, late + width, late + width + in_up_ref.shape[0] - inner)


def final_sums(sizes, width, section, *sums):
    s = sizes
    shapes = [(width, LANES), (s.inner + s.mixed + s.heads, LANES), (s.inner, LANES), (LANES, width)]
    return pl.pallas_call(
        functools.partial(final_kernel, width, s.inner),
        grid=(1,),
        in_specs=[SMALL] + whole_specs(*sums),
        out_specs=[whole(shape) for shape in shapes],
        out_shape=[shape_of(shape, F32) for shape in shapes],
        compiler_params=PARAMS,
    )(section[None], *sums)


def token_kernel(spans, row_ref, before_ref, after_ref, table_ref, valid_ref, next_ref, column_ref, mask_ref, flags_ref):
    length = row_ref.shape[1]
    row = row_ref[...].astype(F32)
    ids = jnp.concatenate([before_ref[...].astype(F32), row, after_ref[...].astype(F32)], axis=1)
    behind = jnp.zeros((1, length + LANES), F32)
    for back in (1, 2, 3):
        same = ids[:, LANES - back : 2 * LANES - back + length] == ids[:, LANES : 2 * LANES + length]
        behind = behind + jnp.where(same, 1.0, 0.0)
    adapter = jnp.zeros_like(row)
    for document in range(table_ref.shape[0]):
        adapter = jnp.where(row == document, table_ref[document].astype(F32), adapter)
    rows = jnp.concatenate([behind[:, :length], row, adapter, jnp.zeros((5, length), F32)], axis=0).T
    wide = (length, LANES)
    valid_ref[...] = jnp.broadcast_to(rows[:, :1], wide).astype(jnp.int32)
    column_ref[...] = jnp.broadcast_to(rows[:, 1:2], wide).astype(jnp.int32)
    lanes = lax.broadcasted_iota(jnp.int32, wide, 1) // RANK
    mask_ref[...] = jnp.where(lanes == jnp.broadcast_to(rows[:, 2:3], wide).astype(jnp.int32), 1.0, 0.0)
    last = jnp.concatenate([behind[:, length:], jnp.zeros((7, LANES), F32)], axis=0).T
    next_ref[...] = jnp.broadcast_to(last[:8, :1], (8, LANES)).astype(jnp.int32)
    zeros = jnp.zeros((5, SPAN), F32)
    for span in range(spans):
        here = row[:, span * SPAN : (span + 1) * SPAN]
        start = ids[:, LANES + span * SPAN - 1 : LANES + span * SPAN]
        end = here[:, SPAN - 1 :]
        keep = jnp.broadcast_to(jnp.where(start == end, 1.0, 0.0), here.shape)
        flags_ref[span] = jnp.concatenate(
            [jnp.where(here == start, 1.0, 0.0), jnp.where(here == end, 1.0, 0.0), keep, zeros], axis=0
        )


def token_tables(doc_ids, table):
    rows = doc_ids.shape[1]
    before = from_behind(doc_ids[:, rows - LANES :], SEQ, 1)
    after = from_behind(doc_ids[:, :LANES], SEQ, -1)
    shapes = [((rows, LANES), jnp.int32), ((8, LANES), jnp.int32), ((rows, LANES), jnp.int32), ((rows, LANES), F32)]
    shapes.append(((rows // SPAN, 8, SPAN), F32))
    valid, next_valid, column, mask, flags = pl.pallas_call(
        functools.partial(token_kernel, rows // SPAN),
        grid=(1,),
        in_specs=whole_specs(doc_ids, before, after) + [SMALL],
        out_specs=[whole(shape) for shape, _ in shapes],
        out_shape=[jax.ShapeDtypeStruct(*one) for one in shapes],
        compiler_params=PARAMS,
    )(doc_ids, before, after, table)
    row = jnp.broadcast_to(doc_ids, (8, rows))
    return Bag(valid=valid, next_valid=next_valid, column=column, row=row, flags=flags), mask


def state_hops(rows, block_rows):
    eighth = block_rows // DOCS_PER_BLOCK
    if rows // SPAN > 1 and eighth > SPAN:
        raise ValueError("unsupported block")
    return 1 if rows >= eighth else 2 * eighth // rows - 1


def pass_states(sizes, local, conv, tokens, hops, direction):
    if hops > 1:
        keep = jnp.exp2(conv.step[sizes.heads : 2 * sizes.heads, -1]) * tokens.flags[0, 2, 0]
        keep = jnp.repeat(keep, sizes.head)[:, None]
        total = local.astype(F32)
        reach = 1
        while reach < hops:
            total = total + keep * from_behind(total.astype(BF16), SEQ, direction * reach).astype(F32)
            keep = keep * from_behind(keep, SEQ, direction * reach)
            reach *= 2
        local = total.astype(BF16)
    return from_behind(local, SEQ, direction)


def layer_forward(sizes, inputs, level, lane_mask, tokens, hops):
    s = sizes
    normed, mixed, raw, rim = project_mixed(s, inputs, level, lane_mask)
    rim = from_behind(rim, SEQ, 1)
    yield mixed
    gate = None
    if level.gate_first:
        gate = project_gate(s, normed, level)
        rim = tie(rim, gate)
    (values, slope, maps, step), states = conv_forward(s, mixed, raw, rim, level, tokens)
    conv = Bag(values=values, slope=slope, maps=maps, step=step)
    states_in = [pass_states(s, states[-1], conv, tokens, hops, 1)] + list(states[:-1])
    yield values
    if gate is None:
        gate = project_gate(s, normed, level)
    outputs = None
    for span in reversed(range(s.spans)):
        outputs = scan_forward(s, span, conv, states_in[span], gate, level, tokens, outputs)
        if span == s.spans - 1:
            yield outputs[0]
    mixed_out, normed_out = outputs
    narrow_out, result = project_out(s, normed_out, inputs, level, lane_mask)
    yield result
    kept = Bag(
        inputs=inputs, normed=normed, gate=gate, conv=conv, states_in=states_in, mixed_out=mixed_out,
        normed_out=normed_out, narrow_out=narrow_out,
    )
    return result, kept


def layer_backward(sizes, upstream, kept, level, lane_mask, tokens, hops):
    s = sizes
    conv = kept.conv
    early_rows, late_rows = grad_rows(s, upstream.shape[1])
    all_rows = early_rows + late_rows
    grad_gate, turned, grad_narrow_out, *local = out_backward(
        s, upstream, kept.mixed_out, kept.gate, conv, level, lane_mask, tokens
    )
    grad_states = list(local[1:]) + [pass_states(s, local[0], conv, tokens, hops, -1)]
    buffer = early_grads(s, upstream, kept, grad_narrow_out, grad_gate, 0, None, all_rows)
    outputs = None
    for span in range(s.spans):
        outputs = scan_backward(
            s, span, conv, turned, kept.states_in[span], grad_states[span], level, tokens, outputs
        )
        if span == 0:
            later = from_behind(outputs[3], SEQ, -1)
            turned = yield outputs[0], turned
    grad_values, grad_maps, raw = outputs[:3]
    grad_values = yield grad_values, grad_values
    grad_mixed = conv_backward(s, grad_values, grad_maps, conv, later, level, tokens)
    part = gate_in_backward(s, grad_gate, level)
    grad_mixed = yield grad_mixed, grad_mixed
    narrow = narrow_backward(s, grad_mixed, raw, part, level, lane_mask)
    buffer = late_grads(s, kept, narrow, grad_mixed, raw, early_rows, buffer, all_rows)
    grad_mixed = yield buffer, grad_mixed
    return mixed_in_backward(s, grad_mixed, raw, part, kept.inputs, upstream, narrow, level)


def make_level(sizes, vector, numbers, adapters, where):
    s = sizes
    in_down, in_up, out_down, out_up = adapters
    dt_bias, a_log, skip_gain = numbers
    rate = -jnp.exp(a_log)[:, None]
    lane = jnp.arange(LANES)[None, :]
    table = jnp.where(lane == 1, skip_gain[:, None], jnp.where(lane == 2, dt_bias[:, None], rate))
    table = jnp.where(lane == 0, rate * LOG2E, table)
    return Bag(
        vector=vector, heads=table, in_down=in_down, in_up=in_up, out_down=out_down,
        out_up=out_up, where=where, mixed_where=where,
    )


def swap(value):
    return lax.ppermute(value, SECTION, [(0, 1), (1, 0)])


def exchange(value, axis, distance):
    count = lax.axis_size(axis)
    return lax.ppermute(value, axis, [(place, place ^ distance) for place in range(count)])


def rows_at(value, index, rows):
    return lax.dynamic_slice_in_dim(value, index * rows, rows, axis=0)


def put_at(buffer, value, *index):
    start = list(index) + [0] * (buffer.ndim - len(index))
    return lax.dynamic_update_slice(buffer, value.reshape((1,) * len(index) + value.shape), start)


def across(value, second):
    count = lax.axis_size(WSHARD)
    pairs = []
    for section in range(2):
        distance = 2 - section if second else 1 + section
        pairs += [(section * count + place, section * count + (place ^ distance)) for place in range(count)]
    return lax.ppermute(value, (SECTION, WSHARD), pairs)


class Parts:
    def __init__(self, quarters):
        self.section = lax.axis_index(SECTION)
        self.quarters, self.near, self.parts = quarters, {}, {}
        other = swap(quarters[0][0])
        self.own = [jnp.where(self.section == 0, quarters[0][0], other)]
        others = [other] + [swap(tie(matrix, self.own[0])) for matrix, _, _ in quarters[1:]]
        self.later = others[1]
        for layer in range(2):
            for (matrix, _, _), other in list(zip(quarters, others, strict=True))[1 - layer :]:
                self.own.append(jnp.where(self.section == layer, matrix, other))

    def start(self, index, *after):
        self.near[index] = across(tie(self.own[index], *after), False)

    def forward(self, index, *after):
        _, half, step = self.quarters[index % len(self.quarters)]
        near = tie(self.near[index], *after)
        apart = across(lax.dynamic_slice_in_dim(near, self.section * step, half, axis=0), True)
        self.halfway = (self.own[index], near, swap(near), apart)
        return apart

    def finish(self, index, *after):
        self.parts[index] = self.halfway + (swap(tie(self.halfway[3], *after)),)


def scatter_start(value, axis):
    count, place = lax.axis_size(axis), lax.axis_index(axis)
    rows = value.shape[0] // count
    sent = [exchange(rows_at(value, place ^ away, rows), axis, away) for away in range(1, count)]
    return rows_at(value, place, rows), sent


def scatter_done(parts, *after):
    own, received = parts
    total = own.astype(F32)
    for part in tie(received, *after):
        total = total + part.astype(F32)
    return total.astype(BF16)


def gather_start(value, axis):
    return value, [exchange(value, axis, away) for away in range(1, lax.axis_size(axis))]


def gather_done(parts, axis, *after):
    own, received = parts
    count, place = lax.axis_size(axis), lax.axis_index(axis)
    buffer = jnp.zeros((count,) + own.shape, own.dtype)
    for away, part in enumerate([own] + tie(received, *after)):
        buffer = put_at(buffer, part, place ^ away)
    return buffer.reshape((count * own.shape[0],) + own.shape[1:])


def chip_start(packed):
    section = lax.axis_index(SECTION)
    half = packed.shape[0] // 2
    return rows_at(packed, section, half), [swap(rows_at(packed, 1 - section, half))]


def both_layers(own):
    section = lax.axis_index(SECTION)
    other = swap(own)
    return [jnp.where(section == layer, own, other) for layer in range(2)]


def on_device(
    layer_input, out_grad, doc_index, doc_adapter, in_weight, out_weight, norm_gain, conv_weight, conv_bias, dt_bias,
    a_log, skip_gain, gate_gain, *adapters,
):
    section, place = lax.axis_index(SECTION), lax.axis_index(WSHARD)
    batches, rows, width = layer_input.shape
    heads, inner = dt_bias.shape[1], gate_gain.shape[1]
    taps, mixed = conv_weight.shape[1:]
    sizes = Sizes(rows, inner, heads, (mixed - inner) // 2, in_weight.shape[1], taps)
    block_rows = rows * lax.axis_size(SEQ)
    hops = state_hops(rows, block_rows)

    pick = lambda array: lax.dynamic_index_in_dim(array, section, 0, keepdims=False)
    turned = in_weight[0].T
    main = mixed // 2
    weights = Parts(
        [
            (turned[inner:], main + heads, main),
            (turned[:inner], inner // 2, inner // 2),
            (out_weight[0], out_weight.shape[1] // 2, out_weight.shape[1] // 2),
        ]
    )
    weights.start(0)
    weights.start(1, weights.forward(0))
    weights.finish(0)
    rest = (layer_input, out_grad, doc_index, doc_adapter, norm_gain, conv_weight, conv_bias, dt_bias, a_log, skip_gain)
    rest, gate_gain, adapters = tie((rest, gate_gain, adapters), weights.later)
    layer_input, out_grad, doc_index, doc_adapter, norm_gain, conv_weight, conv_bias, dt_bias, a_log, skip_gain = rest
    inputs, grads, doc_ids, table = pick(layer_input), pick(out_grad), pick(doc_index), pick(doc_adapter)[0]
    tokens, lane_mask = token_tables(doc_ids[None, :], table)
    vectors = both_layers(jnp.concatenate([conv_weight[0].reshape(1, -1), conv_bias, gate_gain, norm_gain], axis=1))
    numbers = both_layers(jnp.concatenate([dt_bias, a_log, skip_gain], axis=0))
    in_down, in_up, out_down, out_up = adapters
    both = [both_layers(array) for array in (in_down[0], in_up[0].T, out_down[0], out_up[0])]
    where = jnp.stack([place, place ^ (1 + section), place ^ (2 - section), place ^ 3, section]).astype(jnp.int32)
    levels = [
        make_level(sizes, vectors[layer], numbers[layer], [pair[layer] for pair in both], where)
        for layer in range(2)
    ]
    small = [inputs, grads, lane_mask, tokens.__dict__, weights.own[1:]] + [level.__dict__ for level in levels]
    small, weights.parts[0] = lax.optimization_barrier((small, weights.parts[0]))
    inputs, grads, lane_mask, token_fields, weights.own[1:], *level_fields = small
    tokens, levels = Bag(**token_fields), [Bag(**fields) for fields in level_fields]
    levels[0].mixed = weights.parts[0]
    levels[0].gate_first = levels[1].gate_first = False

    passes = {(0, 0): 1, (0, 1): 2, (0, 2): 3, (0, 4): 4, (1, 1): 5}
    ends = {(0, 1): 1, (0, 2): 2, (0, 3): 3, (1, 0): 4, (1, 2): 5}
    results, kept = [], []
    rows_now = inputs
    for layer in range(2):
        stages = layer_forward(sizes, rows_now, levels[layer], lane_mask, tokens, hops)
        for stage in range(5):
            try:
                token = next(stages)
            except StopIteration as end:
                rows_now, stored = end.value
            move = ends.get((layer, stage))
            if move is not None:
                weights.finish(move, token)
                owner, parts = levels[move // 3], weights.parts[move]
                if move % 3 == 0:
                    owner.mixed = parts
                elif move % 3 == 1:
                    owner.gate = parts
                else:
                    owner.out = parts
            move = passes.get((layer, stage))
            if move is not None:
                weights.forward(move, token)
                if move < 5:
                    weights.start(move + 1, token)
        results.append(rows_now)
        kept.append(stored)

    def placed(pair):
        here = jnp.where(section == 0, pair[0], pair[1])
        there = swap(jnp.where(section == 0, pair[1], pair[0]))
        first, second = jnp.where(section == 0, here, there), jnp.where(section == 0, there, here)
        return jnp.stack([first, second])[None]

    direct = lax.axis_size(SEQ) == 4
    both_axes = (WSHARD, SEQ)

    def finish(stages, value):
        try:
            stages.send(value)
        except StopIteration as end:
            return end.value

    stages = layer_backward(sizes, tie(grads, rows_now), kept[1], levels[1], lane_mask, tokens, hops)
    _, pending = next(stages)
    for _ in range(2):
        _, pending = stages.send(pending)
    upper, pending = stages.send(pending)
    upper = chip_start(upper)
    upper_grad = finish(stages, pending)
    upper = scatter_done(upper, upper_grad)
    upper_grad = tie(upper_grad, upper)
    upper = scatter_start(upper, WSHARD) if direct else lax.psum(upper, both_axes)

    stages = layer_backward(sizes, upper_grad, kept[0], levels[0], lane_mask, tokens, hops)
    token, pending = next(stages)
    if direct:
        upper = scatter_start(scatter_done(upper, token), SEQ)
    token, pending = stages.send(tie(pending, upper[0]))
    if direct:
        upper = gather_start(scatter_done(upper, token), SEQ)
    token, pending = stages.send(tie(pending, upper[0]))
    if direct:
        upper = gather_start(gather_done(upper, SEQ, token), WSHARD)
    lower, pending = stages.send(tie(pending, upper[0]))
    lower = chip_start(lower)
    if direct:
        upper = gather_done(upper, WSHARD, lower[0])
    lower = scatter_done(lower, upper)
    if direct:
        lower = scatter_start(lower, WSHARD)
    lower_grad = finish(stages, tie(pending, lower[0]))
    outputs = (placed(results), placed([lower_grad, upper_grad]))
    if direct:
        lower = scatter_start(scatter_done(lower, lower_grad), SEQ)
        lower = gather_start(scatter_done(lower), SEQ)
        lower = gather_start(gather_done(lower, SEQ), WSHARD)
        lower = gather_done(lower, WSHARD, outputs)
    else:
        lower = lax.psum(lower, both_axes)
    sums = final_sums(sizes, width, section, upper, swap(upper), lower, swap(lower))
    down_in, in_up, down_out, out_up = sums
    return (
        *outputs, down_in[None], in_up.T[None], down_out[None], out_up[None],
    )


def solution(mesh):
    tokens, matrix, vector = P(None, (WSHARD, SEQ), None), P(SECTION, None, None), P(SECTION, None)
    in_specs = (tokens, tokens, P(None, (WSHARD, SEQ)), P(None, WSHARD, None))
    in_specs += (P(SECTION, WSHARD, None),) * 2
    in_specs += (vector, matrix) + (vector,) * 5 + (matrix,) * 4
    out_specs = (P(SECTION, None, (WSHARD, SEQ), None),) * 2 + (matrix,) * 4
    return jax.shard_map(on_device, mesh=mesh, in_specs=in_specs, out_specs=out_specs, check_vma=False)
```

```python
import functools

import jax
import jax.numpy as jnp
from jax import lax
from jax.experimental import pallas as pl
from jax.experimental.pallas import tpu as pltpu
from jax.sharding import PartitionSpec as P

SPAN = 256
RANK = 16
LANES = 128
DOCS_PER_BLOCK = 8
EPSILON = 1e-05
LOG2E = 1.4426950408889634
EXACT = lax.Precision.HIGHEST
SEQ, WSHARD, SECTION = "seq", "wshard", "section"
BF16 = jnp.bfloat16
F32 = jnp.float32
PARAMS = pltpu.CompilerParams(vmem_limit_bytes=20 * 1024 * 1024)


class Bag:
    def __init__(self, **fields):
        self.__dict__.update(fields)


def tie(value, *others):
    return lax.optimization_barrier((value, *others))[0]


def from_behind(value, axis, steps):
    count = lax.axis_size(axis)
    initial, last = (max(0, -steps), min(count, count - steps))
    return lax.ppermute(value, axis, [(source, source + steps) for source in range(initial, last)])


def dot(left, right):
    return jnp.dot(left, right, preferred_element_type=F32)


def dot_last(left, right):
    return lax.dot_general(left, right, (((1,), (1,)), ((), ())), preferred_element_type=F32)


def dot_first(left, right):
    return lax.dot_general(left, right, (((0,), (0,)), ((), ())), preferred_element_type=F32)


def rms_rate(values):
    return lax.rsqrt(jnp.mean(values * values, axis=-1, keepdims=True) + EPSILON)


def sigmoid(v):
    return 0.5 + 0.5 * jnp.tanh(0.5 * v)


def lower_ones(shape):
    rows = lax.broadcasted_iota(jnp.int32, shape, 0)
    columns = lax.broadcasted_iota(jnp.int32, shape, 1)
    return rows <= columns


def conv_rows(rows, rim, weight, offset, valid):
    length = rows.shape[0]
    valid = jnp.concatenate([valid] * (rows.shape[1] // LANES), axis=1)
    extended = jnp.concatenate([rim, rows], axis=0)
    taps = weight.shape[0]
    total = offset + weight[taps - 1 : taps] * rows
    for back in range(1, taps):
        shifted = extended[8 - back : 8 - back + length]
        total = total + jnp.where(valid >= back, shifted, 0.0) * weight[taps - 1 - back : taps - back]
    gate = sigmoid(total)
    active = total * gate
    return active, gate + active * (1.0 - gate)


def taps_at(vector_ref, places, first, width):
    rows = [vector_ref[:, pl.ds(pl.multiple_of(place + first, LANES), width)] for place in places]
    return jnp.concatenate(rows[:-1], axis=0), rows[-1]


def conv_kernel(
    spans, head, heads, state, places,
    mixed_ref, mixed_bc_ref, rim_ref, rim_bc_ref, vector_ref, valid_ref, raw_ref, head_ref, token_ref,
    values_ref, slope_ref, bc_ref, step_ref, *rest,
):
    state_refs, tail_ref = rest[:-1], rest[-1]
    group = pl.program_id(0)
    valid = valid_ref[...]
    width = mixed_ref.shape[1]
    heads_here = width // head

    @pl.when(group == 0)
    def _():
        weight, offset = taps_at(vector_ref, places, pl.num_programs(0) * width, 2 * state)
        active, slope = conv_rows(
            mixed_bc_ref[...].astype(F32), rim_bc_ref[...].astype(F32), weight, offset, valid
        )
        bc_ref[...] = jnp.concatenate([active, slope], axis=1).astype(BF16)
        raw = raw_ref[...].astype(F32).T[:heads] + head_ref[:, 2:3]
        step = (jnp.maximum(raw, 0.0) + jnp.log1p(jnp.exp(-jnp.abs(raw)))).astype(BF16).astype(F32)
        step_ref[:heads, :] = step
        step_ref[2 * heads :, :] = sigmoid(raw)
        drop = step * head_ref[:, :1]
        ones = lower_ones((SPAN, SPAN)).astype(F32)
        for span in range(spans):
            here = slice(span * SPAN, (span + 1) * SPAN)
            decay = jnp.dot(drop[:, here], ones, precision=EXACT, preferred_element_type=F32)
            step_ref[heads : 2 * heads, here] = decay
            tail = jnp.exp2(decay[:, SPAN - 1 :] - decay) * token_ref[span][1:2]
            tail_ref[:, here] = tail * step[:, here]

    weight, offset = taps_at(vector_ref, places, group * width, width)
    active, slope = conv_rows(
        mixed_ref[...].astype(F32), rim_ref[...].astype(F32), weight, offset, valid
    )
    slope_ref[...] = slope.astype(BF16)
    low = active.T.astype(BF16)
    values_ref[...] = low
    low = low.astype(F32)
    first = pl.multiple_of(group * heads_here, heads_here)
    tail_rows = tail_ref[pl.ds(first, heads_here), :]
    for span in range(spans):
        here = slice(span * SPAN, (span + 1) * SPAN)
        driven = jnp.concatenate(
            [
                (low[place * head : (place + 1) * head, here] * tail_rows[place : place + 1, here]).astype(BF16)
                for place in range(heads_here)
            ],
            axis=0,
        )
        state_refs[span][...] = dot(driven, bc_ref[here, :state]).astype(BF16)


def faded(row, column, score_ref):
    half = SPAN // 2
    upper = jnp.exp2(jnp.minimum(row - column[:half], 0.0))
    lower = jnp.exp2(jnp.minimum(row[:, half:] - column[half:], 0.0))
    lower = jnp.concatenate([jnp.zeros_like(lower), lower], axis=1)
    return (upper, lower), (upper * score_ref[:half, :], lower * score_ref[half:, :])


def scan_kernel(
    head, state, gain,
    values_ref, bc_ref, step_ref, decay_ref, token_ref, doc_column_ref, doc_row_ref, state_ref, head_ref, gate_ref,
    vector_ref, *rest,
):
    mixed_ref, normed_ref, score_ref, scanned_ref = rest[-4:]
    group, groups = pl.program_id(0), pl.num_programs(0)
    width = values_ref.shape[0]
    heads_here = width // head

    @pl.when(group == 0)
    def _():
        score = dot_last(bc_ref[:, :state], bc_ref[:, state:])
        same = (jnp.concatenate([doc_column_ref[...]] * (SPAN // LANES), axis=1) == doc_row_ref[:1]) & lower_ones((SPAN, SPAN))
        score_ref[...] = jnp.where(same, score, 0.0)

    decay, step = decay_ref[...], step_ref[...]
    carry = jnp.exp2(decay) * token_ref[0][:1]
    columns = jnp.concatenate([decay] * (LANES // heads_here), axis=0).T
    out_map = bc_ref[:, state:]
    parts = []
    for place in range(heads_here):
        rows = slice(place * head, (place + 1) * head)
        one = slice(place, place + 1)
        kernel = jnp.concatenate([part.astype(BF16) for part in faded(decay[one], columns[:, one], score_ref)[1]], axis=0)
        values = values_ref[rows].astype(F32)
        driven = (values * step[one]).astype(BF16)
        before = dot_last(state_ref[rows], out_map) * carry[one]
        parts.append(dot(driven, kernel) + before + head_ref[one, 1:2] * values)
    low = jnp.concatenate(parts, axis=0).astype(BF16).T
    mixed_ref[...] = low
    scanned_ref[:, pl.ds(pl.multiple_of(group * width, width), width)] = low

    @pl.when(group == groups - 1)
    def _():
        def rows_at(index, _):
            rows = pl.ds(pl.multiple_of(index * 16, 16), 16)
            mixed = scanned_ref[rows, :]
            gate = gate_ref[rows, :].astype(F32)
            gated = mixed.astype(F32) * (gate * sigmoid(gate))
            normed_ref[rows, :] = (gated * rms_rate(gated) * vector_ref[:, gain : gain + gated.shape[1]]).astype(BF16)
            return 0

        lax.fori_loop(0, SPAN // 16, rows_at, 0, unroll=4)


def out_back_kernel(
    head, heads, state, gain, count,
    up_ref, lane_ref, up_out_ref, down_out_ref, mixed_ref, gate_ref, vector_ref, decay_ref, token_ref, bc_ref, where_ref,
    *rest,
):
    parts, rest = rest[:count], rest[count:]
    (project_ref, turned_ref, narrow_ref), state_refs, (grad_ref, grad_mixed_ref) = rest[:3], rest[3:-2], rest[-2:]
    width = mixed_ref.shape[1]
    up = up_ref[...]
    narrow = (dot_last(up, up_out_ref[...]) * lane_ref[...]).astype(BF16)
    narrow_ref[...] = narrow
    left = jnp.concatenate([up, narrow], axis=1)
    for offset, part in out_places(where_ref, parts):
        here = pl.ds(offset, part.shape[0])
        grad_ref[:, here] = dot_last(left, jnp.concatenate([part[...], down_out_ref[here, :]], axis=1))

    def rows_at(index, _):
        rows = pl.ds(pl.multiple_of(index * 16, 16), 16)
        mixed = mixed_ref[rows, :].astype(F32)
        gate = gate_ref[rows, :].astype(F32)
        share = sigmoid(gate)
        silu = gate * share
        gated = mixed * silu
        grad = grad_ref[rows, :] * vector_ref[:, gain : gain + width]
        rate = rms_rate(gated)
        pull = jnp.mean(gated * grad, axis=-1, keepdims=True) * rate * rate * rate
        grad_gated = rate * grad - gated * pull
        project_ref[rows, :] = (grad_gated * mixed * (share + silu * (1.0 - share))).astype(BF16)
        grad_mixed_ref[rows, :] = (grad_gated * silu).astype(BF16)
        return 0

    lax.fori_loop(0, SPAN // 16, rows_at, 0, unroll=4)
    carry = jnp.exp2(decay_ref[...]) * token_ref[0][:1]
    out_map = bc_ref[:, state:]
    wide = 512
    for first in range(0, width, wide):
        low = grad_mixed_ref[:, first : first + wide].astype(F32).T
        turned_ref[first : first + wide, :] = low.astype(BF16)
        scaled = [
            (low[place * head : (place + 1) * head] * carry[first // head + place : first // head + place + 1]).astype(BF16)
            for place in range(wide // head)
        ]
        local = dot(jnp.concatenate(scaled, axis=0), out_map).astype(BF16)
        for span, state_ref in enumerate(state_refs):

            @pl.when(pl.program_id(0) == span)
            def _(state_ref=state_ref, first=first, local=local):
                state_ref[first : first + wide, :] = local


def aligned(value, unit):
    return pl.multiple_of(value * unit, unit)


def out_places(where_ref, parts):
    if len(parts) == 1:
        half = parts[0].shape[1]
        return [((2 * place + side) * half, parts[0].at[4 * side + place]) for place in range(4) for side in range(2)]
    rows, half = parts[0].shape[0], parts[3].shape[0]
    places = [(aligned(where_ref[place], rows), part) for place, part in enumerate(parts[:3])]
    apart = where_ref[3] * 2
    places.append((aligned(apart + where_ref[4], half), parts[3]))
    places.append((aligned(apart + 1 - where_ref[4], half), parts[4]))
    return places


def in_rows(where_ref, parts, step, start, size):
    side = int(start >= step)
    there = slice(start - side * step, start - side * step + size)
    if len(parts) == 1:
        return [parts[0][4 * side + place, there, :] for place in range(4)]
    pair = (parts[3][there], parts[4][there])
    apart = jnp.where(where_ref[4] == 0, pair[side], pair[1 - side])
    return [part[start : start + size] for part in parts[:3]] + [apart]


def in_columns(ref, where_ref, parts):
    columns = (ref.shape[1] - LANES) // parts
    places = [pl.ds(aligned(where_ref[place], columns), columns) for place in range(parts)]
    return jnp.concatenate([ref[:, here] for here in places + [pl.ds(parts * columns, LANES)]], axis=1)


def mixed_kernel(
    main, lanes, gain, count, input_ref, vector_ref, down_ref, lane_ref, up_ref, where_ref, *rest
):
    parts, (normed_ref, mixed_ref, raw_ref, rim_ref) = rest[:count], rest[count:]
    rows = input_ref.shape[0]
    inputs = input_ref[...].astype(F32)
    normed = (inputs * rms_rate(inputs) * vector_ref[:, gain : gain + inputs.shape[1]]).astype(BF16)
    narrow = (dot(normed, down_ref[...]) * lane_ref[...]).astype(BF16)
    normed_ref[...] = jnp.concatenate([normed, narrow], axis=1)
    left = in_columns(normed_ref, where_ref, 4)
    step, extra = main // 6, raw_ref.shape[1] // 4
    before = up_ref.shape[0] - main - extra

    def product(start, size):
        right = in_rows(where_ref, parts, main // 2, start, size)
        right.append(up_ref[before + start : before + start + size])
        return dot_last(left, jnp.concatenate(right, axis=1))

    for start in range(0, main, step):
        low = product(start, step).astype(BF16)
        mixed_ref[:, start : start + step] = low
        rim_ref[:, start : start + step] = low[rows - 8 :]
    raw_ref[...] = jnp.concatenate([product(main, extra), jnp.zeros((rows, lanes - extra), F32)], axis=1).astype(BF16)


def gate_kernel(count, normed_ref, up_ref, where_ref, *rest):
    parts, gate_ref = rest[:count], rest[count]
    left = in_columns(normed_ref, where_ref, 4)
    wide = 512
    inner = gate_ref.shape[1]
    for start in range(0, inner, wide):
        right = in_rows(where_ref, parts, inner // 2, start, wide) + [up_ref[start : start + wide]]
        gate_ref[:, start : start + wide] = dot_last(left, jnp.concatenate(right, axis=1)).astype(BF16)


def out_kernel(count, normed_ref, input_ref, down_ref, lane_ref, up_ref, where_ref, *rest):
    parts, (narrow_ref, out_ref) = rest[:count], rest[count:]
    narrow = (dot(normed_ref[...], down_ref[...]) * lane_ref[...]).astype(BF16)
    narrow_ref[...] = narrow
    places = out_places(where_ref, parts)
    left = [normed_ref[:, pl.ds(offset, part.shape[0])] for offset, part in places]
    left = jnp.concatenate(left + [narrow], axis=1)
    wide = 256
    for start in range(0, out_ref.shape[1], wide):
        here = slice(start, start + wide)
        right = jnp.concatenate([part[:, here] for _, part in places] + [up_ref[:, here]], axis=0)
        out_ref[:, here] = (input_ref[:, here].astype(F32) + dot(left, right)).astype(BF16)


def gate_in_back_kernel(count, grad_ref, where_ref, *rest):
    parts, out_ref = rest[:count], rest[count]
    grad = grad_ref[...]
    half = grad.shape[1] // 2
    lower, upper = [in_rows(where_ref, parts, half, side * half, half) for side in range(2)]
    columns = lower[0].shape[1]
    for place in range(4):
        product = dot(grad[:, :half], lower[place]) + dot(grad[:, half:], upper[place])
        out_ref[:, place * columns : (place + 1) * columns] = product


def narrow_back_kernel(extra, grad_gate_ref, grad_ref, raw_ref, lane_ref, up_ref, narrow_ref):
    left = jnp.concatenate([grad_gate_ref[...], grad_ref[...], raw_ref[...][:, :extra]], axis=1)
    narrow_ref[...] = (dot(left, up_ref[...]) * lane_ref[...]).astype(BF16)


def mixed_in_back_kernel(
    main, extra, gain, count,
    grad_ref, raw_ref, part_ref, input_ref, up_stream_ref, vector_ref, narrow_ref, down_ref, where_ref, *rest
):
    parts, (out_ref, total_ref) = rest[:count], rest[count:]
    width = input_ref.shape[1]
    columns = width // 4
    half = main // 2
    left = jnp.concatenate([grad_ref[...], raw_ref[...][:, :extra]], axis=1)
    lower = in_rows(where_ref, parts, half, 0, half)
    upper = in_rows(where_ref, parts, half, half, half + extra)
    for place in range(4):
        product = dot(left[:, :half], lower[place]) + dot(left[:, half:], upper[place])
        here = slice(place * columns, (place + 1) * columns)
        total_ref[:, pl.ds(aligned(where_ref[place], columns), columns)] = part_ref[:, here] + product
    scaled = (total_ref[...] + dot_last(narrow_ref[...], down_ref[...])) * vector_ref[:, gain : gain + width]
    inputs = input_ref[...].astype(F32)
    rate = rms_rate(inputs)
    pull = jnp.mean(inputs * scaled, axis=-1, keepdims=True) * rate * rate * rate
    out_ref[...] = (up_stream_ref[...].astype(F32) + rate * scaled - inputs * pull).astype(BF16)


def scan_back_kernel(
    head, heads, state, edge,
    values_ref, grad_ref, bc_ref, step_ref, decay_ref, sig_ref, token_ref, doc_column_ref, doc_row_ref, state_ref,
    grad_state_ref, head_ref, rate_ref, slope_ref, slope_bc_ref, *rest,
):
    outputs = rest[:-6]
    if edge:
        outputs, edge_ref = outputs[:-1], outputs[-1]
    out_values_ref, out_bc_ref, out_raw_ref = outputs[-3:]
    score_ref, grad_score_ref, pull_ref, direct_ref, grad_in_ref, grad_out_ref = rest[-6:]
    group, groups = pl.program_id(0), pl.num_programs(0)
    width = values_ref.shape[0]
    heads_here = width // head
    in_map, out_map = bc_ref[:, :state], bc_ref[:, state:]

    def same_doc():
        return (jnp.concatenate([doc_column_ref[...]] * (SPAN // LANES), axis=1) == doc_row_ref[:1]) & lower_ones((SPAN, SPAN))

    @pl.when(group == 0)
    def _():
        score_ref[...] = jnp.where(same_doc(), dot_last(in_map, out_map), 0.0)
        grad_score_ref[...] = jnp.zeros_like(grad_score_ref)
        grad_in_ref[...] = jnp.zeros_like(grad_in_ref)
        grad_out_ref[...] = jnp.zeros_like(grad_out_ref)

    decay, step = decay_ref[...], step_ref[...]
    token = token_ref[0]
    last = decay[:, SPAN - 1 :]
    carry = jnp.exp2(decay) * token[:1]
    tail = jnp.exp2(last - decay) * token[1:2]
    keep = jnp.exp2(last) * token[2:3, :1]
    columns = jnp.concatenate([decay] * (LANES // heads_here), axis=0).T
    at_end = lax.broadcasted_iota(jnp.int32, (1, SPAN), 1) == SPAN - 1
    grads, tails, carried, pulls, directs = [], [], [], [], []
    for place in range(heads_here):
        rows = slice(place * head, (place + 1) * head)
        one = slice(place, place + 1)
        fade, kernel = faded(decay[one], columns[:, one], score_ref)
        kernel = jnp.concatenate([part.astype(BF16) for part in kernel], axis=0)
        values = values_ref[rows].astype(F32)
        driven = (values * step[one]).astype(BF16)
        grad_low = grad_ref[rows]
        grad = grad_low.astype(F32)
        grad_kernel = dot_first(driven, grad_low)
        half = SPAN // 2
        grad_score_ref[:half, :] += grad_kernel[:half] * fade[0]
        grad_score_ref[half:, half:] += grad_kernel[half:, half:] * fade[1][:, half:]
        state_here, grad_state = state_ref[rows], grad_state_ref[rows]
        output = dot(driven, kernel) + dot_last(state_here, out_map) * carry[one]
        by_state = dot_last(grad_state, in_map) * tail[one]
        grad_driven = dot_last(grad_low, kernel) + by_state
        driven = driven.astype(F32)
        pull = jnp.sum(grad * output - driven * grad_driven, axis=0, keepdims=True)
        ending = jnp.sum(jnp.sum(driven * by_state, axis=0, keepdims=True), axis=1, keepdims=True)
        kept = jnp.sum(state_here.astype(F32) * grad_state.astype(F32), axis=0, keepdims=True)
        ending = ending + keep[one] * jnp.sum(kept, axis=1, keepdims=True)
        pulls.append(pull + jnp.where(at_end, ending, 0.0))
        directs.append(jnp.sum(values * grad_driven, axis=0, keepdims=True))
        grads.append(step[one] * grad_driven + head_ref[one, 1:2] * grad)
        tails.append((driven * tail[one]).astype(BF16))
        carried.append((grad * carry[one]).astype(BF16))
    grad_in_ref[...] += dot_first(jnp.concatenate(tails, axis=0), grad_state_ref[...])
    grad_out_ref[...] += dot_first(jnp.concatenate(carried, axis=0), state_ref[...])
    grads = jnp.concatenate(grads, axis=0).T.astype(BF16)
    out_values_ref[...] = grads
    if edge:
        product = grads[:8].astype(F32) * slope_ref[...][:8].astype(F32)
        edge_ref[:, pl.ds(pl.multiple_of(group * width, width), width)] = product.astype(BF16)
    here = pl.ds(pl.multiple_of(group * heads_here, heads_here), heads_here)
    pull_ref[here, :] = jnp.concatenate(pulls, axis=0)
    direct_ref[here, :] = jnp.concatenate(directs, axis=0)

    @pl.when(group == groups - 1)
    def _():
        ones = lower_ones((SPAN, SPAN)).astype(F32)
        summed = lax.dot_general(
            pull_ref[...], ones, (((1,), (1,)), ((), ())), precision=EXACT, preferred_element_type=F32
        )
        grad_step = (direct_ref[...] + rate_ref[:, 3:4] * summed).astype(BF16).astype(F32)
        grad_raw = grad_step * sig_ref[...]
        padded = jnp.concatenate([grad_raw, jnp.zeros((LANES - heads, SPAN), F32)], axis=0)
        out_raw_ref[...] = padded.T.astype(BF16)
        grad_score = jnp.where(same_doc(), grad_score_ref[...], 0.0).astype(BF16)
        grad_in = grad_in_ref[...] + dot(grad_score, out_map)
        grad_out = grad_out_ref[...] + dot_first(grad_score, in_map)
        low = jnp.concatenate([grad_in, grad_out], axis=1).astype(BF16)
        out_bc_ref[...] = low
        if edge:
            product = low[:8].astype(F32) * slope_bc_ref[...][:8].astype(F32)
            edge_ref[:, groups * width :] = product.astype(BF16)


def conv_back_kernel(
    value_blocks, places,
    grad_ref, grad_bc_ref, slope_ref, slope_bc_ref, next_ref, vector_ref, valid_ref, next_valid_ref, project_ref,
):
    block = pl.program_id(0)
    length = grad_ref.shape[0]

    def back(grad_low, slope_low):
        grad = grad_low.astype(F32) * slope_low.astype(F32)
        later = next_ref[...].astype(F32)
        weight, _ = taps_at(vector_ref, places, block * grad.shape[1], grad.shape[1])
        valid, next_valid = [jnp.concatenate([ref[...]] * (grad.shape[1] // LANES), axis=1) for ref in (valid_ref, next_valid_ref)]
        taps = weight.shape[0]
        total = weight[taps - 1 : taps] * grad
        for ahead in range(1, taps):
            extended = jnp.concatenate(
                [jnp.where(valid >= ahead, grad, 0.0), jnp.where(next_valid >= ahead, later, 0.0)], axis=0
            )
            total = total + weight[taps - 1 - ahead : taps - ahead] * extended[ahead : ahead + length]
        project_ref[...] = total.astype(BF16)

    @pl.when(block < value_blocks)
    def _():
        back(grad_ref[...], slope_ref[...])

    @pl.when(block == value_blocks)
    def _():
        back(grad_bc_ref[...], slope_bc_ref[...])


def spec(shape, index):
    return pl.BlockSpec(shape, index)


def whole(shape):
    return pl.BlockSpec(shape, lambda *_: (0,) * len(shape))


def cost(microseconds):
    return pl.CostEstimate(flops=int(microseconds * 3.45e+09), bytes_accessed=1 << 16, transcendentals=0)


class Sizes:
    def __init__(self, rows, inner, heads, state, columns, taps):
        self.rows, self.inner, self.heads, self.state, self.columns, self.taps = rows, inner, heads, state, columns, taps
        self.head = inner // heads
        self.spans = rows // SPAN
        self.mixed = inner + 2 * state
        self.group_heads = 8
        self.groups = heads // self.group_heads
        self.wide = self.group_heads * self.head
        self.places = tuple(tap * self.mixed for tap in range(taps + 1))
        self.gate_gain = (taps + 1) * self.mixed
        self.norm_gain = self.gate_gain + inner


def conv_forward(sizes, mixed, raw, rim, level, tokens):
    s = sizes
    rows, wide, heads, state = s.rows, s.wide, s.heads, s.state
    maps = s.inner // (2 * state)
    shapes = [(s.inner, rows), (rows, s.inner), (rows, 4 * state)]
    args = [level.vector, tokens.valid, raw, level.heads, tokens.flags]
    outputs = pl.pallas_call(
        functools.partial(conv_kernel, s.spans, s.head, heads, state, s.places),
        grid=(s.groups,),
        in_specs=[
            spec((rows, wide), lambda g: (0, g)), spec((rows, 2 * state), lambda g: (0, maps)),
            spec((8, wide), lambda g: (0, g)), spec((8, 2 * state), lambda g: (0, maps)), *whole_specs(*args),
        ],
        out_specs=[
            spec((wide, rows), lambda g: (g, 0)), spec((rows, wide), lambda g: (0, g)), whole(shapes[2]),
            whole((3 * heads, rows)),
        ] + [spec((wide, state), lambda g: (g, 0))] * s.spans,
        out_shape=[shape_of(shapes[0]), far_shape(shapes[1]), shape_of(shapes[2]), shape_of((3 * heads, rows), F32)]
        + [shape_of((s.inner, state))] * s.spans,
        scratch_shapes=[pltpu.VMEM((heads, rows), F32)],
        compiler_params=PARAMS,
        cost_estimate=cost(8.5),
    )(mixed, mixed, rim, rim, *args)
    return outputs[:4], outputs[4:]


def span_specs(sizes, span):
    s = sizes
    return Bag(
        turned=spec((s.wide, SPAN), lambda g: (g, span)),
        maps=spec((SPAN, 2 * s.state), lambda g: (span, 0)),
        rows=spec((s.group_heads, SPAN), lambda g: (g, span)),
        decay=spec((s.group_heads, SPAN), lambda g: (s.groups + g, span)),
        flags=spec((1, 8, SPAN), lambda g: (span, 0, 0)),
        doc_column=spec((SPAN, LANES), lambda g: (span, 0)),
        doc_row=spec((8, SPAN), lambda g: (0, span)),
        state=spec((s.wide, s.state), lambda g: (g, 0)),
        head=spec((s.group_heads, LANES), lambda g: (g, 0)),
        full=spec((SPAN, s.inner), lambda g: (span, 0)),
    )


ANYWHERE = pl.BlockSpec(memory_space=pl.ANY)


def scan_forward(sizes, span, conv, state_in, gate, level, tokens, earlier):
    s = sizes
    at = span_specs(s, span)
    args = [
        conv.values, conv.maps, conv.step, conv.step, tokens.flags, tokens.column, tokens.row, state_in, level.heads,
        gate, level.vector,
    ]
    in_specs = [
        at.turned, at.maps, at.rows, at.decay, at.flags, at.doc_column, at.doc_row, at.state,
        at.head, at.full, whole(level.vector.shape),
    ]
    aliases = {}
    if earlier is not None:
        aliases = {len(args): 0, len(args) + 1: 1}
        args, in_specs = args + list(earlier), in_specs + [ANYWHERE] * 2
    shape = (s.rows, s.inner)
    return pl.pallas_call(
        functools.partial(scan_kernel, s.head, s.state, s.gate_gain),
        grid=(s.groups,),
        in_specs=in_specs,
        out_specs=[spec((SPAN, s.wide), lambda g: (span, g)), at.full],
        out_shape=[shape_of(shape), shape_of(shape)],
        scratch_shapes=[pltpu.VMEM((SPAN, SPAN), F32), pltpu.VMEM((SPAN, s.inner), BF16)],
        input_output_aliases=aliases,
        compiler_params=PARAMS,
        cost_estimate=cost(6.5),
    )(*args)


SMALL = pl.BlockSpec(memory_space=pltpu.SMEM)


def shape_of(shape, dtype=BF16):
    return jax.ShapeDtypeStruct(shape, dtype)


def far_shape(shape, dtype=BF16):
    return pltpu.HBM(shape, dtype)


def whole_specs(*arrays):
    return [whole(array.shape) for array in arrays]


def project_mixed(sizes, inputs, level, lane_mask):
    s = sizes
    args = [inputs, level.vector, level.in_down, lane_mask, level.in_up]
    width = inputs.shape[1]
    shapes = [(s.rows, width + LANES), (s.rows, s.mixed), (s.rows, LANES), (8, s.mixed)]
    return pl.pallas_call(
        functools.partial(mixed_kernel, s.mixed, LANES, s.norm_gain, len(level.mixed)),
        grid=(1,),
        in_specs=whole_specs(*args) + [SMALL] + whole_specs(*level.mixed),
        out_specs=[whole(shape) for shape in shapes],
        out_shape=[shape_of(shape) for shape in shapes],
        compiler_params=PARAMS,
        cost_estimate=cost(6),
    )(*args, level.mixed_where, *level.mixed)


def gate_specs(sizes, level):
    return [whole((sizes.inner, LANES)), SMALL] + whole_specs(*level.gate)


def project_gate(sizes, normed, level):
    s = sizes
    return pl.pallas_call(
        functools.partial(gate_kernel, len(level.gate)),
        grid=(1,),
        in_specs=whole_specs(normed) + gate_specs(s, level),
        out_specs=whole((s.rows, s.inner)),
        out_shape=shape_of((s.rows, s.inner)),
        compiler_params=PARAMS,
        cost_estimate=cost(3.6),
    )(normed, level.in_up, level.where, *level.gate)


def project_out(sizes, normed_out, inputs, level, lane_mask):
    s = sizes
    args = [normed_out, inputs, level.out_down, lane_mask, level.out_up]
    shapes = [(s.rows, LANES), inputs.shape]
    return pl.pallas_call(
        functools.partial(out_kernel, len(level.out)),
        grid=(1,),
        in_specs=whole_specs(*args) + [SMALL] + whole_specs(*level.out),
        out_specs=[whole(shape) for shape in shapes],
        out_shape=[shape_of(shape) for shape in shapes],
        compiler_params=PARAMS,
        cost_estimate=cost(4),
    )(*args, level.where, *level.out)


def out_backward(sizes, upstream, mixed, gate, conv, level, lane_mask, tokens):
    s = sizes
    full = spec((SPAN, s.inner), lambda k: (k, 0))
    width = upstream.shape[1]
    return pl.pallas_call(
        functools.partial(out_back_kernel, s.head, s.heads, s.state, s.gate_gain, len(level.out)),
        grid=(s.spans,),
        in_specs=[
            spec((SPAN, width), lambda k: (k, 0)), spec((SPAN, LANES), lambda k: (k, 0)),
            *whole_specs(level.out_up, level.out_down), full, full, whole(level.vector.shape),
            spec((s.heads, SPAN), lambda k: (1, k)), spec((1, 8, SPAN), lambda k: (k, 0, 0)),
            spec((SPAN, 2 * s.state), lambda k: (k, 0)), SMALL, *whole_specs(*level.out),
        ],
        out_specs=[
            full, spec((s.inner, SPAN), lambda k: (0, k)), spec((SPAN, LANES), lambda k: (k, 0)),
        ] + [whole((s.inner, s.state))] * s.spans,
        out_shape=[
            shape_of((s.rows, s.inner)), shape_of((s.inner, s.rows)), shape_of((s.rows, LANES)),
        ] + [shape_of((s.inner, s.state))] * s.spans,
        scratch_shapes=[pltpu.VMEM((SPAN, s.inner), F32), pltpu.VMEM((SPAN, s.inner), BF16)],
        compiler_params=PARAMS,
        cost_estimate=cost(13.5),
    )(
        upstream, lane_mask, level.out_up, level.out_down, mixed, gate, level.vector, conv.step, tokens.flags, conv.maps,
        level.where, *level.out,
    )


def gate_in_backward(sizes, grad_gate, level):
    s = sizes
    width = 4 * s.columns
    return pl.pallas_call(
        functools.partial(gate_in_back_kernel, len(level.gate)),
        grid=(1,),
        in_specs=whole_specs(grad_gate) + gate_specs(s, level)[1:],
        out_specs=whole((s.rows, width)),
        out_shape=shape_of((s.rows, width), F32),
        compiler_params=PARAMS,
        cost_estimate=cost(3.5),
    )(grad_gate, level.where, *level.gate)


def narrow_backward(sizes, grad_gate, grad_mixed, raw, level, lane_mask):
    s = sizes
    args = [grad_gate, grad_mixed, raw, lane_mask, level.in_up]
    return pl.pallas_call(
        functools.partial(narrow_back_kernel, s.heads),
        grid=(1,),
        in_specs=whole_specs(*args),
        out_specs=whole((s.rows, LANES)),
        out_shape=shape_of((s.rows, LANES)),
        compiler_params=PARAMS,
        cost_estimate=cost(1.3),
    )(*args)


def mixed_in_backward(sizes, grad_mixed, raw, part, inputs, upstream, narrow, level):
    s = sizes
    width = inputs.shape[1]
    rows = lambda columns: spec((SPAN, columns), lambda k: (k, 0))
    return pl.pallas_call(
        functools.partial(mixed_in_back_kernel, s.mixed, s.heads, s.norm_gain, len(level.mixed)),
        grid=(s.spans,),
        in_specs=[
            rows(s.mixed), rows(LANES), rows(width), rows(width), rows(width), whole(level.vector.shape),
            rows(LANES), *whole_specs(level.in_down), SMALL, *whole_specs(*level.mixed),
        ],
        out_specs=rows(width),
        out_shape=shape_of((s.rows, width)),
        scratch_shapes=[pltpu.VMEM((SPAN, width), F32)],
        compiler_params=PARAMS,
        cost_estimate=cost(4.7),
    )(grad_mixed, raw, part, inputs, upstream, level.vector, narrow, level.in_down, level.mixed_where, *level.mixed)


def scan_backward(sizes, span, conv, grad_turned, state_in, grad_state, level, tokens, earlier):
    s = sizes
    at = span_specs(s, span)
    args = [
        conv.values, grad_turned, conv.maps, conv.step, conv.step, conv.step, tokens.flags, tokens.column, tokens.row,
        state_in, grad_state, level.heads, level.heads, conv.slope, conv.maps,
    ]
    in_specs = [
        at.turned, at.turned, at.maps, at.rows, at.decay, spec((s.heads, SPAN), lambda g: (2, span)), at.flags,
        at.doc_column, at.doc_row, at.state, at.state, at.head, whole((s.heads, LANES)),
        spec((16, s.wide), lambda g: (0, g)), spec((16, 2 * s.state), lambda g: (0, 1)),
    ]
    aliases = {}
    if earlier is not None:
        aliases = {len(args) + place: place for place in range(3)}
        args, in_specs = args + list(earlier[:3]), in_specs + [ANYWHERE] * 3
    out_specs = [spec((SPAN, s.wide), lambda g: (span, g)), at.maps, spec((SPAN, LANES), lambda g: (span, 0))]
    out_shape = [shape_of((s.rows, s.inner)), shape_of((s.rows, 2 * s.state)), shape_of((s.rows, LANES))]
    if span == 0:
        out_specs, out_shape = out_specs + [whole((8, s.mixed))], out_shape + [shape_of((8, s.mixed))]
    return pl.pallas_call(
        functools.partial(scan_back_kernel, s.head, s.heads, s.state, span == 0),
        grid=(s.groups,),
        in_specs=in_specs,
        out_specs=out_specs,
        out_shape=out_shape,
        scratch_shapes=[
            pltpu.VMEM((SPAN, SPAN), F32), pltpu.VMEM((SPAN, SPAN), F32), pltpu.VMEM((s.heads, SPAN), F32),
            pltpu.VMEM((s.heads, SPAN), F32), pltpu.VMEM((SPAN, s.state), F32), pltpu.VMEM((SPAN, s.state), F32),
        ],
        input_output_aliases=aliases,
        compiler_params=PARAMS,
        cost_estimate=cost(8.5),
    )(*args)


def conv_backward(sizes, grad_values, grad_maps, conv, later, level, tokens):
    s = sizes
    wide = 2 * s.state
    blocks = s.inner // wide
    values = spec((s.rows, wide), lambda i: (0, jnp.minimum(i, blocks - 1)))
    maps, slopes = whole((s.rows, wide)), spec((s.rows, wide), lambda i: (0, 1))
    fixed = [level.vector, tokens.valid, tokens.next_valid]
    return pl.pallas_call(
        functools.partial(conv_back_kernel, blocks, s.places),
        grid=(blocks + 1,),
        in_specs=[values, maps, values, slopes, spec((8, wide), lambda i: (0, i)), *whole_specs(*fixed)],
        out_specs=spec((s.rows, wide), lambda i: (0, i)),
        out_shape=shape_of((s.rows, s.mixed)),
        compiler_params=PARAMS,
        cost_estimate=cost(4.4),
    )(grad_values, grad_maps, conv.slope, conv.maps, later, *fixed)


def stacked_kernel(places, *refs):
    out_ref = refs[-1]
    first = 0
    for left, right in places:
        rows = refs[left].shape[1]
        out_ref[first : first + rows, :] = dot_first(refs[left][...], refs[right][...]).astype(BF16)
        first += rows
    if first < out_ref.shape[0]:
        out_ref[first:, :] = jnp.zeros((out_ref.shape[0] - first, out_ref.shape[1]), BF16)


def stacked(sizes, args, places, columns, rows, first, buffer, all_rows):
    s = sizes
    in_specs = [spec((s.rows, width), functools.partial(lambda at, _: (0, at), at)) for at, width in columns]
    aliases = {}
    if buffer is not None:
        aliases = {len(args): 0}
        args, in_specs = args + [buffer], in_specs + [ANYWHERE]
    return pl.pallas_call(
        functools.partial(stacked_kernel, places),
        grid=(1,),
        in_specs=in_specs,
        out_specs=pl.BlockSpec((pl.Element(rows), pl.Element(LANES)), lambda _: (first, 0)),
        out_shape=shape_of((all_rows, LANES)),
        input_output_aliases=aliases,
        compiler_params=PARAMS,
        cost_estimate=cost(1.6),
    )(*args)


def grad_rows(sizes, width):
    return width + 2 * sizes.inner, -(-(width + sizes.mixed + LANES) // 512) * 512


def early_grads(sizes, upstream, kept, grad_narrow_out, grad_gate, first, buffer, all_rows):
    s = sizes
    width = upstream.shape[1]
    args = [upstream, kept.narrow_out, kept.normed_out, grad_narrow_out, grad_gate, kept.normed]
    columns = [(0, width), (0, LANES), (0, s.inner), (0, LANES), (0, s.inner), (width // LANES, LANES)]
    return stacked(
        s, args, ((0, 1), (2, 3), (4, 5)), columns, grad_rows(s, width)[0], first, buffer, all_rows
    )


def late_grads(sizes, kept, grad_narrow, grad_mixed, raw, first, buffer, all_rows):
    s = sizes
    width = kept.inputs.shape[1]
    args = [kept.normed, grad_narrow, grad_mixed, raw, kept.normed]
    columns = [(0, width), (0, LANES), (0, s.mixed), (0, LANES), (width // LANES, LANES)]
    return stacked(s, args, ((0, 1), (2, 4), (3, 4)), columns, grad_rows(s, width)[1], first, buffer, all_rows)


def final_kernel(width, inner, where_ref, *refs):
    upper, upper_other, lower, lower_other, down_in_ref, in_up_ref, down_out_ref, out_up_ref = refs
    first = where_ref[0] == 0
    half = upper.shape[0]

    def rows(start, stop):
        pieces = []
        for side, (mine, yours) in enumerate(((lower, upper_other), (lower_other, upper))):
            low, high = max(start - side * half, 0), min(stop - side * half, half)
            if low < high:
                pieces.append(jnp.where(first, mine[low:high], yours[low:high]).astype(F32))
        return pieces

    def put(ref, at, start, stop):
        for piece in rows(start, stop):
            ref[at : at + piece.shape[0], :] = piece
            at += piece.shape[0]

    out_up_ref[...] = jnp.concatenate(rows(0, width), axis=0).T
    put(down_out_ref, 0, width, width + inner)
    put(in_up_ref, 0, width + inner, width + 2 * inner)
    late = width + 2 * inner
    put(down_in_ref, 0, late, late + width)
    put(in_up_ref, inner, late + width, late + width + in_up_ref.shape[0] - inner)


def final_sums(sizes, width, section, *sums):
    s = sizes
    shapes = [(width, LANES), (s.inner + s.mixed + s.heads, LANES), (s.inner, LANES), (LANES, width)]
    return pl.pallas_call(
        functools.partial(final_kernel, width, s.inner),
        grid=(1,),
        in_specs=[SMALL] + whole_specs(*sums),
        out_specs=[whole(shape) for shape in shapes],
        out_shape=[shape_of(shape, F32) for shape in shapes],
        compiler_params=PARAMS,
    )(section[None], *sums)


def token_kernel(spans, row_ref, before_ref, after_ref, table_ref, valid_ref, next_ref, column_ref, mask_ref, flags_ref):
    length = row_ref.shape[1]
    row = row_ref[...].astype(F32)
    ids = jnp.concatenate([before_ref[...].astype(F32), row, after_ref[...].astype(F32)], axis=1)
    behind = jnp.zeros((1, length + LANES), F32)
    for back in (1, 2, 3):
        same = ids[:, LANES - back : 2 * LANES - back + length] == ids[:, LANES : 2 * LANES + length]
        behind = behind + jnp.where(same, 1.0, 0.0)
    adapter = jnp.zeros_like(row)
    for document in range(table_ref.shape[0]):
        adapter = jnp.where(row == document, table_ref[document].astype(F32), adapter)
    rows = jnp.concatenate([behind[:, :length], row, adapter, jnp.zeros((5, length), F32)], axis=0).T
    wide = (length, LANES)
    valid_ref[...] = jnp.broadcast_to(rows[:, :1], wide).astype(jnp.int32)
    column_ref[...] = jnp.broadcast_to(rows[:, 1:2], wide).astype(jnp.int32)
    lanes = lax.broadcasted_iota(jnp.int32, wide, 1) // RANK
    mask_ref[...] = jnp.where(lanes == jnp.broadcast_to(rows[:, 2:3], wide).astype(jnp.int32), 1.0, 0.0)
    last = jnp.concatenate([behind[:, length:], jnp.zeros((7, LANES), F32)], axis=0).T
    next_ref[...] = jnp.broadcast_to(last[:8, :1], (8, LANES)).astype(jnp.int32)
    zeros = jnp.zeros((5, SPAN), F32)
    for span in range(spans):
        here = row[:, span * SPAN : (span + 1) * SPAN]
        start = ids[:, LANES + span * SPAN - 1 : LANES + span * SPAN]
        end = here[:, SPAN - 1 :]
        keep = jnp.broadcast_to(jnp.where(start == end, 1.0, 0.0), here.shape)
        flags_ref[span] = jnp.concatenate(
            [jnp.where(here == start, 1.0, 0.0), jnp.where(here == end, 1.0, 0.0), keep, zeros], axis=0
        )


def token_tables(doc_ids, table):
    rows = doc_ids.shape[1]
    before = from_behind(doc_ids[:, rows - LANES :], SEQ, 1)
    after = from_behind(doc_ids[:, :LANES], SEQ, -1)
    shapes = [((rows, LANES), jnp.int32), ((8, LANES), jnp.int32), ((rows, LANES), jnp.int32), ((rows, LANES), F32)]
    shapes.append(((rows // SPAN, 8, SPAN), F32))
    valid, next_valid, column, mask, flags = pl.pallas_call(
        functools.partial(token_kernel, rows // SPAN),
        grid=(1,),
        in_specs=whole_specs(doc_ids, before, after) + [SMALL],
        out_specs=[whole(shape) for shape, _ in shapes],
        out_shape=[jax.ShapeDtypeStruct(*one) for one in shapes],
        compiler_params=PARAMS,
    )(doc_ids, before, after, table)
    row = jnp.broadcast_to(doc_ids, (8, rows))
    return Bag(valid=valid, next_valid=next_valid, column=column, row=row, flags=flags), mask


def state_hops(rows, block_rows):
    eighth = block_rows // DOCS_PER_BLOCK
    if rows // SPAN > 1 and eighth > SPAN:
        raise ValueError("unsupported block")
    return 1 if rows >= eighth else 2 * eighth // rows - 1


def pass_states(sizes, local, conv, tokens, hops, direction):
    if hops > 1:
        keep = jnp.exp2(conv.step[sizes.heads : 2 * sizes.heads, -1]) * tokens.flags[0, 2, 0]
        keep = jnp.repeat(keep, sizes.head)[:, None]
        total = local.astype(F32)
        reach = 1
        while reach < hops:
            total = total + keep * from_behind(total.astype(BF16), SEQ, direction * reach).astype(F32)
            keep = keep * from_behind(keep, SEQ, direction * reach)
            reach *= 2
        local = total.astype(BF16)
    return from_behind(local, SEQ, direction)


def layer_forward(sizes, inputs, level, lane_mask, tokens, hops):
    s = sizes
    normed, mixed, raw, rim = project_mixed(s, inputs, level, lane_mask)
    rim = from_behind(rim, SEQ, 1)
    yield mixed
    gate = None
    if level.gate_first:
        gate = project_gate(s, normed, level)
        rim = tie(rim, gate)
    (values, slope, maps, step), states = conv_forward(s, mixed, raw, rim, level, tokens)
    conv = Bag(values=values, slope=slope, maps=maps, step=step)
    states_in = [pass_states(s, states[-1], conv, tokens, hops, 1)] + list(states[:-1])
    yield values
    if gate is None:
        gate = project_gate(s, normed, level)
    outputs = None
    for span in reversed(range(s.spans)):
        outputs = scan_forward(s, span, conv, states_in[span], gate, level, tokens, outputs)
        if span == s.spans - 1:
            yield outputs[0]
    mixed_out, normed_out = outputs
    narrow_out, result = project_out(s, normed_out, inputs, level, lane_mask)
    yield result
    kept = Bag(
        inputs=inputs, normed=normed, gate=gate, conv=conv, states_in=states_in, mixed_out=mixed_out,
        normed_out=normed_out, narrow_out=narrow_out,
    )
    return result, kept


def layer_backward(sizes, upstream, kept, level, lane_mask, tokens, hops):
    s = sizes
    conv = kept.conv
    early_rows, late_rows = grad_rows(s, upstream.shape[1])
    all_rows = early_rows + late_rows
    grad_gate, turned, grad_narrow_out, *local = out_backward(
        s, upstream, kept.mixed_out, kept.gate, conv, level, lane_mask, tokens
    )
    grad_states = list(local[1:]) + [pass_states(s, local[0], conv, tokens, hops, -1)]
    buffer = early_grads(s, upstream, kept, grad_narrow_out, grad_gate, 0, None, all_rows)
    outputs = None
    for span in range(s.spans):
        outputs = scan_backward(
            s, span, conv, turned, kept.states_in[span], grad_states[span], level, tokens, outputs
        )
        if span == 0:
            later = from_behind(outputs[3], SEQ, -1)
            turned = yield outputs[0], turned
    grad_values, grad_maps, raw = outputs[:3]
    grad_values = yield grad_values, grad_values
    grad_mixed = conv_backward(s, grad_values, grad_maps, conv, later, level, tokens)
    grad_mixed = yield grad_mixed, grad_mixed
    narrow = narrow_backward(s, grad_gate, grad_mixed, raw, level, lane_mask)
    buffer = late_grads(s, kept, narrow, grad_mixed, raw, early_rows, buffer, all_rows)
    grad_mixed = yield buffer, grad_mixed
    part = gate_in_backward(s, tie(grad_gate, grad_mixed), level)
    return mixed_in_backward(s, grad_mixed, raw, part, kept.inputs, upstream, narrow, level)


def make_level(sizes, vector, numbers, adapters, where):
    s = sizes
    in_down, in_up = adapters
    dt_bias, a_log, skip_gain = numbers
    rate = -jnp.exp(a_log)[:, None]
    lane = jnp.arange(LANES)[None, :]
    table = jnp.where(lane == 1, skip_gain[:, None], jnp.where(lane == 2, dt_bias[:, None], rate))
    table = jnp.where(lane == 0, rate * LOG2E, table)
    return Bag(vector=vector, heads=table, in_down=in_down, in_up=in_up, where=where, mixed_where=where)


def swap(value):
    return lax.ppermute(value, SECTION, [(0, 1), (1, 0)])


def exchange(value, axis, distance):
    count = lax.axis_size(axis)
    return lax.ppermute(value, axis, [(place, place ^ distance) for place in range(count)])


def rows_at(value, index, rows):
    return lax.dynamic_slice_in_dim(value, index * rows, rows, axis=0)


def put_at(buffer, value, *index):
    start = list(index) + [0] * (buffer.ndim - len(index))
    return lax.dynamic_update_slice(buffer, value.reshape((1,) * len(index) + value.shape), start)


def across(value, second):
    count = lax.axis_size(WSHARD)
    pairs = []
    for section in range(2):
        distance = 2 - section if second else 1 + section
        pairs += [(section * count + place, section * count + (place ^ distance)) for place in range(count)]
    return lax.ppermute(value, (SECTION, WSHARD), pairs)


class Parts:
    def __init__(self, quarters):
        self.section = lax.axis_index(SECTION)
        self.quarters, self.near, self.parts = quarters, {}, {}
        other = swap(quarters[0][0])
        self.own = [jnp.where(self.section == 0, quarters[0][0], other)]
        others = [other] + [swap(tie(matrix, self.own[0])) for matrix, _, _ in quarters[1:]]
        self.later = others[1]
        for layer in range(2):
            for (matrix, _, _), other in list(zip(quarters, others, strict=True))[1 - layer :]:
                self.own.append(jnp.where(self.section == layer, matrix, other))

    def start(self, index, *after):
        self.near[index] = across(tie(self.own[index], *after), False)

    def forward(self, index, *after):
        _, half, step = self.quarters[index % len(self.quarters)]
        near = tie(self.near[index], *after)
        apart = across(lax.dynamic_slice_in_dim(near, self.section * step, half, axis=0), True)
        self.halfway = (self.own[index], near, swap(near), apart)
        return apart

    def finish(self, index, *after):
        self.parts[index] = self.halfway + (swap(tie(self.halfway[3], *after)),)


def scatter_start(value, axis):
    count, place = lax.axis_size(axis), lax.axis_index(axis)
    rows = value.shape[0] // count
    sent = [exchange(rows_at(value, place ^ away, rows), axis, away) for away in range(1, count)]
    return rows_at(value, place, rows), sent


def scatter_done(parts, *after):
    own, received = parts
    total = own.astype(F32)
    for part in tie(received, *after):
        total = total + part.astype(F32)
    return total.astype(BF16)


def gather_start(value, axis):
    return value, [exchange(value, axis, away) for away in range(1, lax.axis_size(axis))]


def gather_done(parts, axis, *after):
    own, received = parts
    count, place = lax.axis_size(axis), lax.axis_index(axis)
    buffer = jnp.zeros((count,) + own.shape, own.dtype)
    for away, part in enumerate([own] + tie(received, *after)):
        buffer = put_at(buffer, part, place ^ away)
    return buffer.reshape((count * own.shape[0],) + own.shape[1:])


def chip_start(packed):
    section = lax.axis_index(SECTION)
    half = packed.shape[0] // 2
    return rows_at(packed, section, half), [swap(rows_at(packed, 1 - section, half))]


def both_layers(own):
    section = lax.axis_index(SECTION)
    other = swap(own)
    return [jnp.where(section == layer, own, other) for layer in range(2)]


def on_device(
    layer_input, out_grad, doc_index, doc_adapter, in_weight, out_weight, norm_gain, conv_weight, conv_bias, dt_bias,
    a_log, skip_gain, gate_gain, *adapters,
):
    section, place = lax.axis_index(SECTION), lax.axis_index(WSHARD)
    batches, rows, width = layer_input.shape
    heads, inner = dt_bias.shape[1], gate_gain.shape[1]
    taps, mixed = conv_weight.shape[1:]
    sizes = Sizes(rows, inner, heads, (mixed - inner) // 2, in_weight.shape[1], taps)
    block_rows = rows * lax.axis_size(SEQ)
    hops = state_hops(rows, block_rows)

    pick = lambda array: lax.dynamic_index_in_dim(array, section, 0, keepdims=False)
    turned = in_weight[0].T
    main = mixed // 2
    weights = Parts(
        [
            (turned[inner:], main + heads, main),
            (turned[:inner], inner // 2, inner // 2),
            (out_weight[0], out_weight.shape[1] // 2, out_weight.shape[1] // 2),
        ]
    )
    weights.start(0)
    weights.start(1, weights.forward(0))
    weights.finish(0)
    rest = (layer_input, doc_index, doc_adapter, norm_gain, conv_weight, conv_bias, dt_bias, a_log, skip_gain)
    rest, gate_gain, adapters = tie((rest, gate_gain, adapters), weights.later)
    layer_input, doc_index, doc_adapter, norm_gain, conv_weight, conv_bias, dt_bias, a_log, skip_gain = rest
    inputs, doc_ids, table = pick(layer_input), pick(doc_index), pick(doc_adapter)[0]
    tokens, lane_mask = token_tables(doc_ids[None, :], table)
    vectors = both_layers(jnp.concatenate([conv_weight[0].reshape(1, -1), conv_bias, gate_gain, norm_gain], axis=1))
    numbers = both_layers(jnp.concatenate([dt_bias, a_log, skip_gain], axis=0))
    in_down, in_up, out_down, out_up = adapters
    both = [both_layers(array) for array in (in_down[0], in_up[0].T)]
    out_adapters = [(array[0], swap(array[0])) for array in (out_down, out_up)]
    where = jnp.stack([place, place ^ (1 + section), place ^ (2 - section), place ^ 3, section]).astype(jnp.int32)
    levels = [
        make_level(sizes, vectors[layer], numbers[layer], [pair[layer] for pair in both], where)
        for layer in range(2)
    ]
    small = [inputs, lane_mask, tokens.__dict__, weights.own[1:]] + [level.__dict__ for level in levels]
    small, weights.parts[0] = lax.optimization_barrier((small, weights.parts[0]))
    inputs, lane_mask, token_fields, weights.own[1:], *level_fields = small
    tokens, levels = Bag(**token_fields), [Bag(**fields) for fields in level_fields]
    levels[0].mixed = weights.parts[0]
    levels[0].gate_first = levels[1].gate_first = False

    passes = {(0, 0): 1, (0, 1): 2, (0, 2): 3, (0, 4): 4, (1, 1): 5}
    ends = {(0, 1): 1, (0, 2): 2, (0, 3): 3, (1, 0): 4, (1, 2): 5}
    results, kept = [], []
    rows_now = inputs
    for layer in range(2):
        stages = layer_forward(sizes, rows_now, levels[layer], lane_mask, tokens, hops)
        for stage in range(5):
            try:
                token = next(stages)
            except StopIteration as end:
                rows_now, stored = end.value
            if (layer, stage) == (0, 0):
                chosen = [
                    [jnp.where(section == choice, tie(here, token), there) for choice in range(2)]
                    for here, there in out_adapters
                ]
                for choice in range(2):
                    levels[choice].out_down, levels[choice].out_up = chosen[0][choice], chosen[1][choice]
            if (layer, stage) == (1, 0):
                grads = pick(tie(out_grad, token))
            move = ends.get((layer, stage))
            if move is not None:
                weights.finish(move, token)
                owner, parts = levels[move // 3], weights.parts[move]
                if move % 3 == 0:
                    owner.mixed = parts
                elif move % 3 == 1:
                    owner.gate = parts
                else:
                    owner.out = parts
            move = passes.get((layer, stage))
            if move is not None:
                weights.forward(move, token)
                if move < 5:
                    weights.start(move + 1, token)
        results.append(rows_now)
        kept.append(stored)

    def placed(pair):
        here = jnp.where(section == 0, pair[0], pair[1])
        there = swap(jnp.where(section == 0, pair[1], pair[0]))
        first, second = jnp.where(section == 0, here, there), jnp.where(section == 0, there, here)
        return jnp.stack([first, second])[None]

    direct = lax.axis_size(SEQ) == 4
    both_axes = (WSHARD, SEQ)

    def finish(stages, value):
        try:
            stages.send(value)
        except StopIteration as end:
            return end.value

    stages = layer_backward(sizes, tie(grads, rows_now), kept[1], levels[1], lane_mask, tokens, hops)
    _, pending = next(stages)
    for _ in range(2):
        _, pending = stages.send(pending)
    upper, pending = stages.send(pending)
    upper = chip_start(upper)
    upper_grad = finish(stages, pending)
    upper = scatter_done(upper, upper_grad)
    upper_grad = tie(upper_grad, upper)
    upper = scatter_start(upper, WSHARD) if direct else lax.psum(upper, both_axes)

    stages = layer_backward(sizes, upper_grad, kept[0], levels[0], lane_mask, tokens, hops)
    token, pending = next(stages)
    if direct:
        upper = scatter_start(scatter_done(upper, token), SEQ)
    token, pending = stages.send(tie(pending, upper[0]))
    if direct:
        upper = gather_start(scatter_done(upper, token), SEQ)
    token, pending = stages.send(tie(pending, upper[0]))
    if direct:
        upper = gather_start(gather_done(upper, SEQ, token), WSHARD)
    lower, pending = stages.send(tie(pending, upper[0]))
    lower = chip_start(lower)
    if direct:
        upper = gather_done(upper, WSHARD, lower[0])
    lower = scatter_done(lower, upper)
    if direct:
        lower = scatter_start(lower, WSHARD)
    lower_grad = finish(stages, tie(pending, lower[0]))
    outputs = (placed(results), placed([lower_grad, upper_grad]))
    if direct:
        lower = scatter_start(scatter_done(lower, lower_grad), SEQ)
        lower = gather_start(scatter_done(lower), SEQ)
        lower = gather_start(gather_done(lower, SEQ), WSHARD)
        lower = gather_done(lower, WSHARD, outputs)
    else:
        lower = lax.psum(lower, both_axes)
    sums = final_sums(sizes, width, section, upper, swap(upper), lower, swap(lower))
    down_in, in_up, down_out, out_up = sums
    return (
        *outputs, down_in[None], in_up.T[None], down_out[None], out_up[None],
    )


def solution(mesh):
    tokens, matrix, vector = P(None, (WSHARD, SEQ), None), P(SECTION, None, None), P(SECTION, None)
    in_specs = (tokens, tokens, P(None, (WSHARD, SEQ)), P(None, WSHARD, None))
    in_specs += (P(SECTION, WSHARD, None),) * 2
    in_specs += (vector, matrix) + (vector,) * 5 + (matrix,) * 4
    out_specs = (P(SECTION, None, (WSHARD, SEQ), None),) * 2 + (matrix,) * 4
    return jax.shard_map(on_device, mesh=mesh, in_specs=in_specs, out_specs=out_specs, check_vma=False)
```

```python
import functools

import jax
import jax.numpy as jnp
from jax import lax
from jax.experimental import pallas as pl
from jax.experimental.pallas import tpu as pltpu
from jax.sharding import PartitionSpec as P

SPAN = 256
RANK = 16
LANES = 128
DOCS_PER_BLOCK = 8
EPSILON = 1e-05
LOG2E = 1.4426950408889634
EXACT = lax.Precision.HIGHEST
SEQ, WSHARD, SECTION = "seq", "wshard", "section"
BF16 = jnp.bfloat16
F32 = jnp.float32
PARAMS = pltpu.CompilerParams(vmem_limit_bytes=20 * 1024 * 1024)


class Bag:
    def __init__(self, **fields):
        self.__dict__.update(fields)


def tie(value, *others):
    return lax.optimization_barrier((value, *others))[0]


def from_behind(value, axis, steps):
    count = lax.axis_size(axis)
    initial, last = (max(0, -steps), min(count, count - steps))
    return lax.ppermute(value, axis, [(source, source + steps) for source in range(initial, last)])


def dot(left, right):
    return jnp.dot(left, right, preferred_element_type=F32)


def dot_last(left, right):
    return lax.dot_general(left, right, (((1,), (1,)), ((), ())), preferred_element_type=F32)


def dot_first(left, right):
    return lax.dot_general(left, right, (((0,), (0,)), ((), ())), preferred_element_type=F32)


def rms_rate(values):
    return lax.rsqrt(jnp.mean(values * values, axis=-1, keepdims=True) + EPSILON)


def sigmoid(v):
    return 0.5 + 0.5 * jnp.tanh(0.5 * v)


def lower_ones(shape):
    rows = lax.broadcasted_iota(jnp.int32, shape, 0)
    columns = lax.broadcasted_iota(jnp.int32, shape, 1)
    return rows <= columns


def conv_rows(rows, rim, weight, offset, valid):
    length = rows.shape[0]
    valid = jnp.concatenate([valid] * (rows.shape[1] // LANES), axis=1)
    extended = jnp.concatenate([rim, rows], axis=0)
    taps = weight.shape[0]
    total = offset + weight[taps - 1 : taps] * rows
    for back in range(1, taps):
        shifted = extended[8 - back : 8 - back + length]
        total = total + jnp.where(valid >= back, shifted, 0.0) * weight[taps - 1 - back : taps - back]
    gate = sigmoid(total)
    active = total * gate
    return active, gate + active * (1.0 - gate)


def taps_at(vector_ref, places, first, width):
    rows = [vector_ref[:, pl.ds(pl.multiple_of(place + first, LANES), width)] for place in places]
    return jnp.concatenate(rows[:-1], axis=0), rows[-1]


def conv_kernel(
    spans, head, heads, state, places,
    mixed_ref, mixed_bc_ref, rim_ref, rim_bc_ref, vector_ref, valid_ref, raw_ref, head_ref, token_ref,
    values_ref, slope_ref, bc_ref, step_ref, *rest,
):
    state_refs, tail_ref = rest[:-1], rest[-1]
    group = pl.program_id(0)
    valid = valid_ref[...]
    width = mixed_ref.shape[1]
    heads_here = width // head

    @pl.when(group == 0)
    def _():
        weight, offset = taps_at(vector_ref, places, pl.num_programs(0) * width, 2 * state)
        active, slope = conv_rows(
            mixed_bc_ref[...].astype(F32), rim_bc_ref[...].astype(F32), weight, offset, valid
        )
        bc_ref[...] = jnp.concatenate([active, slope], axis=1).astype(BF16)
        raw = raw_ref[...].astype(F32).T[:heads] + head_ref[:, 2:3]
        step = (jnp.maximum(raw, 0.0) + jnp.log1p(jnp.exp(-jnp.abs(raw)))).astype(BF16).astype(F32)
        step_ref[:heads, :] = step
        step_ref[2 * heads :, :] = sigmoid(raw)
        drop = step * head_ref[:, :1]
        ones = lower_ones((SPAN, SPAN)).astype(F32)
        for span in range(spans):
            here = slice(span * SPAN, (span + 1) * SPAN)
            decay = jnp.dot(drop[:, here], ones, precision=EXACT, preferred_element_type=F32)
            step_ref[heads : 2 * heads, here] = decay
            tail = jnp.exp2(decay[:, SPAN - 1 :] - decay) * token_ref[span][1:2]
            tail_ref[:, here] = tail * step[:, here]

    weight, offset = taps_at(vector_ref, places, group * width, width)
    active, slope = conv_rows(
        mixed_ref[...].astype(F32), rim_ref[...].astype(F32), weight, offset, valid
    )
    slope_ref[...] = slope.astype(BF16)
    low = active.T.astype(BF16)
    values_ref[...] = low
    low = low.astype(F32)
    first = pl.multiple_of(group * heads_here, heads_here)
    tail_rows = tail_ref[pl.ds(first, heads_here), :]
    for span in range(spans):
        here = slice(span * SPAN, (span + 1) * SPAN)
        driven = jnp.concatenate(
            [
                (low[place * head : (place + 1) * head, here] * tail_rows[place : place + 1, here]).astype(BF16)
                for place in range(heads_here)
            ],
            axis=0,
        )
        state_refs[span][...] = dot(driven, bc_ref[here, :state]).astype(BF16)


def faded(row, column, score_ref):
    half = SPAN // 2
    upper = jnp.exp2(jnp.minimum(row - column[:half], 0.0))
    lower = jnp.exp2(jnp.minimum(row[:, half:] - column[half:], 0.0))
    lower = jnp.concatenate([jnp.zeros_like(lower), lower], axis=1)
    return (upper, lower), (upper * score_ref[:half, :], lower * score_ref[half:, :])


def scan_kernel(
    head, state, gain,
    values_ref, bc_ref, step_ref, decay_ref, token_ref, doc_column_ref, doc_row_ref, state_ref, head_ref, gate_ref,
    vector_ref, *rest,
):
    mixed_ref, normed_ref, score_ref, scanned_ref = rest[-4:]
    group, groups = pl.program_id(0), pl.num_programs(0)
    width = values_ref.shape[0]
    heads_here = width // head

    @pl.when(group == 0)
    def _():
        score = dot_last(bc_ref[:, :state], bc_ref[:, state:])
        same = (jnp.concatenate([doc_column_ref[...]] * (SPAN // LANES), axis=1) == doc_row_ref[:1]) & lower_ones((SPAN, SPAN))
        score_ref[...] = jnp.where(same, score, 0.0)

    decay, step = decay_ref[...], step_ref[...]
    carry = jnp.exp2(decay) * token_ref[0][:1]
    columns = jnp.concatenate([decay] * (LANES // heads_here), axis=0).T
    out_map = bc_ref[:, state:]
    parts = []
    for place in range(heads_here):
        rows = slice(place * head, (place + 1) * head)
        one = slice(place, place + 1)
        kernel = jnp.concatenate([part.astype(BF16) for part in faded(decay[one], columns[:, one], score_ref)[1]], axis=0)
        values = values_ref[rows].astype(F32)
        driven = (values * step[one]).astype(BF16)
        before = dot_last(state_ref[rows], out_map) * carry[one]
        parts.append(dot(driven, kernel) + before + head_ref[one, 1:2] * values)
    low = jnp.concatenate(parts, axis=0).astype(BF16).T
    mixed_ref[...] = low
    scanned_ref[:, pl.ds(pl.multiple_of(group * width, width), width)] = low

    @pl.when(group == groups - 1)
    def _():
        def rows_at(index, _):
            rows = pl.ds(pl.multiple_of(index * 16, 16), 16)
            mixed = scanned_ref[rows, :]
            gate = gate_ref[rows, :].astype(F32)
            gated = mixed.astype(F32) * (gate * sigmoid(gate))
            normed_ref[rows, :] = (gated * rms_rate(gated) * vector_ref[:, gain : gain + gated.shape[1]]).astype(BF16)
            return 0

        lax.fori_loop(0, SPAN // 16, rows_at, 0, unroll=8)


def out_back_kernel(
    head, heads, state, gain, count,
    up_ref, lane_ref, up_out_ref, down_out_ref, mixed_ref, gate_ref, vector_ref, decay_ref, token_ref, bc_ref, where_ref,
    *rest,
):
    parts, rest = rest[:count], rest[count:]
    (project_ref, turned_ref, narrow_ref), state_refs, (grad_ref, grad_mixed_ref) = rest[:3], rest[3:-2], rest[-2:]
    width = mixed_ref.shape[1]
    up = up_ref[...]
    narrow = (dot_last(up, up_out_ref[...]) * lane_ref[...]).astype(BF16)
    narrow_ref[...] = narrow
    left = jnp.concatenate([up, narrow], axis=1)
    for offset, part in out_places(where_ref, parts):
        here = pl.ds(offset, part.shape[0])
        grad_ref[:, here] = dot_last(left, jnp.concatenate([part[...], down_out_ref[here, :]], axis=1))

    def rows_at(index, _):
        rows = pl.ds(pl.multiple_of(index * 16, 16), 16)
        mixed = mixed_ref[rows, :].astype(F32)
        gate = gate_ref[rows, :].astype(F32)
        share = sigmoid(gate)
        silu = gate * share
        gated = mixed * silu
        grad = grad_ref[rows, :] * vector_ref[:, gain : gain + width]
        rate = rms_rate(gated)
        pull = jnp.mean(gated * grad, axis=-1, keepdims=True) * rate * rate * rate
        grad_gated = rate * grad - gated * pull
        project_ref[rows, :] = (grad_gated * mixed * (share + silu * (1.0 - share))).astype(BF16)
        grad_mixed_ref[rows, :] = (grad_gated * silu).astype(BF16)
        return 0

    lax.fori_loop(0, SPAN // 16, rows_at, 0, unroll=8)
    carry = jnp.exp2(decay_ref[...]) * token_ref[0][:1]
    out_map = bc_ref[:, state:]
    wide = 512
    for first in range(0, width, wide):
        low = grad_mixed_ref[:, first : first + wide].astype(F32).T
        turned_ref[first : first + wide, :] = low.astype(BF16)
        scaled = [
            (low[place * head : (place + 1) * head] * carry[first // head + place : first // head + place + 1]).astype(BF16)
            for place in range(wide // head)
        ]
        local = dot(jnp.concatenate(scaled, axis=0), out_map).astype(BF16)
        for span, state_ref in enumerate(state_refs):

            @pl.when(pl.program_id(0) == span)
            def _(state_ref=state_ref, first=first, local=local):
                state_ref[first : first + wide, :] = local


def aligned(value, unit):
    return pl.multiple_of(value * unit, unit)


def out_places(where_ref, parts):
    if len(parts) == 1:
        half = parts[0].shape[1]
        return [((2 * place + side) * half, parts[0].at[4 * side + place]) for place in range(4) for side in range(2)]
    rows, half = parts[0].shape[0], parts[3].shape[0]
    places = [(aligned(where_ref[place], rows), part) for place, part in enumerate(parts[:3])]
    apart = where_ref[3] * 2
    places.append((aligned(apart + where_ref[4], half), parts[3]))
    places.append((aligned(apart + 1 - where_ref[4], half), parts[4]))
    return places


def in_rows(where_ref, parts, step, start, size):
    side = int(start >= step)
    there = slice(start - side * step, start - side * step + size)
    if len(parts) == 1:
        return [parts[0][4 * side + place, there, :] for place in range(4)]
    pair = (parts[3][there], parts[4][there])
    apart = jnp.where(where_ref[4] == 0, pair[side], pair[1 - side])
    return [part[start : start + size] for part in parts[:3]] + [apart]


def in_columns(ref, where_ref, parts):
    columns = (ref.shape[1] - LANES) // parts
    places = [pl.ds(aligned(where_ref[place], columns), columns) for place in range(parts)]
    return jnp.concatenate([ref[:, here] for here in places + [pl.ds(parts * columns, LANES)]], axis=1)


def mixed_kernel(
    main, lanes, gain, count, input_ref, vector_ref, down_ref, lane_ref, up_ref, where_ref, *rest
):
    parts, (normed_ref, mixed_ref, raw_ref, rim_ref) = rest[:count], rest[count:]
    rows = input_ref.shape[0]
    inputs = input_ref[...].astype(F32)
    normed = (inputs * rms_rate(inputs) * vector_ref[:, gain : gain + inputs.shape[1]]).astype(BF16)
    narrow = (dot(normed, down_ref[...]) * lane_ref[...]).astype(BF16)
    normed_ref[...] = jnp.concatenate([normed, narrow], axis=1)
    left = in_columns(normed_ref, where_ref, 4)
    step, extra = main // 6, raw_ref.shape[1] // 4
    before = up_ref.shape[0] - main - extra

    def product(start, size):
        right = in_rows(where_ref, parts, main // 2, start, size)
        right.append(up_ref[before + start : before + start + size])
        return dot_last(left, jnp.concatenate(right, axis=1))

    for start in range(0, main, step):
        low = product(start, step).astype(BF16)
        mixed_ref[:, start : start + step] = low
        rim_ref[:, start : start + step] = low[rows - 8 :]
    raw_ref[...] = jnp.concatenate([product(main, extra), jnp.zeros((rows, lanes - extra), F32)], axis=1).astype(BF16)


def gate_kernel(count, normed_ref, up_ref, where_ref, *rest):
    parts, gate_ref = rest[:count], rest[count]
    left = in_columns(normed_ref, where_ref, 4)
    wide = 512
    inner = gate_ref.shape[1]
    for start in range(0, inner, wide):
        right = in_rows(where_ref, parts, inner // 2, start, wide) + [up_ref[start : start + wide]]
        gate_ref[:, start : start + wide] = dot_last(left, jnp.concatenate(right, axis=1)).astype(BF16)


def out_kernel(count, normed_ref, input_ref, down_ref, lane_ref, up_ref, where_ref, *rest):
    parts, (narrow_ref, out_ref) = rest[:count], rest[count:]
    narrow = (dot(normed_ref[...], down_ref[...]) * lane_ref[...]).astype(BF16)
    narrow_ref[...] = narrow
    places = out_places(where_ref, parts)
    left = [normed_ref[:, pl.ds(offset, part.shape[0])] for offset, part in places]
    left = jnp.concatenate(left + [narrow], axis=1)
    wide = 256
    for start in range(0, out_ref.shape[1], wide):
        here = slice(start, start + wide)
        right = jnp.concatenate([part[:, here] for _, part in places] + [up_ref[:, here]], axis=0)
        out_ref[:, here] = (input_ref[:, here].astype(F32) + dot(left, right)).astype(BF16)


def gate_in_back_kernel(count, grad_ref, where_ref, *rest):
    parts, out_ref = rest[:count], rest[count]
    grad = grad_ref[...]
    half = grad.shape[1] // 2
    lower, upper = [in_rows(where_ref, parts, half, side * half, half) for side in range(2)]
    columns = lower[0].shape[1]
    for place in range(4):
        product = dot(grad[:, :half], lower[place]) + dot(grad[:, half:], upper[place])
        out_ref[:, place * columns : (place + 1) * columns] = product


def narrow_back_kernel(extra, grad_gate_ref, grad_ref, raw_ref, lane_ref, up_ref, narrow_ref):
    left = jnp.concatenate([grad_gate_ref[...], grad_ref[...], raw_ref[...][:, :extra]], axis=1)
    narrow_ref[...] = (dot(left, up_ref[...]) * lane_ref[...]).astype(BF16)


def mixed_in_back_kernel(
    main, extra, gain, count,
    grad_ref, raw_ref, part_ref, input_ref, up_stream_ref, vector_ref, narrow_ref, down_ref, where_ref, *rest
):
    parts, (out_ref, total_ref) = rest[:count], rest[count:]
    width = input_ref.shape[1]
    columns = width // 4
    half = main // 2
    left = jnp.concatenate([grad_ref[...], raw_ref[...][:, :extra]], axis=1)
    lower = in_rows(where_ref, parts, half, 0, half)
    upper = in_rows(where_ref, parts, half, half, half + extra)
    for place in range(4):
        product = dot(left[:, :half], lower[place]) + dot(left[:, half:], upper[place])
        here = slice(place * columns, (place + 1) * columns)
        total_ref[:, pl.ds(aligned(where_ref[place], columns), columns)] = part_ref[:, here] + product
    scaled = (total_ref[...] + dot_last(narrow_ref[...], down_ref[...])) * vector_ref[:, gain : gain + width]
    inputs = input_ref[...].astype(F32)
    rate = rms_rate(inputs)
    pull = jnp.mean(inputs * scaled, axis=-1, keepdims=True) * rate * rate * rate
    out_ref[...] = (up_stream_ref[...].astype(F32) + rate * scaled - inputs * pull).astype(BF16)


def scan_back_kernel(
    head, heads, state, edge,
    values_ref, grad_ref, bc_ref, step_ref, decay_ref, sig_ref, token_ref, doc_column_ref, doc_row_ref, state_ref,
    grad_state_ref, head_ref, rate_ref, slope_ref, slope_bc_ref, *rest,
):
    outputs = rest[:-6]
    if edge:
        outputs, edge_ref = outputs[:-1], outputs[-1]
    out_values_ref, out_bc_ref, out_raw_ref = outputs[-3:]
    score_ref, grad_score_ref, pull_ref, direct_ref, grad_in_ref, grad_out_ref = rest[-6:]
    group, groups = pl.program_id(0), pl.num_programs(0)
    width = values_ref.shape[0]
    heads_here = width // head
    in_map, out_map = bc_ref[:, :state], bc_ref[:, state:]

    def same_doc():
        return (jnp.concatenate([doc_column_ref[...]] * (SPAN // LANES), axis=1) == doc_row_ref[:1]) & lower_ones((SPAN, SPAN))

    @pl.when(group == 0)
    def _():
        score_ref[...] = jnp.where(same_doc(), dot_last(in_map, out_map), 0.0)
        grad_score_ref[...] = jnp.zeros_like(grad_score_ref)
        grad_in_ref[...] = jnp.zeros_like(grad_in_ref)
        grad_out_ref[...] = jnp.zeros_like(grad_out_ref)

    decay, step = decay_ref[...], step_ref[...]
    token = token_ref[0]
    last = decay[:, SPAN - 1 :]
    carry = jnp.exp2(decay) * token[:1]
    tail = jnp.exp2(last - decay) * token[1:2]
    keep = jnp.exp2(last) * token[2:3, :1]
    columns = jnp.concatenate([decay] * (LANES // heads_here), axis=0).T
    at_end = lax.broadcasted_iota(jnp.int32, (1, SPAN), 1) == SPAN - 1
    grads, tails, carried, pulls, directs = [], [], [], [], []
    for place in range(heads_here):
        rows = slice(place * head, (place + 1) * head)
        one = slice(place, place + 1)
        fade, kernel = faded(decay[one], columns[:, one], score_ref)
        kernel = jnp.concatenate([part.astype(BF16) for part in kernel], axis=0)
        values = values_ref[rows].astype(F32)
        driven = (values * step[one]).astype(BF16)
        grad_low = grad_ref[rows]
        grad = grad_low.astype(F32)
        grad_kernel = dot_first(driven, grad_low)
        half = SPAN // 2
        grad_score_ref[:half, :] += grad_kernel[:half] * fade[0]
        grad_score_ref[half:, half:] += grad_kernel[half:, half:] * fade[1][:, half:]
        state_here, grad_state = state_ref[rows], grad_state_ref[rows]
        output = dot(driven, kernel) + dot_last(state_here, out_map) * carry[one]
        by_state = dot_last(grad_state, in_map) * tail[one]
        grad_driven = dot_last(grad_low, kernel) + by_state
        driven = driven.astype(F32)
        pull = jnp.sum(grad * output - driven * grad_driven, axis=0, keepdims=True)
        ending = jnp.sum(jnp.sum(driven * by_state, axis=0, keepdims=True), axis=1, keepdims=True)
        kept = jnp.sum(state_here.astype(F32) * grad_state.astype(F32), axis=0, keepdims=True)
        ending = ending + keep[one] * jnp.sum(kept, axis=1, keepdims=True)
        pulls.append(pull + jnp.where(at_end, ending, 0.0))
        directs.append(jnp.sum(values * grad_driven, axis=0, keepdims=True))
        grads.append(step[one] * grad_driven + head_ref[one, 1:2] * grad)
        tails.append((driven * tail[one]).astype(BF16))
        carried.append((grad * carry[one]).astype(BF16))
    grad_in_ref[...] += dot_first(jnp.concatenate(tails, axis=0), grad_state_ref[...])
    grad_out_ref[...] += dot_first(jnp.concatenate(carried, axis=0), state_ref[...])
    grads = jnp.concatenate(grads, axis=0).T.astype(BF16)
    out_values_ref[...] = grads
    if edge:
        product = grads[:8].astype(F32) * slope_ref[...][:8].astype(F32)
        edge_ref[:, pl.ds(pl.multiple_of(group * width, width), width)] = product.astype(BF16)
    here = pl.ds(pl.multiple_of(group * heads_here, heads_here), heads_here)
    pull_ref[here, :] = jnp.concatenate(pulls, axis=0)
    direct_ref[here, :] = jnp.concatenate(directs, axis=0)

    @pl.when(group == groups - 1)
    def _():
        ones = lower_ones((SPAN, SPAN)).astype(F32)
        summed = lax.dot_general(
            pull_ref[...], ones, (((1,), (1,)), ((), ())), precision=EXACT, preferred_element_type=F32
        )
        grad_step = (direct_ref[...] + rate_ref[:, 3:4] * summed).astype(BF16).astype(F32)
        grad_raw = grad_step * sig_ref[...]
        padded = jnp.concatenate([grad_raw, jnp.zeros((LANES - heads, SPAN), F32)], axis=0)
        out_raw_ref[...] = padded.T.astype(BF16)
        grad_score = jnp.where(same_doc(), grad_score_ref[...], 0.0).astype(BF16)
        grad_in = grad_in_ref[...] + dot(grad_score, out_map)
        grad_out = grad_out_ref[...] + dot_first(grad_score, in_map)
        low = jnp.concatenate([grad_in, grad_out], axis=1).astype(BF16)
        out_bc_ref[...] = low
        if edge:
            product = low[:8].astype(F32) * slope_bc_ref[...][:8].astype(F32)
            edge_ref[:, groups * width :] = product.astype(BF16)


def conv_back_kernel(
    value_blocks, places,
    grad_ref, grad_bc_ref, slope_ref, slope_bc_ref, next_ref, vector_ref, valid_ref, next_valid_ref, project_ref,
):
    block = pl.program_id(0)
    length = grad_ref.shape[0]

    def back(grad_low, slope_low):
        grad = grad_low.astype(F32) * slope_low.astype(F32)
        later = next_ref[...].astype(F32)
        weight, _ = taps_at(vector_ref, places, block * grad.shape[1], grad.shape[1])
        valid, next_valid = [jnp.concatenate([ref[...]] * (grad.shape[1] // LANES), axis=1) for ref in (valid_ref, next_valid_ref)]
        taps = weight.shape[0]
        total = weight[taps - 1 : taps] * grad
        for ahead in range(1, taps):
            extended = jnp.concatenate(
                [jnp.where(valid >= ahead, grad, 0.0), jnp.where(next_valid >= ahead, later, 0.0)], axis=0
            )
            total = total + weight[taps - 1 - ahead : taps - ahead] * extended[ahead : ahead + length]
        project_ref[...] = total.astype(BF16)

    @pl.when(block < value_blocks)
    def _():
        back(grad_ref[...], slope_ref[...])

    @pl.when(block == value_blocks)
    def _():
        back(grad_bc_ref[...], slope_bc_ref[...])


def spec(shape, index):
    return pl.BlockSpec(shape, index)


def whole(shape):
    return pl.BlockSpec(shape, lambda *_: (0,) * len(shape))


def cost(microseconds):
    return pl.CostEstimate(flops=int(microseconds * 2.3e+09), bytes_accessed=1 << 16, transcendentals=0)


class Sizes:
    def __init__(self, rows, inner, heads, state, columns, taps):
        self.rows, self.inner, self.heads, self.state, self.columns, self.taps = rows, inner, heads, state, columns, taps
        self.head = inner // heads
        self.spans = rows // SPAN
        self.mixed = inner + 2 * state
        self.group_heads = 8
        self.groups = heads // self.group_heads
        self.wide = self.group_heads * self.head
        self.places = tuple(tap * self.mixed for tap in range(taps + 1))
        self.gate_gain = (taps + 1) * self.mixed
        self.norm_gain = self.gate_gain + inner


def conv_forward(sizes, mixed, raw, rim, level, tokens):
    s = sizes
    rows, wide, heads, state = s.rows, s.wide, s.heads, s.state
    maps = s.inner // (2 * state)
    shapes = [(s.inner, rows), (rows, s.inner), (rows, 4 * state)]
    args = [level.vector, tokens.valid, raw, level.heads, tokens.flags]
    outputs = pl.pallas_call(
        functools.partial(conv_kernel, s.spans, s.head, heads, state, s.places),
        grid=(s.groups,),
        in_specs=[
            spec((rows, wide), lambda g: (0, g)), spec((rows, 2 * state), lambda g: (0, maps)),
            spec((8, wide), lambda g: (0, g)), spec((8, 2 * state), lambda g: (0, maps)), *whole_specs(*args),
        ],
        out_specs=[
            spec((wide, rows), lambda g: (g, 0)), spec((rows, wide), lambda g: (0, g)), whole(shapes[2]),
            whole((3 * heads, rows)),
        ] + [spec((wide, state), lambda g: (g, 0))] * s.spans,
        out_shape=[shape_of(shapes[0]), far_shape(shapes[1]), shape_of(shapes[2]), shape_of((3 * heads, rows), F32)]
        + [shape_of((s.inner, state))] * s.spans,
        scratch_shapes=[pltpu.VMEM((heads, rows), F32)],
        compiler_params=PARAMS,
        cost_estimate=cost(8.5),
    )(mixed, mixed, rim, rim, *args)
    return outputs[:4], outputs[4:]


def span_specs(sizes, span):
    s = sizes
    return Bag(
        turned=spec((s.wide, SPAN), lambda g: (g, span)),
        maps=spec((SPAN, 2 * s.state), lambda g: (span, 0)),
        rows=spec((s.group_heads, SPAN), lambda g: (g, span)),
        decay=spec((s.group_heads, SPAN), lambda g: (s.groups + g, span)),
        flags=spec((1, 8, SPAN), lambda g: (span, 0, 0)),
        doc_column=spec((SPAN, LANES), lambda g: (span, 0)),
        doc_row=spec((8, SPAN), lambda g: (0, span)),
        state=spec((s.wide, s.state), lambda g: (g, 0)),
        head=spec((s.group_heads, LANES), lambda g: (g, 0)),
        full=spec((SPAN, s.inner), lambda g: (span, 0)),
    )


ANYWHERE = pl.BlockSpec(memory_space=pl.ANY)


def scan_forward(sizes, span, conv, state_in, gate, level, tokens, earlier):
    s = sizes
    at = span_specs(s, span)
    args = [
        conv.values, conv.maps, conv.step, conv.step, tokens.flags, tokens.column, tokens.row, state_in, level.heads,
        gate, level.vector,
    ]
    in_specs = [
        at.turned, at.maps, at.rows, at.decay, at.flags, at.doc_column, at.doc_row, at.state,
        at.head, at.full, whole(level.vector.shape),
    ]
    aliases = {}
    if earlier is not None:
        aliases = {len(args): 0, len(args) + 1: 1}
        args, in_specs = args + list(earlier), in_specs + [ANYWHERE] * 2
    shape = (s.rows, s.inner)
    return pl.pallas_call(
        functools.partial(scan_kernel, s.head, s.state, s.gate_gain),
        grid=(s.groups,),
        in_specs=in_specs,
        out_specs=[spec((SPAN, s.wide), lambda g: (span, g)), at.full],
        out_shape=[shape_of(shape), shape_of(shape)],
        scratch_shapes=[pltpu.VMEM((SPAN, SPAN), F32), pltpu.VMEM((SPAN, s.inner), BF16)],
        input_output_aliases=aliases,
        compiler_params=PARAMS,
        cost_estimate=cost(6.5),
    )(*args)


SMALL = pl.BlockSpec(memory_space=pltpu.SMEM)


def shape_of(shape, dtype=BF16):
    return jax.ShapeDtypeStruct(shape, dtype)


def far_shape(shape, dtype=BF16):
    return pltpu.HBM(shape, dtype)


def whole_specs(*arrays):
    return [whole(array.shape) for array in arrays]


def project_mixed(sizes, inputs, level, lane_mask):
    s = sizes
    args = [inputs, level.vector, level.in_down, lane_mask, level.in_up]
    width = inputs.shape[1]
    shapes = [(s.rows, width + LANES), (s.rows, s.mixed), (s.rows, LANES), (8, s.mixed)]
    return pl.pallas_call(
        functools.partial(mixed_kernel, s.mixed, LANES, s.norm_gain, len(level.mixed)),
        grid=(1,),
        in_specs=whole_specs(*args) + [SMALL] + whole_specs(*level.mixed),
        out_specs=[whole(shape) for shape in shapes],
        out_shape=[shape_of(shape) for shape in shapes],
        compiler_params=PARAMS,
        cost_estimate=cost(6),
    )(*args, level.mixed_where, *level.mixed)


def gate_specs(sizes, level):
    return [whole((sizes.inner, LANES)), SMALL] + whole_specs(*level.gate)


def project_gate(sizes, normed, level):
    s = sizes
    return pl.pallas_call(
        functools.partial(gate_kernel, len(level.gate)),
        grid=(1,),
        in_specs=whole_specs(normed) + gate_specs(s, level),
        out_specs=whole((s.rows, s.inner)),
        out_shape=shape_of((s.rows, s.inner)),
        compiler_params=PARAMS,
        cost_estimate=cost(3.6),
    )(normed, level.in_up, level.where, *level.gate)


def project_out(sizes, normed_out, inputs, level, lane_mask):
    s = sizes
    args = [normed_out, inputs, level.out_down, lane_mask, level.out_up]
    shapes = [(s.rows, LANES), inputs.shape]
    return pl.pallas_call(
        functools.partial(out_kernel, len(level.out)),
        grid=(1,),
        in_specs=whole_specs(*args) + [SMALL] + whole_specs(*level.out),
        out_specs=[whole(shape) for shape in shapes],
        out_shape=[shape_of(shape) for shape in shapes],
        compiler_params=PARAMS,
        cost_estimate=cost(4),
    )(*args, level.where, *level.out)


def out_backward(sizes, upstream, mixed, gate, conv, level, lane_mask, tokens):
    s = sizes
    full = spec((SPAN, s.inner), lambda k: (k, 0))
    width = upstream.shape[1]
    return pl.pallas_call(
        functools.partial(out_back_kernel, s.head, s.heads, s.state, s.gate_gain, len(level.out)),
        grid=(s.spans,),
        in_specs=[
            spec((SPAN, width), lambda k: (k, 0)), spec((SPAN, LANES), lambda k: (k, 0)),
            *whole_specs(level.out_up, level.out_down), full, full, whole(level.vector.shape),
            spec((s.heads, SPAN), lambda k: (1, k)), spec((1, 8, SPAN), lambda k: (k, 0, 0)),
            spec((SPAN, 2 * s.state), lambda k: (k, 0)), SMALL, *whole_specs(*level.out),
        ],
        out_specs=[
            full, spec((s.inner, SPAN), lambda k: (0, k)), spec((SPAN, LANES), lambda k: (k, 0)),
        ] + [whole((s.inner, s.state))] * s.spans,
        out_shape=[
            shape_of((s.rows, s.inner)), shape_of((s.inner, s.rows)), shape_of((s.rows, LANES)),
        ] + [shape_of((s.inner, s.state))] * s.spans,
        scratch_shapes=[pltpu.VMEM((SPAN, s.inner), F32), pltpu.VMEM((SPAN, s.inner), BF16)],
        compiler_params=PARAMS,
        cost_estimate=cost(13.5),
    )(
        upstream, lane_mask, level.out_up, level.out_down, mixed, gate, level.vector, conv.step, tokens.flags, conv.maps,
        level.where, *level.out,
    )


def gate_in_backward(sizes, grad_gate, level):
    s = sizes
    width = 4 * s.columns
    return pl.pallas_call(
        functools.partial(gate_in_back_kernel, len(level.gate)),
        grid=(1,),
        in_specs=whole_specs(grad_gate) + gate_specs(s, level)[1:],
        out_specs=whole((s.rows, width)),
        out_shape=shape_of((s.rows, width), F32),
        compiler_params=PARAMS,
        cost_estimate=cost(3.5),
    )(grad_gate, level.where, *level.gate)


def narrow_backward(sizes, grad_gate, grad_mixed, raw, level, lane_mask):
    s = sizes
    args = [grad_gate, grad_mixed, raw, lane_mask, level.in_up]
    return pl.pallas_call(
        functools.partial(narrow_back_kernel, s.heads),
        grid=(1,),
        in_specs=whole_specs(*args),
        out_specs=whole((s.rows, LANES)),
        out_shape=shape_of((s.rows, LANES)),
        compiler_params=PARAMS,
        cost_estimate=cost(1.3),
    )(*args)


def mixed_in_backward(sizes, grad_mixed, raw, part, inputs, upstream, narrow, level):
    s = sizes
    width = inputs.shape[1]
    rows = lambda columns: spec((SPAN, columns), lambda k: (k, 0))
    return pl.pallas_call(
        functools.partial(mixed_in_back_kernel, s.mixed, s.heads, s.norm_gain, len(level.mixed)),
        grid=(s.spans,),
        in_specs=[
            rows(s.mixed), rows(LANES), rows(width), rows(width), rows(width), whole(level.vector.shape),
            rows(LANES), *whole_specs(level.in_down), SMALL, *whole_specs(*level.mixed),
        ],
        out_specs=rows(width),
        out_shape=shape_of((s.rows, width)),
        scratch_shapes=[pltpu.VMEM((SPAN, width), F32)],
        compiler_params=PARAMS,
        cost_estimate=cost(4.7),
    )(grad_mixed, raw, part, inputs, upstream, level.vector, narrow, level.in_down, level.mixed_where, *level.mixed)


def scan_backward(sizes, span, conv, grad_turned, state_in, grad_state, level, tokens, earlier):
    s = sizes
    at = span_specs(s, span)
    args = [
        conv.values, grad_turned, conv.maps, conv.step, conv.step, conv.step, tokens.flags, tokens.column, tokens.row,
        state_in, grad_state, level.heads, level.heads, conv.slope, conv.maps,
    ]
    in_specs = [
        at.turned, at.turned, at.maps, at.rows, at.decay, spec((s.heads, SPAN), lambda g: (2, span)), at.flags,
        at.doc_column, at.doc_row, at.state, at.state, at.head, whole((s.heads, LANES)),
        spec((16, s.wide), lambda g: (0, g)), spec((16, 2 * s.state), lambda g: (0, 1)),
    ]
    aliases = {}
    if earlier is not None:
        aliases = {len(args) + place: place for place in range(3)}
        args, in_specs = args + list(earlier[:3]), in_specs + [ANYWHERE] * 3
    out_specs = [spec((SPAN, s.wide), lambda g: (span, g)), at.maps, spec((SPAN, LANES), lambda g: (span, 0))]
    out_shape = [shape_of((s.rows, s.inner)), shape_of((s.rows, 2 * s.state)), shape_of((s.rows, LANES))]
    if span == 0:
        out_specs, out_shape = out_specs + [whole((8, s.mixed))], out_shape + [shape_of((8, s.mixed))]
    return pl.pallas_call(
        functools.partial(scan_back_kernel, s.head, s.heads, s.state, span == 0),
        grid=(s.groups,),
        in_specs=in_specs,
        out_specs=out_specs,
        out_shape=out_shape,
        scratch_shapes=[
            pltpu.VMEM((SPAN, SPAN), F32), pltpu.VMEM((SPAN, SPAN), F32), pltpu.VMEM((s.heads, SPAN), F32),
            pltpu.VMEM((s.heads, SPAN), F32), pltpu.VMEM((SPAN, s.state), F32), pltpu.VMEM((SPAN, s.state), F32),
        ],
        input_output_aliases=aliases,
        compiler_params=PARAMS,
        cost_estimate=cost(8.5),
    )(*args)


def conv_backward(sizes, grad_values, grad_maps, conv, later, level, tokens):
    s = sizes
    wide = 2 * s.state
    blocks = s.inner // wide
    values = spec((s.rows, wide), lambda i: (0, jnp.minimum(i, blocks - 1)))
    maps, slopes = whole((s.rows, wide)), spec((s.rows, wide), lambda i: (0, 1))
    fixed = [level.vector, tokens.valid, tokens.next_valid]
    return pl.pallas_call(
        functools.partial(conv_back_kernel, blocks, s.places),
        grid=(blocks + 1,),
        in_specs=[values, maps, values, slopes, spec((8, wide), lambda i: (0, i)), *whole_specs(*fixed)],
        out_specs=spec((s.rows, wide), lambda i: (0, i)),
        out_shape=shape_of((s.rows, s.mixed)),
        compiler_params=PARAMS,
        cost_estimate=cost(4.4),
    )(grad_values, grad_maps, conv.slope, conv.maps, later, *fixed)


def stacked_kernel(places, *refs):
    out_ref = refs[-1]
    first = 0
    for left, right in places:
        rows = refs[left].shape[1]
        out_ref[first : first + rows, :] = dot_first(refs[left][...], refs[right][...]).astype(BF16)
        first += rows
    if first < out_ref.shape[0]:
        out_ref[first:, :] = jnp.zeros((out_ref.shape[0] - first, out_ref.shape[1]), BF16)


def stacked(sizes, args, places, columns, rows, first, buffer, all_rows):
    s = sizes
    in_specs = [spec((s.rows, width), functools.partial(lambda at, _: (0, at), at)) for at, width in columns]
    aliases = {}
    if buffer is not None:
        aliases = {len(args): 0}
        args, in_specs = args + [buffer], in_specs + [ANYWHERE]
    return pl.pallas_call(
        functools.partial(stacked_kernel, places),
        grid=(1,),
        in_specs=in_specs,
        out_specs=pl.BlockSpec((pl.Element(rows), pl.Element(LANES)), lambda _: (first, 0)),
        out_shape=shape_of((all_rows, LANES)),
        input_output_aliases=aliases,
        compiler_params=PARAMS,
        cost_estimate=cost(1.6),
    )(*args)


def grad_rows(sizes, width):
    return width + 2 * sizes.inner, -(-(width + sizes.mixed + LANES) // 512) * 512


def early_grads(sizes, upstream, kept, grad_narrow_out, grad_gate, first, buffer, all_rows):
    s = sizes
    width = upstream.shape[1]
    args = [upstream, kept.narrow_out, kept.normed_out, grad_narrow_out, grad_gate, kept.normed]
    columns = [(0, width), (0, LANES), (0, s.inner), (0, LANES), (0, s.inner), (width // LANES, LANES)]
    return stacked(
        s, args, ((0, 1), (2, 3), (4, 5)), columns, grad_rows(s, width)[0], first, buffer, all_rows
    )


def late_grads(sizes, kept, grad_narrow, grad_mixed, raw, first, buffer, all_rows):
    s = sizes
    width = kept.inputs.shape[1]
    args = [kept.normed, grad_narrow, grad_mixed, raw, kept.normed]
    columns = [(0, width), (0, LANES), (0, s.mixed), (0, LANES), (width // LANES, LANES)]
    return stacked(s, args, ((0, 1), (2, 4), (3, 4)), columns, grad_rows(s, width)[1], first, buffer, all_rows)


def final_kernel(width, inner, where_ref, *refs):
    upper, upper_other, lower, lower_other, down_in_ref, in_up_ref, down_out_ref, out_up_ref = refs
    first = where_ref[0] == 0
    half = upper.shape[0]

    def rows(start, stop):
        pieces = []
        for side, (mine, yours) in enumerate(((lower, upper_other), (lower_other, upper))):
            low, high = max(start - side * half, 0), min(stop - side * half, half)
            if low < high:
                pieces.append(jnp.where(first, mine[low:high], yours[low:high]).astype(F32))
        return pieces

    def put(ref, at, start, stop):
        for piece in rows(start, stop):
            ref[at : at + piece.shape[0], :] = piece
            at += piece.shape[0]

    out_up_ref[...] = jnp.concatenate(rows(0, width), axis=0).T
    put(down_out_ref, 0, width, width + inner)
    put(in_up_ref, 0, width + inner, width + 2 * inner)
    late = width + 2 * inner
    put(down_in_ref, 0, late, late + width)
    put(in_up_ref, inner, late + width, late + width + in_up_ref.shape[0] - inner)


def final_sums(sizes, width, section, *sums):
    s = sizes
    shapes = [(width, LANES), (s.inner + s.mixed + s.heads, LANES), (s.inner, LANES), (LANES, width)]
    return pl.pallas_call(
        functools.partial(final_kernel, width, s.inner),
        grid=(1,),
        in_specs=[SMALL] + whole_specs(*sums),
        out_specs=[whole(shape) for shape in shapes],
        out_shape=[shape_of(shape, F32) for shape in shapes],
        compiler_params=PARAMS,
    )(section[None], *sums)


def token_kernel(spans, row_ref, before_ref, after_ref, table_ref, valid_ref, next_ref, column_ref, mask_ref, flags_ref):
    length = row_ref.shape[1]
    row = row_ref[...].astype(F32)
    ids = jnp.concatenate([before_ref[...].astype(F32), row, after_ref[...].astype(F32)], axis=1)
    behind = jnp.zeros((1, length + LANES), F32)
    for back in (1, 2, 3):
        same = ids[:, LANES - back : 2 * LANES - back + length] == ids[:, LANES : 2 * LANES + length]
        behind = behind + jnp.where(same, 1.0, 0.0)
    adapter = jnp.zeros_like(row)
    for document in range(table_ref.shape[0]):
        adapter = jnp.where(row == document, table_ref[document].astype(F32), adapter)
    rows = jnp.concatenate([behind[:, :length], row, adapter, jnp.zeros((5, length), F32)], axis=0).T
    wide = (length, LANES)
    valid_ref[...] = jnp.broadcast_to(rows[:, :1], wide).astype(jnp.int32)
    column_ref[...] = jnp.broadcast_to(rows[:, 1:2], wide).astype(jnp.int32)
    lanes = lax.broadcasted_iota(jnp.int32, wide, 1) // RANK
    mask_ref[...] = jnp.where(lanes == jnp.broadcast_to(rows[:, 2:3], wide).astype(jnp.int32), 1.0, 0.0)
    last = jnp.concatenate([behind[:, length:], jnp.zeros((7, LANES), F32)], axis=0).T
    next_ref[...] = jnp.broadcast_to(last[:8, :1], (8, LANES)).astype(jnp.int32)
    zeros = jnp.zeros((5, SPAN), F32)
    for span in range(spans):
        here = row[:, span * SPAN : (span + 1) * SPAN]
        start = ids[:, LANES + span * SPAN - 1 : LANES + span * SPAN]
        end = here[:, SPAN - 1 :]
        keep = jnp.broadcast_to(jnp.where(start == end, 1.0, 0.0), here.shape)
        flags_ref[span] = jnp.concatenate(
            [jnp.where(here == start, 1.0, 0.0), jnp.where(here == end, 1.0, 0.0), keep, zeros], axis=0
        )


def token_tables(doc_ids, table):
    rows = doc_ids.shape[1]
    before = from_behind(doc_ids[:, rows - LANES :], SEQ, 1)
    after = from_behind(doc_ids[:, :LANES], SEQ, -1)
    shapes = [((rows, LANES), jnp.int32), ((8, LANES), jnp.int32), ((rows, LANES), jnp.int32), ((rows, LANES), F32)]
    shapes.append(((rows // SPAN, 8, SPAN), F32))
    valid, next_valid, column, mask, flags = pl.pallas_call(
        functools.partial(token_kernel, rows // SPAN),
        grid=(1,),
        in_specs=whole_specs(doc_ids, before, after) + [SMALL],
        out_specs=[whole(shape) for shape, _ in shapes],
        out_shape=[jax.ShapeDtypeStruct(*one) for one in shapes],
        compiler_params=PARAMS,
    )(doc_ids, before, after, table)
    row = jnp.broadcast_to(doc_ids, (8, rows))
    return Bag(valid=valid, next_valid=next_valid, column=column, row=row, flags=flags), mask


def state_hops(rows, block_rows):
    eighth = block_rows // DOCS_PER_BLOCK
    if rows // SPAN > 1 and eighth > SPAN:
        raise ValueError("unsupported block")
    return 1 if rows >= eighth else 2 * eighth // rows - 1


def pass_states(sizes, local, conv, tokens, hops, direction):
    if hops > 1:
        keep = jnp.exp2(conv.step[sizes.heads : 2 * sizes.heads, -1]) * tokens.flags[0, 2, 0]
        keep = jnp.repeat(keep, sizes.head)[:, None]
        total = local.astype(F32)
        reach = 1
        while reach < hops:
            total = total + keep * from_behind(total.astype(BF16), SEQ, direction * reach).astype(F32)
            keep = keep * from_behind(keep, SEQ, direction * reach)
            reach *= 2
        local = total.astype(BF16)
    return from_behind(local, SEQ, direction)


def layer_forward(sizes, inputs, level, lane_mask, tokens, hops):
    s = sizes
    normed, mixed, raw, rim = project_mixed(s, inputs, level, lane_mask)
    rim = from_behind(rim, SEQ, 1)
    yield mixed
    gate = None
    if level.gate_first:
        gate = project_gate(s, normed, level)
        rim = tie(rim, gate)
    (values, slope, maps, step), states = conv_forward(s, mixed, raw, rim, level, tokens)
    conv = Bag(values=values, slope=slope, maps=maps, step=step)
    states_in = [pass_states(s, states[-1], conv, tokens, hops, 1)] + list(states[:-1])
    yield values
    if gate is None:
        gate = project_gate(s, normed, level)
    outputs = None
    for span in reversed(range(s.spans)):
        outputs = scan_forward(s, span, conv, states_in[span], gate, level, tokens, outputs)
        if span == s.spans - 1:
            yield outputs[0]
    mixed_out, normed_out = outputs
    narrow_out, result = project_out(s, normed_out, inputs, level, lane_mask)
    yield result
    kept = Bag(
        inputs=inputs, normed=normed, gate=gate, conv=conv, states_in=states_in, mixed_out=mixed_out,
        normed_out=normed_out, narrow_out=narrow_out,
    )
    return result, kept


def layer_backward(sizes, upstream, kept, level, lane_mask, tokens, hops):
    s = sizes
    conv = kept.conv
    early_rows, late_rows = grad_rows(s, upstream.shape[1])
    all_rows = early_rows + late_rows
    grad_gate, turned, grad_narrow_out, *local = out_backward(
        s, upstream, kept.mixed_out, kept.gate, conv, level, lane_mask, tokens
    )
    grad_states = list(local[1:]) + [pass_states(s, local[0], conv, tokens, hops, -1)]
    buffer = early_grads(s, upstream, kept, grad_narrow_out, grad_gate, 0, None, all_rows)
    outputs = None
    for span in range(s.spans):
        outputs = scan_backward(
            s, span, conv, turned, kept.states_in[span], grad_states[span], level, tokens, outputs
        )
        if span == 0:
            later = from_behind(outputs[3], SEQ, -1)
            turned = yield outputs[0], turned
    grad_values, grad_maps, raw = outputs[:3]
    grad_values = yield grad_values, grad_values
    grad_mixed = conv_backward(s, grad_values, grad_maps, conv, later, level, tokens)
    grad_mixed = yield grad_mixed, grad_mixed
    narrow = narrow_backward(s, grad_gate, grad_mixed, raw, level, lane_mask)
    buffer = late_grads(s, kept, narrow, grad_mixed, raw, early_rows, buffer, all_rows)
    grad_mixed = yield buffer, grad_mixed
    part = gate_in_backward(s, tie(grad_gate, grad_mixed), level)
    return mixed_in_backward(s, grad_mixed, raw, part, kept.inputs, upstream, narrow, level)


def make_level(sizes, vector, numbers, adapters, where):
    s = sizes
    in_down, in_up = adapters
    dt_bias, a_log, skip_gain = numbers
    rate = -jnp.exp(a_log)[:, None]
    lane = jnp.arange(LANES)[None, :]
    table = jnp.where(lane == 1, skip_gain[:, None], jnp.where(lane == 2, dt_bias[:, None], rate))
    table = jnp.where(lane == 0, rate * LOG2E, table)
    return Bag(vector=vector, heads=table, in_down=in_down, in_up=in_up, where=where, mixed_where=where)


def swap(value):
    return lax.ppermute(value, SECTION, [(0, 1), (1, 0)])


def exchange(value, axis, distance):
    count = lax.axis_size(axis)
    return lax.ppermute(value, axis, [(place, place ^ distance) for place in range(count)])


def rows_at(value, index, rows):
    return lax.dynamic_slice_in_dim(value, index * rows, rows, axis=0)


def put_at(buffer, value, *index):
    start = list(index) + [0] * (buffer.ndim - len(index))
    return lax.dynamic_update_slice(buffer, value.reshape((1,) * len(index) + value.shape), start)


def across(value, second):
    count = lax.axis_size(WSHARD)
    pairs = []
    for section in range(2):
        distance = 2 - section if second else 1 + section
        pairs += [(section * count + place, section * count + (place ^ distance)) for place in range(count)]
    return lax.ppermute(value, (SECTION, WSHARD), pairs)


class Parts:
    def __init__(self, quarters):
        self.section = lax.axis_index(SECTION)
        self.quarters, self.near, self.parts = quarters, {}, {}
        other = swap(quarters[0][0])
        self.own = [jnp.where(self.section == 0, quarters[0][0], other)]
        others = [other] + [swap(tie(matrix, self.own[0])) for matrix, _, _ in quarters[1:]]
        self.later = others[1]
        for layer in range(2):
            for (matrix, _, _), other in list(zip(quarters, others, strict=True))[1 - layer :]:
                self.own.append(jnp.where(self.section == layer, matrix, other))

    def start(self, index, *after):
        self.near[index] = across(tie(self.own[index], *after), False)

    def forward(self, index, *after):
        _, half, step = self.quarters[index % len(self.quarters)]
        near = tie(self.near[index], *after)
        apart = across(lax.dynamic_slice_in_dim(near, self.section * step, half, axis=0), True)
        self.halfway = (self.own[index], near, swap(near), apart)
        return apart

    def finish(self, index, *after):
        self.parts[index] = self.halfway + (swap(tie(self.halfway[3], *after)),)


def scatter_start(value, axis):
    count, place = lax.axis_size(axis), lax.axis_index(axis)
    rows = value.shape[0] // count
    sent = [exchange(rows_at(value, place ^ away, rows), axis, away) for away in range(1, count)]
    return rows_at(value, place, rows), sent


def scatter_done(parts, *after):
    own, received = parts
    total = own.astype(F32)
    for part in tie(received, *after):
        total = total + part.astype(F32)
    return total.astype(BF16)


def gather_start(value, axis):
    return value, [exchange(value, axis, away) for away in range(1, lax.axis_size(axis))]


def gather_done(parts, axis, *after):
    own, received = parts
    count, place = lax.axis_size(axis), lax.axis_index(axis)
    buffer = jnp.zeros((count,) + own.shape, own.dtype)
    for away, part in enumerate([own] + tie(received, *after)):
        buffer = put_at(buffer, part, place ^ away)
    return buffer.reshape((count * own.shape[0],) + own.shape[1:])


def chip_start(packed):
    section = lax.axis_index(SECTION)
    half = packed.shape[0] // 2
    return rows_at(packed, section, half), [swap(rows_at(packed, 1 - section, half))]


def both_layers(own):
    section = lax.axis_index(SECTION)
    other = swap(own)
    return [jnp.where(section == layer, own, other) for layer in range(2)]


def on_device(
    layer_input, out_grad, doc_index, doc_adapter, in_weight, out_weight, norm_gain, conv_weight, conv_bias, dt_bias,
    a_log, skip_gain, gate_gain, *adapters,
):
    section, place = lax.axis_index(SECTION), lax.axis_index(WSHARD)
    batches, rows, width = layer_input.shape
    heads, inner = dt_bias.shape[1], gate_gain.shape[1]
    taps, mixed = conv_weight.shape[1:]
    sizes = Sizes(rows, inner, heads, (mixed - inner) // 2, in_weight.shape[1], taps)
    block_rows = rows * lax.axis_size(SEQ)
    hops = state_hops(rows, block_rows)

    pick = lambda array: lax.dynamic_index_in_dim(array, section, 0, keepdims=False)
    turned = in_weight[0].T
    main = mixed // 2
    weights = Parts(
        [
            (turned[inner:], main + heads, main),
            (turned[:inner], inner // 2, inner // 2),
            (out_weight[0], out_weight.shape[1] // 2, out_weight.shape[1] // 2),
        ]
    )
    weights.start(0)
    weights.start(1, weights.forward(0))
    weights.finish(0)
    rest = (layer_input, doc_index, doc_adapter, norm_gain, conv_weight, conv_bias, dt_bias, a_log, skip_gain)
    rest, gate_gain, adapters = tie((rest, gate_gain, adapters), weights.later)
    layer_input, doc_index, doc_adapter, norm_gain, conv_weight, conv_bias, dt_bias, a_log, skip_gain = rest
    inputs, doc_ids, table = pick(layer_input), pick(doc_index), pick(doc_adapter)[0]
    tokens, lane_mask = token_tables(doc_ids[None, :], table)
    vectors = both_layers(jnp.concatenate([conv_weight[0].reshape(1, -1), conv_bias, gate_gain, norm_gain], axis=1))
    numbers = both_layers(jnp.concatenate([dt_bias, a_log, skip_gain], axis=0))
    in_down, in_up, out_down, out_up = adapters
    both = [both_layers(array) for array in (in_down[0], in_up[0].T)]
    out_adapters = [(array[0], swap(array[0])) for array in (out_down, out_up)]
    where = jnp.stack([place, place ^ (1 + section), place ^ (2 - section), place ^ 3, section]).astype(jnp.int32)
    levels = [
        make_level(sizes, vectors[layer], numbers[layer], [pair[layer] for pair in both], where)
        for layer in range(2)
    ]
    small = [inputs, lane_mask, tokens.__dict__, weights.own[1:]] + [level.__dict__ for level in levels]
    small, weights.parts[0] = lax.optimization_barrier((small, weights.parts[0]))
    inputs, lane_mask, token_fields, weights.own[1:], *level_fields = small
    tokens, levels = Bag(**token_fields), [Bag(**fields) for fields in level_fields]
    levels[0].mixed = weights.parts[0]
    levels[0].gate_first = levels[1].gate_first = False

    passes = {(0, 0): 1, (0, 1): 2, (0, 2): 3, (0, 4): 4, (1, 1): 5}
    ends = {(0, 1): 1, (0, 2): 2, (0, 3): 3, (1, 0): 4, (1, 2): 5}
    results, kept = [], []
    rows_now = inputs
    for layer in range(2):
        stages = layer_forward(sizes, rows_now, levels[layer], lane_mask, tokens, hops)
        for stage in range(5):
            try:
                token = next(stages)
            except StopIteration as end:
                rows_now, stored = end.value
            if (layer, stage) == (0, 0):
                chosen = [
                    [jnp.where(section == choice, tie(here, token), there) for choice in range(2)]
                    for here, there in out_adapters
                ]
                for choice in range(2):
                    levels[choice].out_down, levels[choice].out_up = chosen[0][choice], chosen[1][choice]
            if (layer, stage) == (1, 0):
                grads = pick(tie(out_grad, token))
            move = ends.get((layer, stage))
            if move is not None:
                weights.finish(move, token)
                owner, parts = levels[move // 3], weights.parts[move]
                if move % 3 == 0:
                    owner.mixed = parts
                elif move % 3 == 1:
                    owner.gate = parts
                else:
                    owner.out = parts
            move = passes.get((layer, stage))
            if move is not None:
                weights.forward(move, token)
                if move < 5:
                    weights.start(move + 1, token)
        results.append(rows_now)
        kept.append(stored)

    def placed(pair):
        here = jnp.where(section == 0, pair[0], pair[1])
        there = swap(jnp.where(section == 0, pair[1], pair[0]))
        first, second = jnp.where(section == 0, here, there), jnp.where(section == 0, there, here)
        return jnp.stack([first, second])[None]

    direct = lax.axis_size(SEQ) == 4
    both_axes = (WSHARD, SEQ)

    def finish(stages, value):
        try:
            stages.send(value)
        except StopIteration as end:
            return end.value

    stages = layer_backward(sizes, tie(grads, rows_now), kept[1], levels[1], lane_mask, tokens, hops)
    _, pending = next(stages)
    for _ in range(2):
        _, pending = stages.send(pending)
    upper, pending = stages.send(pending)
    upper = chip_start(upper)
    upper_grad = finish(stages, pending)
    upper = scatter_done(upper, upper_grad)
    upper_grad = tie(upper_grad, upper)
    upper = scatter_start(upper, WSHARD) if direct else lax.psum(upper, both_axes)

    stages = layer_backward(sizes, upper_grad, kept[0], levels[0], lane_mask, tokens, hops)
    token, pending = next(stages)
    if direct:
        upper = scatter_start(scatter_done(upper, token), SEQ)
    token, pending = stages.send(tie(pending, upper[0]))
    if direct:
        upper = gather_start(scatter_done(upper, token), SEQ)
    token, pending = stages.send(tie(pending, upper[0]))
    if direct:
        upper = gather_start(gather_done(upper, SEQ, token), WSHARD)
    lower, pending = stages.send(tie(pending, upper[0]))
    lower = chip_start(lower)
    if direct:
        upper = gather_done(upper, WSHARD, lower[0])
    lower = scatter_done(lower, upper)
    if direct:
        lower = scatter_start(lower, WSHARD)
    lower_grad = finish(stages, tie(pending, lower[0]))
    outputs = (placed(results), placed([lower_grad, upper_grad]))
    if direct:
        lower = scatter_start(scatter_done(lower, lower_grad), SEQ)
        lower = gather_start(scatter_done(lower), SEQ)
        lower = gather_start(gather_done(lower, SEQ), WSHARD)
        lower = gather_done(lower, WSHARD, outputs)
    else:
        lower = lax.psum(lower, both_axes)
    sums = final_sums(sizes, width, section, upper, swap(upper), lower, swap(lower))
    down_in, in_up, down_out, out_up = sums
    return (
        *outputs, down_in[None], in_up.T[None], down_out[None], out_up[None],
    )


def solution(mesh):
    tokens, matrix, vector = P(None, (WSHARD, SEQ), None), P(SECTION, None, None), P(SECTION, None)
    in_specs = (tokens, tokens, P(None, (WSHARD, SEQ)), P(None, WSHARD, None))
    in_specs += (P(SECTION, WSHARD, None),) * 2
    in_specs += (vector, matrix) + (vector,) * 5 + (matrix,) * 4
    out_specs = (P(SECTION, None, (WSHARD, SEQ), None),) * 2 + (matrix,) * 4
    return jax.shard_map(on_device, mesh=mesh, in_specs=in_specs, out_specs=out_specs, check_vma=False)
```
